128 devices in a mesh: grp: 4 (over x), seq: 16 (over z, y), head: 2 (over core).
Axes of the slice: x: 4, y: 4, z: 4, core: 2. Of those that a mesh axis runs over, the one named last changes fastest.
Arguments:
- enc_ids: int32 [32, 1024], P('grp', 'seq'), may hold values from 0 to 32127
- lengths: int32 [32], P('grp'), may hold values from 1 to 924, as said below
- dec_ids: int32 [32, 128], P('grp', 'seq'), may hold values from 0 to 32127
- target_ids: int32 [32, 128], P('grp', 'seq'), may hold values from 0 to 32127
- loss_mask: int32 [32, 128], P('grp'), may hold values from 0 to 1, as said below
- embedding: bfloat16 [32128, 768], P('head')
- prompt: float32 [100, 768], replicated, may hold values from -6 to 6
- first_moment: float32 [100, 768], replicated, may hold values from -5.722046e-06 to 5.722046e-06
- second_moment: float32 [100, 768], replicated, may hold values from 1.3020833e-13 to 5.208333e-13
- gains: float32 [7, 768], replicated, may hold values from 0.5 to 1.5
- enc_qkv: bfloat16 [768, 2304], replicated, may hold values from -0.21875 to 0.21875
- enc_wo: bfloat16 [768, 768], replicated, may hold values from -0.875 to 0.875
- enc_w1: bfloat16 [768, 3072], replicated, may hold values from -0.21875 to 0.21875
- enc_w2: bfloat16 [3072, 768], replicated, may hold values from -0.109375 to 0.109375
- dec_qkv: bfloat16 [768, 3, 768], P(None, None, 'head'), may hold values from -0.21875 to 0.21875
- dec_wo: bfloat16 [768, 768], P('head'), may hold values from -0.625 to 0.625
- cross_q: bfloat16 [768, 768], P(None, 'head'), may hold values from -0.21875 to 0.21875
- cross_kv: bfloat16 [768, 2, 768], P(None, None, 'head'), may hold values from -0.21875 to 0.21875
- cross_wo: bfloat16 [768, 768], P('head'), may hold values from -0.875 to 0.875
- dec_w1: bfloat16 [768, 3072], P(None, 'head'), may hold values from -0.21875 to 0.21875
- dec_w2: bfloat16 [3072, 768], P('head'), may hold values from -0.109375 to 0.109375
Outputs:
- loss: float32 [], replicated
- grad_norm: float32 [], replicated
- trust_norms: float32 [2], replicated
- first_new: float32 [100, 768], replicated
- second_new: float32 [100, 768], replicated
- prompt_new: float32 [100, 768], replicated
The draws below stay inside these ranges and needn't reach their ends.
Inputs may be any that keep to these rules, and one draw needn't show every extreme that they name: `lengths`: in each group of 8 consecutive examples one has exactly 924 input tokens. `loss_mask`: the first target of every example counts.
All inputs are finite; a program needn't handle non-finite values.
Results may differ from the reference program's by a relative error of at most 0.00355.
Values may be sent and summed in bfloat16 or wider, within the bound.
A program may use at most 256 MiB of HBM per device.

```python
import math
import jax
import jax.numpy as jnp
import numpy as np
from jax import lax

D = 768
FF = 3072
HEADS = 12
HD = 64
VOCAB = 32128
PROMPT = 100
L_ENC = 1024
TGT = 128
STEP = 5
SEQS_GRP = 8
SEQS = 32


def draw_embedding(key, part):
    key = jax.random.fold_in(key, 7)
    rows = jnp.arange(VOCAB, dtype=jnp.float32)[:, None] / VOCAB
    base = jax.random.normal(key, (VOCAB, D), jnp.float32)
    rise = 1.0 + 2.0 * rows
    return (base * rise).astype(jnp.bfloat16)


def draw_lengths(key, part):
    key = jax.random.fold_in(key, 11)
    key_len, key_pick = jax.random.split(key)
    most = L_ENC - PROMPT
    roots = jax.random.randint(key_len, (SEQS,), 1, 33)
    short = jnp.maximum(roots * roots * most // 1024, 1)
    picks = jax.random.randint(key_pick, (SEQS // SEQS_GRP,), 0, SEQS_GRP)
    full = jnp.arange(SEQS) % SEQS_GRP == jnp.repeat(picks, SEQS_GRP)
    return jnp.where(full, most, short).astype(jnp.int32)


def draw_loss_mask(key, part):
    key = jax.random.fold_in(key, 5)
    picks = jax.random.randint(key, (SEQS, TGT), 0, 4)
    first = jnp.arange(TGT)[None, :] == 0
    return jnp.where(first | (picks != 0), 1, 0).astype(jnp.int32)


def set_ends(entries, own_key, least, largest):
    extent = entries.shape
    index_at = [jax.random.randint(jax.random.fold_in(own_key, axis), (), 0, extent[axis]) for axis in range(len(extent))]
    entries = entries.at[tuple(index_at)].set(least)
    longest = extent.index(max(extent))
    index_at[longest] = (index_at[longest] + 1) % extent[longest]
    return entries.at[tuple(index_at)].set(largest)


def shard_levels(own_key, dims, cuts, least, high):
    level = 1.0
    for position, blocks in cuts:
        steps = jax.random.uniform(jax.random.fold_in(jax.random.fold_in(own_key, 6), position), (blocks,), jnp.float32, least / len(cuts), high / len(cuts))
        level = level * jnp.repeat(jnp.exp(steps), dims[position] // blocks).reshape((-1,) + (1,) * (len(dims) - 1 - position))
    return level


def rank_bounds(amount, slope):
    loads = [(1 << 20) // math.isqrt(grade ** slope) + 1 for grade in range(1, amount + 1)]
    spread = 1 + sum(loads) // (1 << 30)
    return np.cumsum(np.array([max(1, weight // spread) for weight in loads]))


def ranked(own_key, shape, number_of, lean):
    listing = rank_bounds(number_of, lean)
    lot = jax.random.randint(jax.random.fold_in(own_key, 1), shape, 0, int(listing[number_of - 1]))
    grade = jnp.searchsorted(jnp.asarray(listing, jnp.int32), lot, side="right")
    return jax.random.permutation(jax.random.fold_in(own_key, 2), number_of)[grade].astype(jnp.int32)


def normal_values(rng, shape, scale, bound, pieces=(), kind=jnp.bfloat16):
    loudness = shard_levels(rng, shape, pieces, -0.22, 0.18) if pieces else 1.0
    drawn = jax.random.normal(rng, shape, jnp.float32) * scale * loudness
    return jnp.minimum(jnp.maximum(drawn, -bound), bound).astype(kind)


def setup_inputs(seed: int = 0) -> dict:
    keys = jax.random.split(jax.random.key(seed), 22)
    return {
        "enc_ids": set_ends(jax.random.randint(keys[0], (SEQS, L_ENC), 0, VOCAB), jax.random.fold_in(keys[0], 1), 0, VOCAB - 1).astype(jnp.int32),
        "lengths": draw_lengths(jax.random.fold_in(keys[21], 71), 0),
        "dec_ids": set_ends(ranked(keys[2], (SEQS, TGT), VOCAB, 2), jax.random.fold_in(keys[2], 3), 0, VOCAB - 1).astype(jnp.int32),
        "target_ids": set_ends(ranked(keys[3], (SEQS, TGT), VOCAB, 2), jax.random.fold_in(keys[3], 3), 0, VOCAB - 1).astype(jnp.int32),
        "loss_mask": draw_loss_mask(jax.random.fold_in(keys[21], 71), 0),
        "embedding": draw_embedding(jax.random.fold_in(keys[21], 71), 0),
        "prompt": normal_values(keys[6], (PROMPT, D), 1.0, 6.0, (), jnp.float32),
        "first_moment": normal_values(keys[7], (PROMPT, D), (0.0001 * (PROMPT * D) ** -0.5), 5.7220458984375e-06, (), jnp.float32),
        "second_moment": jnp.clip(jnp.exp(jax.random.uniform(keys[8], (PROMPT, D), jnp.float32, math.log(1.3020833055429198e-13), math.log(5.208333222171679e-13))), 1.3020833055429198e-13, 5.208333222171679e-13),
        "gains": jnp.clip(1.0 + 0.1 * jax.random.normal(keys[9], (7, D), jnp.float32), 0.5, 1.5),
        "enc_qkv": normal_values(keys[10], (D, 3 * D), D ** -0.5, 0.21875),
        "enc_wo": normal_values(keys[11], (D, D), (D // 16) ** -0.5, 0.875),
        "enc_w1": normal_values(keys[12], (D, FF), D ** -0.5, 0.21875),
        "enc_w2": normal_values(keys[13], (FF, D), FF ** -0.5, 0.109375),
        "dec_qkv": normal_values(keys[14], (D, 3, D), D ** -0.5, 0.21875, ((2, 2),)),
        "dec_wo": normal_values(keys[15], (D, D), (D // 8) ** -0.5, 0.625, ((0, 2),)),
        "cross_q": normal_values(keys[16], (D, D), D ** -0.5, 0.21875, ((1, 2),)),
        "cross_kv": normal_values(keys[17], (D, 2, D), D ** -0.5, 0.21875, ((2, 2),)),
        "cross_wo": normal_values(keys[18], (D, D), (D // 16) ** -0.5, 0.875, ((0, 2),)),
        "dec_w1": normal_values(keys[19], (D, FF), D ** -0.5, 0.21875, ((1, 2),)),
        "dec_w2": normal_values(keys[20], (FF, D), FF ** -0.5, 0.109375, ((0, 2),)),
    }


precise = lax.Precision.HIGHEST

@jax.custom_vjp
def low(v):
    return lax.optimization_barrier(v.astype(jnp.bfloat16)).astype(jnp.float32)

@jax.custom_vjp
def low_back(v):
    return v

def low_keep(v):
    return (low(v), None)

def low_pass(kept, grad):
    return (grad,)

def back_keep(v):
    return (v, None)

def back_low(kept, grad):
    return (low(grad),)
low.defvjp(low_keep, low_pass)
low_back.defvjp(back_keep, back_low)

def both_low(value):
    return low_back(low(value))

def matmul_hi(left, right):
    return jnp.matmul(left, right, precision=precise)

def rms_norm(value, gain):
    return value * lax.rsqrt(lax.optimization_barrier(jnp.mean(value * value, axis=-1, keepdims=True)) + 1e-06) * gain

def split_heads(rows):
    return rows.reshape(rows.shape[0], HEADS, HD).transpose(1, 0, 2)

def join_heads(rows):
    return rows.transpose(1, 0, 2).reshape(rows.shape[1], HEADS * HD)

def attend(queries, keys_in, values_in, allowed):
    scores = low_back(jnp.einsum('hqd,hkd->hqk', split_heads(queries), split_heads(keys_in), precision=precise) * HD ** (-0.5))
    probs = jax.nn.softmax(jnp.where(allowed, scores, -1000000000.0), axis=-1)
    return join_heads(jnp.einsum('hqk,hkd->hqd', low(probs), split_heads(values_in), precision=precise))

def gelu_tanh(value):
    return jax.nn.gelu(value, approximate=True)

def sequence_loss(prompt, weights, enc_row, length, dec_row, target_row, mask_row):
    embed, gains, enc_qkv, enc_wo, enc_w1, enc_w2, dec_qkv, dec_wo, cross_q, cross_kv, cross_wo, dec_w1, dec_w2 = weights
    positions = jnp.arange(L_ENC)
    padded = jnp.pad(prompt, ((0, L_ENC - PROMPT), (0, 0)))
    start = jnp.where((positions < PROMPT)[:, None], padded, embed[enc_row])
    normed = low(rms_norm(start, gains[0]))
    joined = matmul_hi(normed, enc_qkv)
    key_ok = (positions < PROMPT + length)[None, None, :]
    attn_out = both_low(attend(both_low(joined[:, :D]), both_low(joined[:, D:2 * D]), both_low(joined[:, 2 * D:]), key_ok))
    hidden_one = start + low_back(matmul_hi(attn_out, enc_wo))
    normed_two = low(rms_norm(hidden_one, gains[1]))
    pre_act = low_back(matmul_hi(normed_two, enc_w1))
    hidden_two = hidden_one + low_back(matmul_hi(low(gelu_tanh(pre_act)), enc_w2))
    enc_out = low(rms_norm(hidden_two, gains[2]))
    dec_start = embed[dec_row]
    dec_norm = low(rms_norm(dec_start, gains[3]))
    self_qkv = low(matmul_hi(dec_norm, dec_qkv.reshape(D, 3 * D)))
    target_pos = jnp.arange(TGT)
    causal = (target_pos[None, :] <= target_pos[:, None])[None]
    self_out = low(attend(self_qkv[:, :D], self_qkv[:, D:2 * D], self_qkv[:, 2 * D:], causal))
    after_self = dec_start + matmul_hi(self_out, dec_wo)
    cross_norm = low(rms_norm(after_self, gains[4]))
    cross_query = low(matmul_hi(cross_norm, cross_q))
    cross_both = matmul_hi(enc_out, cross_kv.reshape(D, 2 * D))
    cross_out = both_low(attend(cross_query, both_low(cross_both[:, :D]), both_low(cross_both[:, D:]), key_ok))
    after_cross = after_self + low_back(matmul_hi(cross_out, cross_wo))
    ffn_norm = low(rms_norm(after_cross, gains[5]))
    dec_pre = low_back(matmul_hi(ffn_norm, dec_w1))
    after_ffn = after_cross + low_back(matmul_hi(low(gelu_tanh(dec_pre)), dec_w2))
    final = low(rms_norm(after_ffn, gains[6] * D ** (-0.5)))
    logits = low_back(matmul_hi(final, embed.T))
    totals = jax.nn.logsumexp(logits, axis=-1)
    picked = jnp.take_along_axis(logits, target_row[:, None], axis=1)[:, 0]
    weight = mask_row.astype(jnp.float32) / jnp.sum(mask_row.astype(jnp.float32))
    return jnp.sum(weight * (totals - picked))

def reference(enc_ids, lengths, dec_ids, target_ids, loss_mask, embedding, prompt, first_moment, second_moment, gains, enc_qkv, enc_wo, enc_w1, enc_w2, dec_qkv, dec_wo, cross_q, cross_kv, cross_wo, dec_w1, dec_w2):
    weights = (embedding.astype(jnp.float32), gains, enc_qkv.astype(jnp.float32), enc_wo.astype(jnp.float32), enc_w1.astype(jnp.float32), enc_w2.astype(jnp.float32), dec_qkv.astype(jnp.float32), dec_wo.astype(jnp.float32), cross_q.astype(jnp.float32), cross_kv.astype(jnp.float32), cross_wo.astype(jnp.float32), dec_w1.astype(jnp.float32), dec_w2.astype(jnp.float32))

    def total_loss(param):

        def one_example(items):
            return jax.checkpoint(sequence_loss)(param, weights, *items)
        return jnp.sum(lax.map(one_example, (enc_ids, lengths, dec_ids, target_ids, loss_mask)))
    loss, puller = jax.vjp(total_loss, prompt)
    grad = puller(jnp.ones_like(loss))[0]
    grad_norm = jnp.sqrt(jnp.sum(grad * grad))
    clipped = grad * (0.0001 / jnp.maximum(grad_norm, 0.0001))
    first_new = 0.5 * first_moment + 0.5 * clipped
    second_new = 0.5 * second_moment + 0.5 * clipped * clipped
    update = first_new / (1.0 - 0.5 ** STEP) / (jnp.sqrt(second_new / (1.0 - 0.5 ** STEP)) + 1e-12) + 0.01 * prompt
    param_norm = jnp.sqrt(jnp.sum(prompt * prompt))
    update_norm = jnp.sqrt(jnp.sum(update * update))
    prompt_new = prompt - 0.3 * (param_norm / update_norm) * update
    return (loss, grad_norm, jnp.stack([param_norm, update_norm]), first_new, second_new, prompt_new)
```

```python
import jax
import jax.numpy as jnp
from jax import lax
from jax.sharding import Mesh
from jax.sharding import PartitionSpec as P

HD = 64
PROMPT = 100
STEP = 5
QUARTERS = 4
SEQ = ("ex", "chip")
CLUSTER = ("chip", "head")
EVERYONE = ("grp", "ex", "chip", "head")
NEG = -1000000000.0

norm_eps = 1e-06
beta_first = 0.5
beta_second = 0.5
adam_eps = 1e-12
decay_rate = 0.01
learn_rate = 0.3
clip_bound = 0.0001


def rounded(value):
    return value.astype(jnp.bfloat16)


def product(left, right):
    return jnp.dot(left, right, preferred_element_type=jnp.float32)


def back_product(grad, weight):
    return jnp.einsum("rc,dc->rd", grad, weight, preferred_element_type=jnp.float32)


def rms_norm(value, gain):
    return value * lax.rsqrt(jnp.mean(value * value, axis=-1, keepdims=True) + norm_eps) * gain


def norm_back(value, gain, grad):
    return jax.vjp(lambda inner: rms_norm(inner, gain), value)[1](grad)[0]


def gelu_tanh(value):
    return jax.nn.gelu(value, approximate=True)


def gelu_back(value, grad):
    return jax.vjp(gelu_tanh, value)[1](grad)[0]


def split_heads(rows):
    return rows.reshape(rows.shape[0], -1, HD).transpose(1, 0, 2)


def join_heads(rows):
    return rows.transpose(1, 0, 2).reshape(rows.shape[1], -1)


def dot_qk(a, b):
    return jnp.einsum("hqd,hkd->hqk", a, b, preferred_element_type=jnp.float32)


def dot_pv(a, b):
    return jnp.einsum("hqk,hkd->hqd", a, b, preferred_element_type=jnp.float32)


def dot_tq(a, b):
    return jnp.einsum("hqk,hqd->hkd", a, b, preferred_element_type=jnp.float32)


def attend(queries, keys_in, values_in, allowed):
    scores = jnp.where(allowed, dot_qk(queries, keys_in) * HD ** (-0.5), NEG)
    top = jnp.max(scores, axis=-1, keepdims=True)
    weights = jnp.exp(scores - top)
    total = jnp.sum(weights, axis=-1, keepdims=True)
    out = dot_pv(rounded(weights), values_in) / total
    return out, top + jnp.log(total)


def over_heads(value):
    pair = lax.all_gather(value.astype(jnp.bfloat16), "head").astype(jnp.float32)
    return pair[0] + pair[1]


def lamb_terms(clipped, first_old, second_old, param):
    first_next = beta_first * first_old + (1.0 - beta_first) * clipped
    second_next = beta_second * second_old + (1.0 - beta_second) * clipped * clipped
    scaled_first = first_next / (1.0 - beta_first**STEP)
    scaled_second = second_next / (1.0 - beta_second**STEP)
    update = scaled_first / (jnp.sqrt(scaled_second) + adam_eps) + decay_rate * param
    return (first_next, second_next, update)


def shards(
    enc_ids,
    lengths,
    dec_ids,
    target_ids,
    loss_mask,
    embedding,
    prompt,
    first_moment,
    second_moment,
    gains,
    enc_qkv,
    enc_wo,
    enc_w1,
    enc_w2,
    dec_qkv,
    dec_wo,
    cross_q,
    cross_kv,
    cross_wo,
    dec_w1,
    dec_w2,
):
    head_idx = lax.axis_index("head")
    chip_idx = lax.axis_index("chip")
    ex_idx = lax.axis_index("ex")
    quarter = 2 * chip_idx + head_idx
    vocab_part, width = embedding.shape
    own = dec_wo.shape[0]
    offset = head_idx * vocab_part
    enc_dev, tgt_dev = enc_ids.shape[1], dec_ids.shape[1]
    seqs = lax.axis_size(SEQ)
    total_len = enc_dev * seqs
    tgt_all = tgt_dev * seqs
    half = tgt_all // 2
    tokens = (total_len - PROMPT) // QUARTERS
    lead = PROMPT // QUARTERS
    rows = total_len // QUARTERS

    ids = jnp.concatenate([enc_ids, dec_ids, target_ids], axis=1)
    every = lax.all_gather(ids, SEQ)
    ids = lax.dynamic_index_in_dim(every, ex_idx, 1, keepdims=False)
    tok_ids = ids[:, :enc_dev].reshape(-1)[PROMPT:].reshape(QUARTERS, tokens)
    tok_ids = jnp.pad(tok_ids, ((0, 0), (lead, 0)))
    chip_ids = lax.dynamic_slice_in_dim(tok_ids, 2 * chip_idx, 2, 0).reshape(-1)
    y_ids = ids[:, enc_dev : enc_dev + tgt_dev].reshape(-1)
    t_ids = lax.dynamic_slice_in_dim(ids[:, enc_dev + tgt_dev :].reshape(-1), chip_idx * half, half)
    local = jnp.concatenate([chip_ids, y_ids, t_ids]) - offset
    inside = (local >= 0) & (local < vocab_part)
    picked = jnp.take(embedding, jnp.clip(local, 0, vocab_part - 1), axis=0)
    picked = jnp.where(inside[:, None], picked, jnp.zeros((), jnp.bfloat16))
    theirs = lax.all_gather(picked, "head")
    picked = theirs[0] + theirs[1]
    own_rows = lax.dynamic_slice_in_dim(picked[: 2 * rows], head_idx * rows, rows, 0)
    y0 = picked[2 * rows : 2 * rows + tgt_all].astype(jnp.float32)
    tgt_rows = picked[2 * rows + tgt_all :].astype(jnp.float32)

    length = lengths[ex_idx]
    slot_q = jnp.arange(QUARTERS)[:, None]
    slot_i = jnp.arange(rows)[None, :]
    key_ok = (slot_i < lead) | (tokens * slot_q + slot_i - lead < length)
    lead_rows = lax.dynamic_slice_in_dim(prompt, quarter * lead, lead, 0)
    x0 = jnp.concatenate([lead_rows, own_rows[lead:].astype(jnp.float32)], axis=0)

    n1 = rounded(rms_norm(x0, gains[0]))
    joined = rounded(product(n1, enc_qkv))
    kv = lax.all_gather(joined[:, width:], CLUSTER).reshape(QUARTERS * rows, 2 * width)
    eq = split_heads(joined[:, :width])
    ek = split_heads(kv[:, :width])
    ev = split_heads(kv[:, width:])
    eo, e_lse = attend(eq, ek, ev, key_ok.reshape(1, 1, -1))
    h1 = x0 + product(rounded(join_heads(eo)), enc_wo)
    n2 = rounded(rms_norm(h1, gains[1]))
    pre = product(n2, enc_w1)
    h2 = h1 + product(rounded(gelu_tanh(pre)), enc_w2)
    enc_out = rounded(rms_norm(h2, gains[2]))

    m1 = rounded(rms_norm(y0, gains[3]))
    sqkv = rounded(product(m1, dec_qkv.reshape(width, 3 * own)))
    causal = (jnp.arange(tgt_all)[None, :] <= jnp.arange(tgt_all)[:, None])[None]
    so, _ = attend(
        split_heads(sqkv[:, :own]), split_heads(sqkv[:, own : 2 * own]), split_heads(sqkv[:, 2 * own :]), causal
    )
    a1 = y0 + over_heads(product(rounded(join_heads(so)), dec_wo))
    m2 = rounded(rms_norm(a1, gains[4]))
    cq = split_heads(rounded(product(m2, cross_q)))

    pair = lax.all_gather(enc_out, "head").reshape(2 * rows, width)
    cross_w = cross_kv.reshape(width, 2 * own)
    ckv = rounded(product(pair, cross_w))
    ck, cv = split_heads(ckv[:, :own]), split_heads(ckv[:, own:])
    chip_ok = lax.dynamic_slice_in_dim(key_ok, 2 * chip_idx, 2, 0).reshape(1, 1, -1)
    co_part, lse_part = attend(cq, ck, cv, chip_ok)
    both_o = lax.all_gather(co_part, "chip")
    both_l = lax.all_gather(lse_part, "chip")
    lse = jnp.logaddexp(both_l[0], both_l[1])
    co_all = jnp.sum(both_o * jnp.exp(both_l - lse[None]), axis=0)
    co = join_heads(lax.dynamic_slice_in_dim(co_all, chip_idx * half, half, 1))
    a1_own = lax.dynamic_slice_in_dim(a1, chip_idx * half, half, 0)
    a2 = a1_own + over_heads(product(rounded(co), cross_wo))
    m3 = rounded(rms_norm(a2, gains[5]))
    dec_pre = product(m3, dec_w1)
    a3 = a2 + over_heads(product(rounded(gelu_tanh(dec_pre)), dec_w2))
    final_gain = gains[6] * width ** (-0.5)
    final = rounded(rms_norm(a3, final_gain))

    logits = jnp.einsum("td,vd->tv", final, embedding, preferred_element_type=jnp.float32)
    top = jnp.max(logits, axis=-1, keepdims=True)
    exps = jnp.exp(logits - top)
    total = jnp.sum(exps, axis=-1, keepdims=True)
    acc = product(rounded(exps), embedding) / total
    v_lse = top + jnp.log(total)
    acc_all = lax.all_gather(acc.astype(jnp.bfloat16), "head").astype(jnp.float32)
    l_all = lax.all_gather(v_lse, "head")
    vocab_lse = jnp.logaddexp(l_all[0], l_all[1])
    mean_row = jnp.sum(acc_all * jnp.exp(l_all - vocab_lse[None]), axis=0)
    pick = jnp.sum(final.astype(jnp.float32) * tgt_rows, axis=-1, keepdims=True)
    mask = loss_mask[ex_idx].astype(jnp.float32)
    weight = (lax.dynamic_slice_in_dim(mask, chip_idx * half, half) / jnp.sum(mask))[:, None]
    loss_term = jnp.sum(weight * (vocab_lse - pick)) * jnp.where(head_idx == 0, 1.0, 0.0)
    grad_final = weight * (mean_row - tgt_rows)

    grad_ffn = norm_back(a3, final_gain, grad_final)
    grad_act = back_product(rounded(grad_ffn), dec_w2)
    grad_pre = rounded(gelu_back(dec_pre, grad_act))
    grad_m3 = over_heads(back_product(grad_pre, dec_w1))
    grad_cross = grad_ffn + norm_back(a2, gains[5], grad_m3)
    grad_co = rounded(back_product(rounded(grad_cross), cross_wo))

    gco = split_heads(lax.all_gather(grad_co, "chip").reshape(tgt_all, own))
    delta = jnp.sum(gco.astype(jnp.float32) * co_all, axis=-1, keepdims=True)
    scores = jnp.where(chip_ok, dot_qk(cq, ck) * HD ** (-0.5), NEG)
    probs = jnp.exp(scores - lse)
    ds = rounded(probs * (dot_qk(gco, cv) - delta))
    g_ck = dot_tq(ds, cq) * HD ** (-0.5)
    g_cv = dot_tq(rounded(probs), gco)
    g_pair = back_product(rounded(jnp.concatenate([join_heads(g_ck), join_heads(g_cv)], axis=-1)), cross_w)
    g_both = lax.all_to_all(g_pair.reshape(2, rows, width).astype(jnp.bfloat16), "head", 0, 0)
    g_enc = g_both[0].astype(jnp.float32) + g_both[1].astype(jnp.float32)

    g_two = norm_back(h2, gains[2], g_enc)
    g_act = back_product(rounded(g_two), enc_w2)
    g_pre = rounded(gelu_back(pre, g_act))
    g_one = g_two + norm_back(h1, gains[1], back_product(g_pre, enc_w1))
    g_o = split_heads(rounded(back_product(rounded(g_one), enc_wo)))
    e_delta = jnp.sum(g_o.astype(jnp.float32) * eo, axis=-1, keepdims=True)
    pad = 32

    def head_rows(value):
        return value.reshape(value.shape[0], QUARTERS, rows, HD)[:, :, :pad].reshape(-1, QUARTERS * pad, HD)

    def slopes(queries, keys_in, values_in, grads, lse_in, delta_in, ok):
        scores = jnp.where(ok, dot_qk(queries, keys_in) * HD ** (-0.5), NEG)
        probs = jnp.exp(scores - lse_in)
        return probs, rounded(probs * (dot_qk(grads, values_in) - delta_in))

    ok_lead = key_ok[:, :pad].reshape(1, 1, -1)
    probs, ds = slopes(eq, head_rows(ek), head_rows(ev), g_o, e_lse, e_delta, ok_lead)
    g_k = join_heads(dot_tq(ds, eq) * HD ** (-0.5))
    g_v = join_heads(dot_tq(rounded(probs), g_o))
    g_kv = jnp.concatenate([g_k, g_v], axis=-1).reshape(QUARTERS, pad, 2 * width)
    g_kv = lax.all_to_all(g_kv.astype(jnp.bfloat16), CLUSTER, 0, 0)
    g_kv = jnp.sum(g_kv.astype(jnp.float32), axis=0)
    _, ds = slopes(
        eq[:, :pad], ek, ev, g_o[:, :pad], e_lse[:, :pad], e_delta[:, :pad], key_ok.reshape(1, 1, -1)
    )
    g_q = join_heads(dot_pv(ds, ek) * HD ** (-0.5))
    g_joined = jnp.concatenate([rounded(g_q), rounded(g_kv)], axis=-1)
    g_start = g_one[:pad] + norm_back(x0[:pad], gains[0], back_product(g_joined, enc_qkv))
    block = g_start[:lead]

    line = jnp.zeros((1, width), jnp.float32).at[0, 0].set(loss_term)
    canvas = jnp.zeros((PROMPT + 1, width), jnp.float32)
    canvas = lax.dynamic_update_slice_in_dim(canvas, block, quarter * lead, 0)
    canvas = canvas.at[PROMPT].set(line[0])
    summed = lax.psum(canvas, EVERYONE)
    loss = summed[PROMPT, 0]
    grad_total = summed[:PROMPT]

    grad_norm = jnp.sqrt(jnp.sum(grad_total * grad_total))
    clip_scale = clip_bound / jnp.maximum(grad_norm, clip_bound)
    first_new, second_new, update = lamb_terms(grad_total * clip_scale, first_moment, second_moment, prompt)
    param_norm = jnp.sqrt(jnp.sum(prompt * prompt))
    update_norm = jnp.sqrt(jnp.sum(update * update))
    prompt_new = prompt - learn_rate * (param_norm / update_norm) * update
    return (
        loss,
        grad_norm,
        jnp.stack([param_norm, update_norm]),
        first_new,
        second_new,
        prompt_new,
    )


def solution(mesh):
    finer = Mesh(
        mesh.devices.reshape(mesh.shape["grp"], mesh.shape["seq"] // 2, 2, mesh.shape["head"]),
        ("grp", "ex", "chip", "head"),
    )
    placed = (
        P("grp", SEQ),
        P("grp"),
        P("grp", SEQ),
        P("grp", SEQ),
        P("grp", None),
        P("head", None),
        P(),
        P(),
        P(),
        P(),
        P(),
        P(),
        P(),
        P(),
        P(None, None, "head"),
        P("head", None),
        P(None, "head"),
        P(None, None, "head"),
        P("head", None),
        P(None, "head"),
        P("head", None),
    )
    return jax.shard_map(
        shards,
        mesh=finer,
        in_specs=placed,
        out_specs=(P(), P(), P(), P(), P(), P()),
        check_vma=False,
    )
```

```python
import jax
import jax.numpy as jnp
from jax import lax
from jax.experimental import pallas as pl
from jax.experimental.pallas import tpu as pltpu
from jax.sharding import Mesh
from jax.sharding import PartitionSpec as P

HD = 64
PROMPT = 100
STEP = 5
QUARTERS = 4
SEQ = ("ex", "chip")
CLUSTER = ("chip", "head")
EVERYONE = ("grp", "ex", "chip", "head")
NEG = -1000000000.0

norm_eps = 1e-06
beta_first = 0.5
beta_second = 0.5
adam_eps = 1e-12
decay_rate = 0.01
learn_rate = 0.3
clip_bound = 0.0001


MESH = pl.DeviceIdType.MESH
BF = jnp.bfloat16
F32 = jnp.float32
LEAD_PAD = 32
CHUNK = 1024
RING = 4
LANES = 128


def dot_nn(left, right):
    return lax.dot_general(left, right, (((1,), (0,)), ((), ())), preferred_element_type=F32)


def dot_nt(left, right):
    return lax.dot_general(left, right, (((1,), (1,)), ((), ())), preferred_element_type=F32)


def dot_tn(left, right):
    return lax.dot_general(left, right, (((0,), (0,)), ((), ())), preferred_element_type=F32)


def rms(value, gain):
    return value * lax.rsqrt(jnp.mean(value * value, axis=-1, keepdims=True) + norm_eps) * gain


def rms_grad(value, gain, grad):
    scale = lax.rsqrt(jnp.mean(value * value, axis=-1, keepdims=True) + norm_eps)
    scaled = grad * gain
    inner = jnp.mean(scaled * value, axis=-1, keepdims=True)
    return scale * scaled - value * (scale * scale * scale * inner)


GELU_A = 0.7978845608028654
GELU_B = 0.044715


def gelu(value):
    return 0.5 * value * (1.0 + jnp.tanh(GELU_A * (value + GELU_B * (value * value * value))))


def gelu_grad(value, grad):
    square = value * value
    bend = jnp.tanh(GELU_A * (value + GELU_B * (square * value)))
    slope = 0.5 * (1.0 + bend) + 0.5 * value * (1.0 - bend * bend) * (GELU_A * (1.0 + 3.0 * GELU_B * square))
    return grad * slope


def tiles(count, size, body):
    def step(index, carry):
        body(pl.ds(pl.multiple_of(index * size, size), size))
        return carry

    lax.fori_loop(0, count, step, 0)


def main_kernel(
    picked, lead, ok_all, ok_chip, ok_lead, weight, gains,
    enc_qkv, enc_wo, enc_w1, enc_w2, dec_qkv, dec_wo, cross_q, cross_kv, cross_wo, dec_w1, dec_w2, embedding,
    out,
    w_qkv, w_o, w_1, w_2, w_dqkv, w_do, w_cq, w_ckv, w_co, w_d1, w_d2, ring,
    enc_my, enc_in, dec_my, dec_in,
    x0, h1, h2, go, spare, n1, q_s, kv, o_f, o_b, s_f, p_b, lse_e, sum_e, nb, u, act,
    eo, ckv, dckv, gp_s, gp_r, gown, d_o, dkv, dkv_r, gj, dl,
    y0, a1, m_b, sqkv, so, dx_s, dx_r, cq, cp, cp_b, st_p, st_r, co_r, co, co_b,
    px_s, px_r, a2, a3, du, dact, f_b, tgt, acc, acc_b, acc_r, vl_s, vl_r, gffn, gco, st_g,
    load_sem, ring_sem, send_sem, recv_sem,
):
    width = x0.shape[1]
    rows = x0.shape[0]
    half = f_b.shape[0]
    own = co.shape[1]
    pairs_e, pairs_d = width // LANES, own // LANES
    head, chip = lax.axis_index("head"), lax.axis_index("chip")
    mate, across = 1 - head, 1 - chip
    me, slot_mate = 2 * chip + head, 2 * chip + mate
    slot_across, slot_diag = 2 * across + head, 2 * across + mate
    to_mate, to_across = {"head": mate}, {"chip": across}
    to_diag = {"chip": across, "head": mate}

    barrier = pltpu.get_barrier_semaphore()
    for peer in (to_mate, to_across, to_diag):
        pl.semaphore_signal(barrier, inc=1, device_id=peer, device_id_type=MESH)

    def load(index, source, target):
        copy = pltpu.make_async_copy(source, target, load_sem.at[index])
        copy.start()
        return copy

    my_rows = pl.ds(pl.multiple_of(head * rows, rows), rows)
    mate_rows = pl.ds(pl.multiple_of(mate * rows, rows), rows)
    dec_rows = pl.ds(2 * rows, dec_my.shape[0])
    load_x = load(0, picked.at[my_rows], enc_my)
    load_y = load(1, picked.at[dec_rows], dec_my)
    load_qkv = load(2, enc_qkv, w_qkv)
    load_dqkv = load(3, dec_qkv, w_dqkv)
    load_do = load(4, dec_wo, w_do)
    load_cq = load(5, cross_q, w_cq)
    load_o = load(6, enc_wo, w_o)
    load_1 = load(7, enc_w1, w_1)
    load_2 = load(8, enc_w2, w_2)
    load_ckv = load(9, cross_kv, w_ckv)
    load_co = load(10, cross_wo, w_co)
    load_d1 = load(11, dec_w1, w_d1)
    load_d2 = load(12, dec_w2, w_d2)

    vocab = embedding.shape[0]
    full = vocab // CHUNK
    tail = vocab - full * CHUNK

    def chunk_copy(index, slot):
        at = pl.ds(pl.multiple_of(index * CHUNK, CHUNK), CHUNK)
        return pltpu.make_async_copy(embedding.at[at], ring.at[slot], ring_sem.at[slot])

    def tail_copy():
        slot = full % RING
        return pltpu.make_async_copy(
            embedding.at[pl.ds(full * CHUNK, tail)], ring.at[slot, pl.ds(0, tail)], ring_sem.at[slot]
        )

    for index in range(RING):
        chunk_copy(index, index).start()

    pl.semaphore_wait(barrier, 3)
    sends = []

    def send(index, source, target, peer):
        copy = pltpu.make_async_remote_copy(
            src_ref=source,
            dst_ref=target,
            send_sem=send_sem.at[index],
            recv_sem=recv_sem.at[index],
            device_id=peer,
            device_id_type=MESH,
        )
        copy.start()
        sends.append(copy)
        return copy

    got_x = send(0, picked.at[mate_rows], enc_in, to_mate)
    got_y = send(1, picked.at[dec_rows], dec_in, to_mate)

    lane = lax.broadcasted_iota(jnp.int32, (1, LANES), 1)
    low_lane = lane < HD
    low_b = jnp.where(low_lane, 1.0, 0.0).astype(BF)
    high_b = jnp.where(low_lane, 0.0, 1.0).astype(BF)
    sides = (low_b, high_b)
    gain = [gains[k : k + 1, :] for k in range(7)]

    load_x.wait()
    got_x.wait_recv()
    for block in range(rows // 64):
        part = pl.ds(block * 64, 64)
        value = enc_my[part].astype(F32) + enc_in[part].astype(F32)
        if block == 0:
            spot = lax.broadcasted_iota(jnp.int32, (64, width), 0)
            value = jnp.where(spot < PROMPT // QUARTERS, lead[...], value)
        x0[part] = value
        n1[me, part] = rms(value, gain[0]).astype(BF)
    got_n = send(2, n1.at[me], n1.at[me], to_across)
    got_m = send(3, n1.at[me], n1.at[me], to_mate)

    load_qkv.wait()

    def key_value(slot):
        def body(at):
            cols = pl.ds(pl.multiple_of(width + at.start, 256), 256)
            kv[slot, :, at] = dot_nn(n1[slot], w_qkv[:, cols]).astype(BF)

        tiles(2 * width // 256, 256, body)

    def query(at):
        q_s[:, at] = (dot_nn(n1[me], w_qkv[:, at]).astype(BF) * HD ** (-0.5)).astype(BF)

    key_value(me)
    tiles(width // 256, 256, query)
    got_m.wait_recv()
    key_value(slot_mate)

    load_y.wait()
    got_y.wait_recv()
    all_tgt = y0.shape[0]
    value = dec_my[0:all_tgt].astype(F32) + dec_in[0:all_tgt].astype(F32)
    y0[...] = value
    m_b[...] = rms(value, gain[3]).astype(BF)
    tgt[...] = dec_my[all_tgt : all_tgt + half].astype(F32) + dec_in[all_tgt : all_tgt + half].astype(F32)
    load_dqkv.wait()

    def self_cols(at):
        sqkv[:, at] = dot_nn(m_b[...], w_dqkv[:, at]).astype(BF)

    tiles(3 * own // 384, 384, self_cols)
    row_at = lax.broadcasted_iota(jnp.int32, (all_tgt, all_tgt), 0)
    col_at = lax.broadcasted_iota(jnp.int32, (all_tgt, all_tgt), 1)
    for pair in range(pairs_d):
        lo = pair * LANES
        q2 = sqkv[:, lo : lo + LANES]
        k2 = sqkv[:, own + lo : own + lo + LANES]
        v2 = sqkv[:, 2 * own + lo : 2 * own + lo + LANES]
        outs = []
        for side in sides:
            scores = dot_nt(q2 * side, k2) * HD ** (-0.5)
            scores = jnp.where(col_at <= row_at, scores, NEG)
            top = jnp.max(scores, axis=-1, keepdims=True)
            probs = jnp.exp(scores - top)
            total = jnp.sum(probs, axis=-1, keepdims=True)
            outs.append(dot_nn(probs.astype(BF), v2) / total)
        so[:, lo : lo + LANES] = jnp.where(low_lane, outs[0], outs[1]).astype(BF)
    load_do.wait()

    def self_out(at):
        dx_s[:, at] = dot_nn(so[...], w_do[:, at]).astype(BF)

    tiles(width // 256, 256, self_out)
    got_d = send(4, dx_s, dx_r, to_mate)

    got_n.wait_recv()
    got_f = send(5, n1.at[slot_across], n1.at[slot_across], to_mate)
    key_value(slot_across)

    got_d.wait_recv()
    value = y0[...] + (dx_s[...].astype(F32) + dx_r[...].astype(F32))
    a1[...] = value
    m_b[...] = rms(value, gain[4]).astype(BF)
    load_cq.wait()
    cq[...] = (dot_nn(m_b[...], w_cq[...]).astype(BF) * HD ** (-0.5)).astype(BF)

    got_f.wait_recv()
    key_value(slot_diag)

    keys = 4 * rows
    ok = ok_all[...] > 0.0

    def pair_lanes(at, base):
        return pl.ds(pl.multiple_of(base + at * LANES, LANES), LANES)

    def attend_pair(pair, carry):
        at = pair_lanes(pair, 0)
        q2 = q_s[:, at]
        k2 = kv[:, :, at].reshape(keys, LANES)
        v2 = kv[:, :, pair_lanes(pair, width)].reshape(keys, LANES)
        outs = []
        for index, side in enumerate(sides):
            s_f[...] = dot_nt(q2 * side, k2)
            for block in range(rows // 32):
                part = pl.ds(block * 32, 32)
                scores = jnp.where(ok, s_f[part], NEG)
                top = jnp.max(scores, axis=-1, keepdims=True)
                probs = jnp.exp(scores - top)
                total = jnp.sum(probs, axis=-1, keepdims=True)
                p_b[part] = probs.astype(BF)
                sum_e[index, part] = jnp.broadcast_to(total, (32, LANES))
                lse = jnp.broadcast_to(top + jnp.log(total), (32, LANES))
                if index == 0:
                    lse_e[pair, part] = lse
                else:
                    lse_e[pair, part] = jnp.where(low_lane, lse_e[pair, part], lse)
            outs.append(dot_nn(p_b[...], v2) / sum_e[index])
        both = jnp.where(low_lane, outs[0], outs[1])
        o_f[:, at] = both
        o_b[:, at] = both.astype(BF)
        return carry

    lax.fori_loop(0, pairs_e, attend_pair, 0)
    load_o.wait()

    def out_cols(at):
        h1[:, at] = x0[:, at] + dot_nn(o_b[...], w_o[:, at])

    tiles(width // 256, 256, out_cols)

    def norm_two(at):
        nb[at] = rms(h1[at], gain[1]).astype(BF)

    tiles(rows // 64, 64, norm_two)
    load_1.wait()

    def hidden(at):
        value = dot_nn(nb[...], w_1[:, at])
        u[:, at] = value
        act[:, at] = gelu(value).astype(BF)

    tiles(u.shape[1] // 256, 256, hidden)
    load_2.wait()

    def hidden_out(at):
        h2[:, at] = h1[:, at] + dot_nn(act[...], w_2[:, at])

    tiles(width // 256, 256, hidden_out)

    def norm_out(at):
        eo[head, at] = rms(h2[at], gain[2]).astype(BF)

    tiles(rows // 64, 64, norm_out)
    got_e = send(6, eo.at[head], eo.at[head], to_mate)
    load_ckv.wait()

    def cross_keys(slot):
        def body(at):
            ckv[slot, :, at] = dot_nn(eo[slot], w_ckv[:, at]).astype(BF)

        tiles(2 * own // 256, 256, body)

    cross_keys(head)
    got_e.wait_recv()
    cross_keys(mate)

    okc = ok_chip[...] > 0.0

    def cross_pair(pair):
        lo = pair * LANES
        k2 = ckv[:, :, lo : lo + LANES].reshape(2 * rows, LANES)
        v2 = ckv[:, :, own + lo : own + lo + LANES].reshape(2 * rows, LANES)
        return lo, cq[:, lo : lo + LANES], k2, v2

    stats = jnp.zeros((all_tgt, LANES), F32)
    for pair in range(pairs_d):
        lo, q2, k2, v2 = cross_pair(pair)
        outs = []
        for index, side in enumerate(sides):
            scores = jnp.where(okc, dot_nt(q2 * side, k2), NEG)
            top = jnp.max(scores, axis=-1, keepdims=True)
            probs = jnp.exp(scores - top)
            total = jnp.sum(probs, axis=-1, keepdims=True)
            outs.append(dot_nn(probs.astype(BF), v2) / total)
            stats = jnp.where(lane == 2 * pair + index, top + jnp.log(total), stats)
        both = jnp.where(low_lane, outs[0], outs[1])
        cp[:, lo : lo + LANES] = both
        cp_b[:, lo : lo + LANES] = both.astype(BF)
    st_p[...] = stats
    mine_t = pl.ds(pl.multiple_of(chip * half, half), half)
    theirs_t = pl.ds(pl.multiple_of(across * half, half), half)
    got_c = send(7, cp_b.at[theirs_t], co_r, to_across)
    got_s = send(8, st_p.at[theirs_t], st_r, to_across)
    got_c.wait_recv()
    got_s.wait_recv()
    l_own, l_oth = st_p[mine_t], st_r[...]
    top = jnp.maximum(l_own, l_oth)
    lse_c = top + jnp.log(jnp.exp(l_own - top) + jnp.exp(l_oth - top))
    w_own, w_oth = jnp.exp(l_own - lse_c), jnp.exp(l_oth - lse_c)

    def side_cols(array, pair):
        return jnp.where(
            low_lane, array[:, 2 * pair : 2 * pair + 1], array[:, 2 * pair + 1 : 2 * pair + 2]
        )

    for pair in range(pairs_d):
        lo = pair * LANES
        both = cp[mine_t, lo : lo + LANES] * side_cols(w_own, pair)
        both = both + co_r[:, lo : lo + LANES].astype(F32) * side_cols(w_oth, pair)
        co[:, lo : lo + LANES] = both
        co_b[:, lo : lo + LANES] = both.astype(BF)

    def exchange(index, value):
        slot = index - 9
        px_s[slot] = value.astype(BF)
        got = send(index, px_s.at[slot], px_r.at[slot], to_mate)
        got.wait_recv()
        return px_s[slot].astype(F32) + px_r[slot].astype(F32)

    load_co.wait()
    a2[...] = a1[mine_t] + exchange(9, dot_nn(co_b[...], w_co[...]))
    m_b[0:half] = rms(a2[...], gain[5]).astype(BF)
    load_d1.wait()

    def dec_hidden(at):
        value = dot_nn(m_b[0:half], w_d1[:, at])
        du[:, at] = value
        dact[:, at] = gelu(value).astype(BF)

    tiles(du.shape[1] // 512, 512, dec_hidden)
    load_d2.wait()
    a3[...] = a2[...] + exchange(10, dot_nn(dact[...], w_d2[...]))
    f_b[...] = rms(a3[...], gain[6]).astype(BF)

    acc[...] = jnp.zeros_like(acc)

    def vocab_step(logits, table, top, total):
        new_top = jnp.maximum(top, jnp.max(logits, axis=-1, keepdims=True))
        fade = jnp.exp(top - new_top)
        probs = jnp.exp(logits - new_top)
        acc[...] = acc[...] * fade + dot_nn(probs.astype(BF), table)
        return new_top, total * fade + jnp.sum(probs, axis=-1, keepdims=True)

    def vocab_chunk(index, carry):
        slot = lax.rem(index, RING)
        chunk_copy(index, slot).wait()
        table = ring[slot]
        carry = vocab_step(dot_nt(f_b[...], table), table, *carry)

        @pl.when(index + RING < full)
        def _():
            chunk_copy(index + RING, slot).start()

        @pl.when(index + RING == full)
        def _():
            tail_copy().start()

        return carry

    carry = (jnp.full((half, 1), NEG, F32), jnp.zeros((half, 1), F32))
    carry = lax.fori_loop(0, full, vocab_chunk, carry)
    tail_copy().wait()
    table = ring[full % RING, 0:tail]
    top, total = vocab_step(dot_nt(f_b[...], table), table, *carry)
    acc_b[...] = (acc[...] / total).astype(BF)
    vl_s[...] = jnp.broadcast_to(top + jnp.log(total), vl_s.shape)
    got_a = send(11, acc_b, acc_r, to_mate)
    got_v = send(12, vl_s, vl_r, to_mate)
    pick = jnp.sum(f_b[...].astype(F32) * tgt[...], axis=-1, keepdims=True)
    got_a.wait_recv()
    got_v.wait_recv()
    l_own, l_oth = vl_s[:, 0:1], vl_r[:, 0:1]
    top = jnp.maximum(l_own, l_oth)
    lse_v = top + jnp.log(jnp.exp(l_own - top) + jnp.exp(l_oth - top))
    share = weight[:, 0:1]
    loss = jnp.sum(share * (lse_v - pick), axis=0, keepdims=True) * jnp.where(head == 0, 1.0, 0.0)
    mean_row = acc_b[...].astype(F32) * jnp.exp(l_own - lse_v) + acc_r[...].astype(F32) * jnp.exp(l_oth - lse_v)
    gffn[...] = rms_grad(a3[...], gain[6], share * (mean_row - tgt[...]))

    m_b[0:half] = gffn[...].astype(BF)

    def dec_hidden_grad(at):
        value = dot_nt(m_b[0:half], w_d2[at])
        dact[:, at] = gelu_grad(du[:, at], value).astype(BF)

    tiles(du.shape[1] // 512, 512, dec_hidden_grad)
    slope = exchange(13, dot_nt(dact[...], w_d1[...]))
    gcross = gffn[...] + rms_grad(a2[...], gain[5], slope)
    gco[chip] = dot_nt(gcross.astype(BF), w_co[...]).astype(BF)
    stats = lse_c
    for pair in range(pairs_d):
        lo = pair * LANES
        value = gco[chip, :, lo : lo + LANES].astype(F32) * co[:, lo : lo + LANES]
        for index in range(2):
            picked_side = jnp.where(low_lane == (index == 0), value, 0.0)
            delta = jnp.sum(picked_side, axis=-1, keepdims=True)
            stats = jnp.where(lane == HD + 2 * pair + index, delta, stats)
    st_g[chip] = stats
    got_g = send(14, gco.at[chip], gco.at[chip], to_across)
    got_t = send(15, st_g.at[chip], st_g.at[chip], to_across)
    got_g.wait_recv()
    got_t.wait_recv()

    stats = st_g[...].reshape(all_tgt, LANES)
    for pair in range(pairs_d):
        lo, q2, k2, v2 = cross_pair(pair)
        do2 = gco[:, :, lo : lo + LANES].reshape(all_tgt, LANES)
        dks, dvs = [], []
        for index, side in enumerate(sides):
            column = 2 * pair + index
            scores = jnp.where(okc, dot_nt(q2 * side, k2), NEG)
            probs = jnp.exp(scores - stats[:, column : column + 1])
            dp = dot_nt(do2 * side, v2)
            ds = (probs * (dp - stats[:, HD + column : HD + column + 1])).astype(BF)
            dks.append(dot_tn(ds, q2))
            dvs.append(dot_tn(probs.astype(BF), do2))
        dckv[:, :, lo : lo + LANES] = jnp.where(low_lane, *dks).astype(BF).reshape(2, rows, LANES)
        dckv[:, :, own + lo : own + lo + LANES] = jnp.where(low_lane, *dvs).astype(BF).reshape(2, rows, LANES)

    def pair_grad_mate(at):
        gp_s[:, at] = dot_nt(dckv[mate], w_ckv[at]).astype(BF)

    tiles(width // 256, 256, pair_grad_mate)
    got_p = send(16, gp_s, gp_r, to_mate)

    def pair_grad_mine(at):
        gown[:, at] = dot_nt(dckv[head], w_ckv[at])

    tiles(width // 256, 256, pair_grad_mine)
    got_p.wait_recv()

    def out_grad(at):
        value = rms_grad(h2[at], gain[2], gown[at].astype(BF).astype(F32) + gp_r[at].astype(F32))
        go[at] = value
        nb[at] = value.astype(BF)

    tiles(rows // 64, 64, out_grad)

    def hidden_grad(at):
        act[:, at] = gelu_grad(u[:, at], dot_nt(nb[...], w_2[at])).astype(BF)

    tiles(u.shape[1] // 256, 256, hidden_grad)

    def norm_two_grad(at):
        spare[:, at] = dot_nt(act[...], w_1[at])

    tiles(width // 256, 256, norm_two_grad)

    def one_grad(at):
        value = go[at] + rms_grad(h1[at], gain[1], spare[at])
        go[at] = value
        nb[at] = value.astype(BF)

    tiles(rows // 64, 64, one_grad)

    def attn_grad(at):
        d_o[:, at] = dot_nt(nb[...], w_o[at]).astype(BF)

    tiles(width // 256, 256, attn_grad)

    okl = ok_lead[...] > 0.0
    lead_keys = 4 * LEAD_PAD

    def lead_pair(pair, carry):
        at = pair_lanes(pair, 0)
        vat = pair_lanes(pair, width)
        q2, do2 = q_s[:, at], d_o[:, at]
        k2 = kv[:, 0:LEAD_PAD, at].reshape(lead_keys, LANES)
        v2 = kv[:, 0:LEAD_PAD, vat].reshape(lead_keys, LANES)
        value = do2.astype(F32) * o_f[:, at]
        dks, dvs, deltas = [], [], []
        for index, side in enumerate(sides):
            delta = jnp.sum(jnp.where(low_lane == (index == 0), value, 0.0), axis=-1, keepdims=True)
            deltas.append(delta)
            lse = lse_e[pair, :, index * HD : index * HD + 1]
            scores = jnp.where(okl, dot_nt(q2 * side, k2), NEG)
            probs = jnp.exp(scores - lse)
            ds = (probs * (dot_nt(do2 * side, v2) - delta)).astype(BF)
            dks.append(dot_tn(ds, q2))
            dvs.append(dot_tn(probs.astype(BF), do2))
        dkv[:, :, at] = jnp.where(low_lane, *dks).astype(BF).reshape(4, LEAD_PAD, LANES)
        dkv[:, :, vat] = jnp.where(low_lane, *dvs).astype(BF).reshape(4, LEAD_PAD, LANES)
        dl[pair] = jnp.where(low_lane, *[d[0:LEAD_PAD] for d in deltas])
        return carry

    lax.fori_loop(0, pairs_e, lead_pair, 0)
    got_k = [
        send(17, dkv.at[slot_across], dkv_r.at[1], to_across),
        send(18, dkv.at[slot_diag], dkv_r.at[2], to_diag),
        send(19, dkv.at[slot_mate], dkv_r.at[0], to_mate),
    ]

    def query_pair(pair, carry):
        at = pair_lanes(pair, 0)
        q2, do2 = q_s[0:LEAD_PAD, at], d_o[0:LEAD_PAD, at]
        k2 = kv[:, :, at].reshape(keys, LANES)
        v2 = kv[:, :, pair_lanes(pair, width)].reshape(keys, LANES)
        dqs = []
        for index, side in enumerate(sides):
            column = slice(index * HD, index * HD + 1)
            scores = jnp.where(ok, dot_nt(q2 * side, k2), NEG)
            probs = jnp.exp(scores - lse_e[pair, 0:LEAD_PAD, column])
            ds = (probs * (dot_nt(do2 * side, v2) - dl[pair, :, column])).astype(BF)
            dqs.append(dot_nn(ds, k2) * HD ** (-0.5))
        gj[:, at] = jnp.where(low_lane, *dqs).astype(BF)
        return carry

    lax.fori_loop(0, pairs_e, query_pair, 0)
    for copy in got_k:
        copy.wait_recv()
    summed = dkv[me].astype(F32)
    for index in range(3):
        summed = summed + dkv_r[index].astype(F32)
    gj[:, width:] = summed.astype(BF)

    def start_grad(at):
        spare[0:LEAD_PAD, at] = dot_nt(gj[...], w_qkv[at])

    tiles(width // 256, 256, start_grad)
    top_rows = slice(0, LEAD_PAD)
    value = go[top_rows] + rms_grad(x0[top_rows], gain[0], spare[top_rows])
    spot = lax.broadcasted_iota(jnp.int32, (LEAD_PAD, width), 0)
    extra = jnp.where(spot == PROMPT // QUARTERS, loss, 0.0)
    out[...] = jnp.where(spot < PROMPT // QUARTERS, value, extra)
    for copy in sends:
        copy.wait_send()


def main_call(vmem, hbm):
    rows, half = 256, vmem[4].shape[0]
    wq, wo, w1, w2, dqkv, dwo, cqw, ckvw, cwo, dw1, dw2, emb = hbm[1:]
    width, own, ff, dff, tgt_all = wo.shape[0], dwo.shape[0], w1.shape[1], dw1.shape[1], 2 * half
    pairs_e = width // LANES

    def v(shape, kind=F32):
        return pltpu.VMEM(shape, kind)

    scratch = [v(w.shape, BF) for w in hbm[1:12]]
    scratch += [v((RING, CHUNK, width), BF)]
    scratch += [v((rows, width), BF), v((rows, width), BF), v((tgt_all + half, width), BF), v((tgt_all + half, width), BF)]
    scratch += [v((rows, width)) for _ in range(5)]
    scratch += [v((4, rows, width), BF), v((rows, width), BF), v((4, rows, 2 * width), BF)]
    scratch += [v((rows, width)), v((rows, width), BF), v((rows, 4 * rows)), v((rows, 4 * rows), BF)]
    scratch += [v((pairs_e, rows, LANES)), v((2, rows, LANES)), v((rows, width), BF)]
    scratch += [v((rows, ff)), v((rows, ff), BF)]
    scratch += [v((2, rows, width), BF), v((2, rows, 2 * own), BF), v((2, rows, 2 * own), BF)]
    scratch += [v((rows, width), BF), v((rows, width), BF), v((rows, width)), v((rows, width), BF)]
    scratch += [v((4, LEAD_PAD, 2 * width), BF), v((3, LEAD_PAD, 2 * width), BF), v((LEAD_PAD, 3 * width), BF)]
    scratch += [v((pairs_e, LEAD_PAD, LANES))]
    scratch += [v((tgt_all, width)), v((tgt_all, width)), v((tgt_all, width), BF), v((tgt_all, 3 * own), BF)]
    scratch += [v((tgt_all, own), BF), v((tgt_all, width), BF), v((tgt_all, width), BF), v((tgt_all, own), BF)]
    scratch += [v((tgt_all, own)), v((tgt_all, own), BF), v((tgt_all, LANES)), v((half, LANES))]
    scratch += [v((half, own), BF), v((half, own)), v((half, own), BF)]
    scratch += [v((5, half, width), BF), v((5, half, width), BF)]
    scratch += [v((half, width)), v((half, width)), v((half, dff)), v((half, dff), BF), v((half, width), BF)]
    scratch += [v((half, width)), v((half, width)), v((half, width), BF), v((half, width), BF)]
    scratch += [v((half, LANES)), v((half, LANES)), v((half, width)), v((2, half, own), BF), v((2, half, LANES))]
    scratch += [
        pltpu.SemaphoreType.DMA((13,)),
        pltpu.SemaphoreType.DMA((RING,)),
        pltpu.SemaphoreType.DMA((20,)),
        pltpu.SemaphoreType.DMA((20,)),
    ]
    any_spec, vmem_spec = pl.BlockSpec(memory_space=pl.ANY), pl.BlockSpec(memory_space=pltpu.VMEM)
    return pl.pallas_call(
        main_kernel,
        out_shape=jax.ShapeDtypeStruct((LEAD_PAD, width), F32),
        in_specs=[any_spec] + [vmem_spec] * len(vmem) + [any_spec] * len(hbm[1:]),
        out_specs=vmem_spec,
        scratch_shapes=scratch,
        compiler_params=pltpu.CompilerParams(
            collective_id=1, has_side_effects=True, vmem_limit_bytes=62 * 1024 * 1024
        ),
        name="step_of_one_example",
    )(hbm[0], *vmem, *hbm[1:])


def lamb_terms(clipped, first_old, second_old, param):
    first_next = beta_first * first_old + (1.0 - beta_first) * clipped
    second_next = beta_second * second_old + (1.0 - beta_second) * clipped * clipped
    scaled_first = first_next / (1.0 - beta_first**STEP)
    scaled_second = second_next / (1.0 - beta_second**STEP)
    update = scaled_first / (jnp.sqrt(scaled_second) + adam_eps) + decay_rate * param
    return (first_next, second_next, update)


def shards(
    enc_ids,
    lengths,
    dec_ids,
    target_ids,
    loss_mask,
    embedding,
    prompt,
    first_moment,
    second_moment,
    gains,
    enc_qkv,
    enc_wo,
    enc_w1,
    enc_w2,
    dec_qkv,
    dec_wo,
    cross_q,
    cross_kv,
    cross_wo,
    dec_w1,
    dec_w2,
):
    head_idx = lax.axis_index("head")
    chip_idx = lax.axis_index("chip")
    ex_idx = lax.axis_index("ex")
    quarter = 2 * chip_idx + head_idx
    vocab_part, width = embedding.shape
    own = dec_wo.shape[0]
    offset = head_idx * vocab_part
    enc_dev, tgt_dev = enc_ids.shape[1], dec_ids.shape[1]
    seqs = lax.axis_size(SEQ)
    total_len = enc_dev * seqs
    tgt_all = tgt_dev * seqs
    half = tgt_all // 2
    tokens = (total_len - PROMPT) // QUARTERS
    lead = PROMPT // QUARTERS
    rows = total_len // QUARTERS

    ids = jnp.concatenate([enc_ids, dec_ids, target_ids], axis=1)
    every = lax.all_gather(ids, SEQ)
    ids = lax.dynamic_index_in_dim(every, ex_idx, 1, keepdims=False)
    tok_ids = ids[:, :enc_dev].reshape(-1)[PROMPT:].reshape(QUARTERS, tokens)
    tok_ids = jnp.pad(tok_ids, ((0, 0), (lead, 0)))
    chip_ids = lax.dynamic_slice_in_dim(tok_ids, 2 * chip_idx, 2, 0).reshape(-1)
    y_ids = ids[:, enc_dev : enc_dev + tgt_dev].reshape(-1)
    t_ids = lax.dynamic_slice_in_dim(ids[:, enc_dev + tgt_dev :].reshape(-1), chip_idx * half, half)
    local = jnp.concatenate([chip_ids, y_ids, t_ids]) - offset
    inside = (local >= 0) & (local < vocab_part)
    picked = jnp.take(embedding, jnp.clip(local, 0, vocab_part - 1), axis=0)
    picked = jnp.where(inside[:, None], picked, jnp.zeros((), jnp.bfloat16))
    length = lengths[ex_idx]
    slot_q = jnp.arange(QUARTERS)[:, None]
    slot_i = jnp.arange(rows)[None, :]
    key_ok = ((slot_i < lead) | (tokens * slot_q + slot_i - lead < length)).astype(F32)
    ok_all = key_ok.reshape(1, -1)
    ok_chip = lax.dynamic_slice_in_dim(key_ok, 2 * chip_idx, 2, 0).reshape(1, -1)
    ok_lead = key_ok[:, :LEAD_PAD].reshape(1, -1)
    lead_rows = lax.dynamic_slice_in_dim(prompt, quarter * lead, lead, 0)
    lead_rows = jnp.pad(lead_rows, ((0, 64 - lead), (0, 0)))
    mask = loss_mask[ex_idx].astype(F32)
    weight = lax.dynamic_slice_in_dim(mask, chip_idx * half, half) / jnp.sum(mask)
    weight = jnp.broadcast_to(weight[:, None], (half, LANES))
    scales = jnp.concatenate([gains[:6], gains[6:] * width ** (-0.5), jnp.zeros((1, width), F32)], axis=0)
    block = main_call(
        (lead_rows, ok_all, ok_chip, ok_lead, weight, scales),
        (
            picked,
            enc_qkv,
            enc_wo,
            enc_w1,
            enc_w2,
            dec_qkv.reshape(width, 3 * own),
            dec_wo,
            cross_q,
            cross_kv.reshape(width, 2 * own),
            cross_wo,
            dec_w1,
            dec_w2,
            embedding,
        ),
    )
    canvas = jnp.zeros((PROMPT + 1, width), F32)
    canvas = lax.dynamic_update_slice_in_dim(canvas, block[:lead], quarter * lead, 0)
    canvas = canvas.at[PROMPT].set(block[lead])
    summed = lax.psum(canvas, EVERYONE)
    loss = summed[PROMPT, 0]
    grad_total = summed[:PROMPT]

    grad_norm = jnp.sqrt(jnp.sum(grad_total * grad_total))
    clip_scale = clip_bound / jnp.maximum(grad_norm, clip_bound)
    first_new, second_new, update = lamb_terms(grad_total * clip_scale, first_moment, second_moment, prompt)
    param_norm = jnp.sqrt(jnp.sum(prompt * prompt))
    update_norm = jnp.sqrt(jnp.sum(update * update))
    prompt_new = prompt - learn_rate * (param_norm / update_norm) * update
    return (
        loss,
        grad_norm,
        jnp.stack([param_norm, update_norm]),
        first_new,
        second_new,
        prompt_new,
    )


def solution(mesh):
    finer = Mesh(
        mesh.devices.reshape(mesh.shape["grp"], mesh.shape["seq"] // 2, 2, mesh.shape["head"]),
        ("grp", "ex", "chip", "head"),
    )
    placed = (
        P("grp", SEQ),
        P("grp"),
        P("grp", SEQ),
        P("grp", SEQ),
        P("grp", None),
        P("head", None),
        P(),
        P(),
        P(),
        P(),
        P(),
        P(),
        P(),
        P(),
        P(None, None, "head"),
        P("head", None),
        P(None, "head"),
        P(None, None, "head"),
        P("head", None),
        P(None, "head"),
        P("head", None),
    )
    return jax.shard_map(
        shards,
        mesh=finer,
        in_specs=placed,
        out_specs=(P(), P(), P(), P(), P(), P()),
        check_vma=False,
    )
```

```python
import functools

import jax
import jax.numpy as jnp
from jax import lax
from jax.experimental import pallas as pl
from jax.experimental.pallas import tpu as pltpu
from jax.sharding import Mesh
from jax.sharding import PartitionSpec as P

HD = 64
PROMPT = 100
STEP = 5
QUARTERS = 4
SEQ = ("ex", "chip")
CLUSTER = ("chip", "head")
EVERYONE = ("grp", "ex", "chip", "head")
NEG = -1000000000.0

norm_eps = 1e-06
beta_first = 0.5
beta_second = 0.5
adam_eps = 1e-12
decay_rate = 0.01
learn_rate = 0.3
clip_bound = 0.0001


MESH = pl.DeviceIdType.MESH
BF = jnp.bfloat16
F32 = jnp.float32
LEAD_PAD = 32
CHUNK = 1024
RING = 4
LANES = 128


def dot_nn(left, right):
    return lax.dot_general(left, right, (((1,), (0,)), ((), ())), preferred_element_type=F32)


def dot_nt(left, right):
    return lax.dot_general(left, right, (((1,), (1,)), ((), ())), preferred_element_type=F32)


def dot_tn(left, right):
    return lax.dot_general(left, right, (((0,), (0,)), ((), ())), preferred_element_type=F32)


def rms(value, gain):
    return value * lax.rsqrt(jnp.mean(value * value, axis=-1, keepdims=True) + norm_eps) * gain


def rms_grad(value, gain, grad):
    scale = lax.rsqrt(jnp.mean(value * value, axis=-1, keepdims=True) + norm_eps)
    scaled = grad * gain
    inner = jnp.mean(scaled * value, axis=-1, keepdims=True)
    return scale * scaled - value * (scale * scale * scale * inner)


GELU_A = 0.7978845608028654
GELU_B = 0.044715


def gelu(value):
    return 0.5 * value * (1.0 + jnp.tanh(GELU_A * (value + GELU_B * (value * value * value))))


def gelu_grad(value, grad):
    square = value * value
    bend = jnp.tanh(GELU_A * (value + GELU_B * (square * value)))
    slope = 0.5 * (1.0 + bend) + 0.5 * value * (1.0 - bend * bend) * (GELU_A * (1.0 + 3.0 * GELU_B * square))
    return grad * slope


def tiles(count, size, body):
    def step(index, carry):
        body(pl.ds(pl.multiple_of(index * size, size), size))
        return carry

    lax.fori_loop(0, count, step, 0)


def main_kernel(
    lengths, picked, prompt, loss_mask, gains,
    enc_qkv, enc_wo, enc_w1, enc_w2, dec_qkv, dec_wo, cross_q, cross_kv, cross_wo, dec_w1, dec_w2, embedding,
    out,
    w_qkv, w_o, w_1, w_2, w_dqkv, w_do, w_cq, w_ckv, w_co, w_d1, w_d2, ring,
    lead, enc_my, enc_in, dec_my, dec_in,
    x0, h1, h2, go, spare, n1, q_s, kv, o_f, o_b, s_f, p_b, lse_e, sum_e, nb, u, act,
    eo, ckv, dckv, gp_s, gp_r, gown, d_o, dkv, dkv_r, gj, dl,
    y0, a1, m_b, sqkv, so, dx_s, dx_r, cq, cp, cp_b, st_p, st_r, co_r, co, co_b,
    px_s, px_r, a2, a3, du, dact, f_b, tgt, acc, acc_b, acc_r, vl_s, vl_r, gffn, gco, st_g,
    load_sem, ring_sem, send_sem, recv_sem,
):
    width = x0.shape[1]
    rows = x0.shape[0]
    half = f_b.shape[0]
    own = co.shape[1]
    pairs_e, pairs_d = width // LANES, own // LANES
    head, chip = lax.axis_index("head"), lax.axis_index("chip")
    mate, across = 1 - head, 1 - chip
    me, slot_mate = 2 * chip + head, 2 * chip + mate
    slot_across, slot_diag = 2 * across + head, 2 * across + mate
    to_mate, to_across = {"head": mate}, {"chip": across}
    to_diag = {"chip": across, "head": mate}

    barrier = pltpu.get_barrier_semaphore()
    for peer in (to_mate, to_across, to_diag):
        pl.semaphore_signal(barrier, inc=1, device_id=peer, device_id_type=MESH)

    ex = lax.axis_index("ex")

    def load(index, source, target):
        copy = pltpu.make_async_copy(source, target, load_sem.at[index])
        copy.start()
        return copy

    my_rows = pl.ds(pl.multiple_of(head * rows, rows), rows)
    mate_rows = pl.ds(pl.multiple_of(mate * rows, rows), rows)
    dec_rows = pl.ds(2 * rows, dec_my.shape[0])
    load_x = load(0, picked.at[my_rows], enc_my)
    load_y = load(1, picked.at[dec_rows], dec_my)
    load_qkv = load(2, enc_qkv, w_qkv)
    load_dqkv = load(3, dec_qkv, w_dqkv)
    load_do = load(4, dec_wo, w_do)
    load_cq = load(5, cross_q, w_cq)
    load_o = load(6, enc_wo, w_o)
    load_1 = load(7, enc_w1, w_1)
    load_2 = load(8, enc_w2, w_2)
    load_ckv = load(9, cross_kv, w_ckv)
    load_co = load(10, cross_wo, w_co)
    load_d1 = load(11, dec_w1, w_d1)
    load_d2 = load(12, dec_w2, w_d2)
    leads = PROMPT // QUARTERS

    vocab = embedding.shape[0]
    full = vocab // CHUNK
    tail = vocab - full * CHUNK

    def chunk_copy(index, slot):
        at = pl.ds(pl.multiple_of(index * CHUNK, CHUNK), CHUNK)
        return pltpu.make_async_copy(embedding.at[at], ring.at[slot], ring_sem.at[slot])

    def tail_copy():
        slot = full % RING
        return pltpu.make_async_copy(
            embedding.at[pl.ds(full * CHUNK, tail)], ring.at[slot, pl.ds(0, tail)], ring_sem.at[slot]
        )

    for index in range(RING):
        chunk_copy(index, index).start()

    pl.semaphore_wait(barrier, 3)
    sends = []

    def send(index, source, target, peer):
        copy = pltpu.make_async_remote_copy(
            src_ref=source,
            dst_ref=target,
            send_sem=send_sem.at[index],
            recv_sem=recv_sem.at[index],
            device_id=peer,
            device_id_type=MESH,
        )
        copy.start()
        sends.append(copy)
        return copy

    got_x = send(0, picked.at[mate_rows], enc_in, to_mate)
    got_y = send(1, picked.at[dec_rows], dec_in, to_mate)

    lane = lax.broadcasted_iota(jnp.int32, (1, LANES), 1)
    low_lane = lane < HD
    low_b = jnp.where(low_lane, 1.0, 0.0).astype(BF)
    high_b = jnp.where(low_lane, 0.0, 1.0).astype(BF)
    sides = (low_b, high_b)
    gain = [gains[k : k + 1, :] for k in range(7)]
    gain[6] = gain[6] * width ** (-0.5)
    length = lengths[ex]
    tokens = kv.shape[1] - leads

    def allowed(slots, span, first):
        at = lax.broadcasted_iota(jnp.int32, (1, slots * span), 1)
        slot = at // span
        inner = at - slot * span
        return (inner < leads) | (tokens * (slot + first) + inner - leads < length)

    ok = allowed(4, rows, 0)
    okc = allowed(2, rows, 2 * chip)
    okl = allowed(4, LEAD_PAD, 0)
    mask_row = loss_mask[pl.ds(ex, 1), :].astype(F32)
    lane_at = lax.broadcasted_iota(jnp.int32, (half, mask_row.shape[1]), 1)
    row_of = lax.broadcasted_iota(jnp.int32, (half, mask_row.shape[1]), 0)
    own_mask = jnp.where(lane_at == row_of + chip * half, jnp.broadcast_to(mask_row, lane_at.shape), 0.0)
    share = jnp.sum(own_mask, axis=-1, keepdims=True) / jnp.sum(mask_row, axis=-1, keepdims=True)

    load_x.wait()
    got_x.wait_recv()
    for block in range(rows // 64):
        part = pl.ds(block * 64, 64)
        value = enc_my[part].astype(F32) + enc_in[part].astype(F32)
        if block == 0:
            spot = lax.broadcasted_iota(jnp.int32, (64, width), 0)
            for slot in range(QUARTERS):
                lead[0:leads] = jnp.where(me == slot, prompt[slot * leads : (slot + 1) * leads], lead[0:leads])
            value = jnp.where(spot < leads, lead[...], value)
        x0[part] = value
        n1[me, part] = rms(value, gain[0]).astype(BF)
    got_n = send(2, n1.at[me], n1.at[me], to_across)
    got_m = send(3, n1.at[me], n1.at[me], to_mate)

    load_qkv.wait()

    def key_value(slot):
        def body(at):
            cols = pl.ds(pl.multiple_of(width + at.start, 256), 256)
            kv[slot, :, at] = dot_nn(n1[slot], w_qkv[:, cols]).astype(BF)

        tiles(2 * width // 256, 256, body)

    def query(at):
        q_s[:, at] = (dot_nn(n1[me], w_qkv[:, at]).astype(BF) * HD ** (-0.5)).astype(BF)

    key_value(me)
    tiles(width // 256, 256, query)
    got_m.wait_recv()
    key_value(slot_mate)

    load_y.wait()
    got_y.wait_recv()
    all_tgt = y0.shape[0]
    value = dec_my[0:all_tgt].astype(F32) + dec_in[0:all_tgt].astype(F32)
    y0[...] = value
    m_b[...] = rms(value, gain[3]).astype(BF)
    tgt[...] = dec_my[all_tgt : all_tgt + half].astype(F32) + dec_in[all_tgt : all_tgt + half].astype(F32)
    load_dqkv.wait()

    def self_cols(at):
        sqkv[:, at] = dot_nn(m_b[...], w_dqkv[:, at]).astype(BF)

    tiles(3 * own // 384, 384, self_cols)
    row_at = lax.broadcasted_iota(jnp.int32, (all_tgt, all_tgt), 0)
    col_at = lax.broadcasted_iota(jnp.int32, (all_tgt, all_tgt), 1)
    for pair in range(pairs_d):
        lo = pair * LANES
        q2 = sqkv[:, lo : lo + LANES]
        k2 = sqkv[:, own + lo : own + lo + LANES]
        v2 = sqkv[:, 2 * own + lo : 2 * own + lo + LANES]
        outs = []
        for side in sides:
            scores = dot_nt(q2 * side, k2) * HD ** (-0.5)
            scores = jnp.where(col_at <= row_at, scores, NEG)
            top = jnp.max(scores, axis=-1, keepdims=True)
            probs = jnp.exp(scores - top)
            total = jnp.sum(probs, axis=-1, keepdims=True)
            outs.append(dot_nn(probs.astype(BF), v2) / total)
        so[:, lo : lo + LANES] = jnp.where(low_lane, outs[0], outs[1]).astype(BF)
    load_do.wait()

    def self_out(at):
        dx_s[:, at] = dot_nn(so[...], w_do[:, at]).astype(BF)

    tiles(width // 256, 256, self_out)
    got_d = send(4, dx_s, dx_r, to_mate)

    got_n.wait_recv()
    got_f = send(5, n1.at[slot_across], n1.at[slot_across], to_mate)
    key_value(slot_across)

    got_d.wait_recv()
    value = y0[...] + (dx_s[...].astype(F32) + dx_r[...].astype(F32))
    a1[...] = value
    m_b[...] = rms(value, gain[4]).astype(BF)
    load_cq.wait()
    cq[...] = (dot_nn(m_b[...], w_cq[...]).astype(BF) * HD ** (-0.5)).astype(BF)

    got_f.wait_recv()
    key_value(slot_diag)

    keys = 4 * rows

    def pair_lanes(at, base):
        return pl.ds(pl.multiple_of(base + at * LANES, LANES), LANES)

    def attend_pair(pair, carry):
        at = pair_lanes(pair, 0)
        q2 = q_s[:, at]
        k2 = kv[:, :, at].reshape(keys, LANES)
        v2 = kv[:, :, pair_lanes(pair, width)].reshape(keys, LANES)
        outs = []
        for index, side in enumerate(sides):
            s_f[...] = dot_nt(q2 * side, k2)
            for block in range(rows // 32):
                part = pl.ds(block * 32, 32)
                scores = jnp.where(ok, s_f[part], NEG)
                top = jnp.max(scores, axis=-1, keepdims=True)
                probs = jnp.exp(scores - top)
                total = jnp.sum(probs, axis=-1, keepdims=True)
                p_b[part] = probs.astype(BF)
                sum_e[index, part] = jnp.broadcast_to(total, (32, LANES))
                lse = jnp.broadcast_to(top + jnp.log(total), (32, LANES))
                if index == 0:
                    lse_e[pair, part] = lse
                else:
                    lse_e[pair, part] = jnp.where(low_lane, lse_e[pair, part], lse)
            outs.append(dot_nn(p_b[...], v2) / sum_e[index])
        both = jnp.where(low_lane, outs[0], outs[1])
        o_f[:, at] = both
        o_b[:, at] = both.astype(BF)
        return carry

    lax.fori_loop(0, pairs_e, attend_pair, 0)
    load_o.wait()

    def out_cols(at):
        h1[:, at] = x0[:, at] + dot_nn(o_b[...], w_o[:, at])

    tiles(width // 256, 256, out_cols)

    def norm_two(at):
        nb[at] = rms(h1[at], gain[1]).astype(BF)

    tiles(rows // 64, 64, norm_two)
    load_1.wait()

    def hidden(at):
        value = dot_nn(nb[...], w_1[:, at])
        u[:, at] = value
        act[:, at] = gelu(value).astype(BF)

    tiles(u.shape[1] // 256, 256, hidden)
    load_2.wait()

    def hidden_out(at):
        h2[:, at] = h1[:, at] + dot_nn(act[...], w_2[:, at])

    tiles(width // 256, 256, hidden_out)

    def norm_out(at):
        eo[head, at] = rms(h2[at], gain[2]).astype(BF)

    tiles(rows // 64, 64, norm_out)
    got_e = send(6, eo.at[head], eo.at[head], to_mate)
    load_ckv.wait()

    def cross_keys(slot):
        def body(at):
            ckv[slot, :, at] = dot_nn(eo[slot], w_ckv[:, at]).astype(BF)

        tiles(2 * own // 256, 256, body)

    cross_keys(head)
    got_e.wait_recv()
    cross_keys(mate)


    def cross_pair(pair):
        lo = pair * LANES
        k2 = ckv[:, :, lo : lo + LANES].reshape(2 * rows, LANES)
        v2 = ckv[:, :, own + lo : own + lo + LANES].reshape(2 * rows, LANES)
        return lo, cq[:, lo : lo + LANES], k2, v2

    stats = jnp.zeros((all_tgt, LANES), F32)
    for pair in range(pairs_d):
        lo, q2, k2, v2 = cross_pair(pair)
        outs = []
        for index, side in enumerate(sides):
            scores = jnp.where(okc, dot_nt(q2 * side, k2), NEG)
            top = jnp.max(scores, axis=-1, keepdims=True)
            probs = jnp.exp(scores - top)
            total = jnp.sum(probs, axis=-1, keepdims=True)
            outs.append(dot_nn(probs.astype(BF), v2) / total)
            stats = jnp.where(lane == 2 * pair + index, top + jnp.log(total), stats)
        both = jnp.where(low_lane, outs[0], outs[1])
        cp[:, lo : lo + LANES] = both
        cp_b[:, lo : lo + LANES] = both.astype(BF)
    st_p[...] = stats
    mine_t = pl.ds(pl.multiple_of(chip * half, half), half)
    theirs_t = pl.ds(pl.multiple_of(across * half, half), half)
    got_c = send(7, cp_b.at[theirs_t], co_r, to_across)
    got_s = send(8, st_p.at[theirs_t], st_r, to_across)
    got_c.wait_recv()
    got_s.wait_recv()
    l_own, l_oth = st_p[mine_t], st_r[...]
    top = jnp.maximum(l_own, l_oth)
    lse_c = top + jnp.log(jnp.exp(l_own - top) + jnp.exp(l_oth - top))
    w_own, w_oth = jnp.exp(l_own - lse_c), jnp.exp(l_oth - lse_c)

    def side_cols(array, pair):
        return jnp.where(
            low_lane, array[:, 2 * pair : 2 * pair + 1], array[:, 2 * pair + 1 : 2 * pair + 2]
        )

    for pair in range(pairs_d):
        lo = pair * LANES
        both = cp[mine_t, lo : lo + LANES] * side_cols(w_own, pair)
        both = both + co_r[:, lo : lo + LANES].astype(F32) * side_cols(w_oth, pair)
        co[:, lo : lo + LANES] = both
        co_b[:, lo : lo + LANES] = both.astype(BF)

    def exchange(index, value):
        slot = index - 9
        px_s[slot] = value.astype(BF)
        got = send(index, px_s.at[slot], px_r.at[slot], to_mate)
        got.wait_recv()
        return px_s[slot].astype(F32) + px_r[slot].astype(F32)

    load_co.wait()
    a2[...] = a1[mine_t] + exchange(9, dot_nn(co_b[...], w_co[...]))
    m_b[0:half] = rms(a2[...], gain[5]).astype(BF)
    load_d1.wait()

    def dec_hidden(at):
        value = dot_nn(m_b[0:half], w_d1[:, at])
        du[:, at] = value
        dact[:, at] = gelu(value).astype(BF)

    tiles(du.shape[1] // 512, 512, dec_hidden)
    load_d2.wait()
    a3[...] = a2[...] + exchange(10, dot_nn(dact[...], w_d2[...]))
    f_b[...] = rms(a3[...], gain[6]).astype(BF)

    acc[...] = jnp.zeros_like(acc)

    def vocab_step(logits, table, top, total):
        new_top = jnp.maximum(top, jnp.max(logits, axis=-1, keepdims=True))
        fade = jnp.exp(top - new_top)
        probs = jnp.exp(logits - new_top)
        acc[...] = acc[...] * fade + dot_nn(probs.astype(BF), table)
        return new_top, total * fade + jnp.sum(probs, axis=-1, keepdims=True)

    def vocab_chunk(index, carry):
        slot = lax.rem(index, RING)
        chunk_copy(index, slot).wait()
        table = ring[slot]
        carry = vocab_step(dot_nt(f_b[...], table), table, *carry)

        @pl.when(index + RING < full)
        def _():
            chunk_copy(index + RING, slot).start()

        @pl.when(index + RING == full)
        def _():
            tail_copy().start()

        return carry

    carry = (jnp.full((half, 1), NEG, F32), jnp.zeros((half, 1), F32))
    carry = lax.fori_loop(0, full, vocab_chunk, carry)
    tail_copy().wait()
    table = ring[full % RING, 0:tail]
    top, total = vocab_step(dot_nt(f_b[...], table), table, *carry)
    acc_b[...] = (acc[...] / total).astype(BF)
    vl_s[...] = jnp.broadcast_to(top + jnp.log(total), vl_s.shape)
    got_a = send(11, acc_b, acc_r, to_mate)
    got_v = send(12, vl_s, vl_r, to_mate)
    pick = jnp.sum(f_b[...].astype(F32) * tgt[...], axis=-1, keepdims=True)
    got_a.wait_recv()
    got_v.wait_recv()
    l_own, l_oth = vl_s[:, 0:1], vl_r[:, 0:1]
    top = jnp.maximum(l_own, l_oth)
    lse_v = top + jnp.log(jnp.exp(l_own - top) + jnp.exp(l_oth - top))
    loss = jnp.sum(share * (lse_v - pick), axis=0, keepdims=True) * jnp.where(head == 0, 1.0, 0.0)
    mean_row = acc_b[...].astype(F32) * jnp.exp(l_own - lse_v) + acc_r[...].astype(F32) * jnp.exp(l_oth - lse_v)
    gffn[...] = rms_grad(a3[...], gain[6], share * (mean_row - tgt[...]))

    m_b[0:half] = gffn[...].astype(BF)

    def dec_hidden_grad(at):
        value = dot_nt(m_b[0:half], w_d2[at])
        dact[:, at] = gelu_grad(du[:, at], value).astype(BF)

    tiles(du.shape[1] // 512, 512, dec_hidden_grad)
    slope = exchange(13, dot_nt(dact[...], w_d1[...]))
    gcross = gffn[...] + rms_grad(a2[...], gain[5], slope)
    gco[chip] = dot_nt(gcross.astype(BF), w_co[...]).astype(BF)
    stats = lse_c
    for pair in range(pairs_d):
        lo = pair * LANES
        value = gco[chip, :, lo : lo + LANES].astype(F32) * co[:, lo : lo + LANES]
        for index in range(2):
            picked_side = jnp.where(low_lane == (index == 0), value, 0.0)
            delta = jnp.sum(picked_side, axis=-1, keepdims=True)
            stats = jnp.where(lane == HD + 2 * pair + index, delta, stats)
    st_g[chip] = stats
    got_g = send(14, gco.at[chip], gco.at[chip], to_across)
    got_t = send(15, st_g.at[chip], st_g.at[chip], to_across)
    got_g.wait_recv()
    got_t.wait_recv()

    stats = st_g[...].reshape(all_tgt, LANES)
    for pair in range(pairs_d):
        lo, q2, k2, v2 = cross_pair(pair)
        do2 = gco[:, :, lo : lo + LANES].reshape(all_tgt, LANES)
        dks, dvs = [], []
        for index, side in enumerate(sides):
            column = 2 * pair + index
            scores = jnp.where(okc, dot_nt(q2 * side, k2), NEG)
            probs = jnp.exp(scores - stats[:, column : column + 1])
            dp = dot_nt(do2 * side, v2)
            ds = (probs * (dp - stats[:, HD + column : HD + column + 1])).astype(BF)
            dks.append(dot_tn(ds, q2))
            dvs.append(dot_tn(probs.astype(BF), do2))
        dckv[:, :, lo : lo + LANES] = jnp.where(low_lane, *dks).astype(BF).reshape(2, rows, LANES)
        dckv[:, :, own + lo : own + lo + LANES] = jnp.where(low_lane, *dvs).astype(BF).reshape(2, rows, LANES)

    def pair_grad_mate(at):
        gp_s[:, at] = dot_nt(dckv[mate], w_ckv[at]).astype(BF)

    tiles(width // 256, 256, pair_grad_mate)
    got_p = send(16, gp_s, gp_r, to_mate)

    def pair_grad_mine(at):
        gown[:, at] = dot_nt(dckv[head], w_ckv[at])

    tiles(width // 256, 256, pair_grad_mine)
    got_p.wait_recv()

    def out_grad(at):
        value = rms_grad(h2[at], gain[2], gown[at].astype(BF).astype(F32) + gp_r[at].astype(F32))
        go[at] = value
        nb[at] = value.astype(BF)

    tiles(rows // 64, 64, out_grad)

    def hidden_grad(at):
        act[:, at] = gelu_grad(u[:, at], dot_nt(nb[...], w_2[at])).astype(BF)

    tiles(u.shape[1] // 256, 256, hidden_grad)

    def norm_two_grad(at):
        spare[:, at] = dot_nt(act[...], w_1[at])

    tiles(width // 256, 256, norm_two_grad)

    def one_grad(at):
        value = go[at] + rms_grad(h1[at], gain[1], spare[at])
        go[at] = value
        nb[at] = value.astype(BF)

    tiles(rows // 64, 64, one_grad)

    def attn_grad(at):
        d_o[:, at] = dot_nt(nb[...], w_o[at]).astype(BF)

    tiles(width // 256, 256, attn_grad)

    lead_keys = 4 * LEAD_PAD

    def lead_pair(pair, carry):
        at = pair_lanes(pair, 0)
        vat = pair_lanes(pair, width)
        q2, do2 = q_s[:, at], d_o[:, at]
        k2 = kv[:, 0:LEAD_PAD, at].reshape(lead_keys, LANES)
        v2 = kv[:, 0:LEAD_PAD, vat].reshape(lead_keys, LANES)
        value = do2.astype(F32) * o_f[:, at]
        dks, dvs, deltas = [], [], []
        for index, side in enumerate(sides):
            delta = jnp.sum(jnp.where(low_lane == (index == 0), value, 0.0), axis=-1, keepdims=True)
            deltas.append(delta)
            lse = lse_e[pair, :, index * HD : index * HD + 1]
            scores = jnp.where(okl, dot_nt(q2 * side, k2), NEG)
            probs = jnp.exp(scores - lse)
            ds = (probs * (dot_nt(do2 * side, v2) - delta)).astype(BF)
            dks.append(dot_tn(ds, q2))
            dvs.append(dot_tn(probs.astype(BF), do2))
        dkv[:, :, at] = jnp.where(low_lane, *dks).astype(BF).reshape(4, LEAD_PAD, LANES)
        dkv[:, :, vat] = jnp.where(low_lane, *dvs).astype(BF).reshape(4, LEAD_PAD, LANES)
        dl[pair] = jnp.where(low_lane, *[d[0:LEAD_PAD] for d in deltas])
        return carry

    lax.fori_loop(0, pairs_e, lead_pair, 0)
    got_k = [
        send(17, dkv.at[slot_across], dkv_r.at[1], to_across),
        send(18, dkv.at[slot_diag], dkv_r.at[2], to_diag),
        send(19, dkv.at[slot_mate], dkv_r.at[0], to_mate),
    ]

    def query_pair(pair, carry):
        at = pair_lanes(pair, 0)
        q2, do2 = q_s[0:LEAD_PAD, at], d_o[0:LEAD_PAD, at]
        k2 = kv[:, :, at].reshape(keys, LANES)
        v2 = kv[:, :, pair_lanes(pair, width)].reshape(keys, LANES)
        dqs = []
        for index, side in enumerate(sides):
            column = slice(index * HD, index * HD + 1)
            scores = jnp.where(ok, dot_nt(q2 * side, k2), NEG)
            probs = jnp.exp(scores - lse_e[pair, 0:LEAD_PAD, column])
            ds = (probs * (dot_nt(do2 * side, v2) - dl[pair, :, column])).astype(BF)
            dqs.append(dot_nn(ds, k2) * HD ** (-0.5))
        gj[:, at] = jnp.where(low_lane, *dqs).astype(BF)
        return carry

    lax.fori_loop(0, pairs_e, query_pair, 0)
    for copy in got_k:
        copy.wait_recv()
    summed = dkv[me].astype(F32)
    for index in range(3):
        summed = summed + dkv_r[index].astype(F32)
    gj[:, width:] = summed.astype(BF)

    def start_grad(at):
        spare[0:LEAD_PAD, at] = dot_nt(gj[...], w_qkv[at])

    tiles(width // 256, 256, start_grad)
    top_rows = slice(0, LEAD_PAD)
    value = go[top_rows] + rms_grad(x0[top_rows], gain[0], spare[top_rows])
    spot = lax.broadcasted_iota(jnp.int32, (LEAD_PAD, width), 0)
    extra = jnp.where(spot == leads, loss, 0.0)
    out[...] = jnp.where(spot < leads, value, extra)
    for copy in sends:
        copy.wait_send()


def main_call(lengths, vmem, hbm):
    half = vmem[1].shape[1] // 2
    rows = (hbm[0].shape[0] - 3 * half) // 2
    wq, wo, w1, w2, dqkv, dwo, cqw, ckvw, cwo, dw1, dw2, emb = hbm[1:]
    width, own, ff, dff, tgt_all = wo.shape[0], dwo.shape[0], w1.shape[1], dw1.shape[1], 2 * half
    pairs_e = width // LANES

    def v(shape, kind=F32):
        return pltpu.VMEM(shape, kind)

    scratch = [v(w.shape, BF) for w in hbm[1:12]]
    scratch += [v((RING, CHUNK, width), BF)]
    scratch += [v((64, width))]
    scratch += [v((rows, width), BF), v((rows, width), BF), v((tgt_all + half, width), BF), v((tgt_all + half, width), BF)]
    scratch += [v((rows, width)) for _ in range(5)]
    scratch += [v((4, rows, width), BF), v((rows, width), BF), v((4, rows, 2 * width), BF)]
    scratch += [v((rows, width)), v((rows, width), BF), v((rows, 4 * rows)), v((rows, 4 * rows), BF)]
    scratch += [v((pairs_e, rows, LANES)), v((2, rows, LANES)), v((rows, width), BF)]
    scratch += [v((rows, ff)), v((rows, ff), BF)]
    scratch += [v((2, rows, width), BF), v((2, rows, 2 * own), BF), v((2, rows, 2 * own), BF)]
    scratch += [v((rows, width), BF), v((rows, width), BF), v((rows, width)), v((rows, width), BF)]
    scratch += [v((4, LEAD_PAD, 2 * width), BF), v((3, LEAD_PAD, 2 * width), BF), v((LEAD_PAD, 3 * width), BF)]
    scratch += [v((pairs_e, LEAD_PAD, LANES))]
    scratch += [v((tgt_all, width)), v((tgt_all, width)), v((tgt_all, width), BF), v((tgt_all, 3 * own), BF)]
    scratch += [v((tgt_all, own), BF), v((tgt_all, width), BF), v((tgt_all, width), BF), v((tgt_all, own), BF)]
    scratch += [v((tgt_all, own)), v((tgt_all, own), BF), v((tgt_all, LANES)), v((half, LANES))]
    scratch += [v((half, own), BF), v((half, own)), v((half, own), BF)]
    scratch += [v((5, half, width), BF), v((5, half, width), BF)]
    scratch += [v((half, width)), v((half, width)), v((half, dff)), v((half, dff), BF), v((half, width), BF)]
    scratch += [v((half, width)), v((half, width)), v((half, width), BF), v((half, width), BF)]
    scratch += [v((half, LANES)), v((half, LANES)), v((half, width)), v((2, half, own), BF), v((2, half, LANES))]
    scratch += [
        pltpu.SemaphoreType.DMA((13,)),
        pltpu.SemaphoreType.DMA((RING,)),
        pltpu.SemaphoreType.DMA((20,)),
        pltpu.SemaphoreType.DMA((20,)),
    ]
    any_spec, vmem_spec = pl.BlockSpec(memory_space=pl.ANY), pl.BlockSpec(memory_space=pltpu.VMEM)
    return pl.pallas_call(
        main_kernel,
        out_shape=jax.ShapeDtypeStruct((LEAD_PAD, width), F32),
        in_specs=[pl.BlockSpec(memory_space=pltpu.SMEM), any_spec] + [vmem_spec] * len(vmem) + [any_spec] * len(hbm[1:]),
        out_specs=vmem_spec,
        scratch_shapes=scratch,
        compiler_params=pltpu.CompilerParams(
            collective_id=1, has_side_effects=True, vmem_limit_bytes=62 * 1024 * 1024
        ),
        name="step_of_one_example",
    )(lengths, hbm[0], *vmem, *hbm[1:])


def ids_kernel(enc_ids, dec_ids, target_ids, out, lines, got, unused, send_sem, recv_sem):
    ex, chip = lax.axis_index("ex"), lax.axis_index("chip")
    chips = lax.axis_size("chip")
    seqs = lax.axis_size(SEQ)
    me = ex * chips + chip
    enc_dev, tgt_dev = enc_ids.shape[1], dec_ids.shape[1]

    def peer_of(step):
        peer = lax.rem(me + step, seqs)
        row = peer // chips
        return row, {"ex": row, "chip": lax.rem(peer, chips)}

    barrier = pltpu.get_barrier_semaphore()

    def greet(step, carry):
        pl.semaphore_signal(barrier, inc=1, device_id=peer_of(step)[1], device_id_type=MESH)
        return carry

    lax.fori_loop(1, seqs, greet, 0)
    lines[:, 0:enc_dev] = enc_ids[...]
    lines[:, enc_dev : enc_dev + tgt_dev] = dec_ids[...]
    lines[:, enc_dev + tgt_dev : enc_dev + 2 * tgt_dev] = target_ids[...]
    lines[:, enc_dev + 2 * tgt_dev :] = jnp.zeros((lines.shape[0], lines.shape[1] - enc_dev - 2 * tgt_dev), jnp.int32)
    pl.semaphore_wait(barrier, seqs - 1)

    def start(step, carry):
        row, peer = peer_of(step)
        pltpu.make_async_remote_copy(
            src_ref=lines.at[pl.ds(row, 1)],
            dst_ref=got.at[pl.ds(me, 1)],
            send_sem=send_sem,
            recv_sem=recv_sem,
            device_id=peer,
            device_id_type=MESH,
        ).start()
        return carry

    lax.fori_loop(1, seqs, start, 0)
    own_line = lines.at[pl.ds(ex, 1)]
    pltpu.make_async_copy(own_line, got.at[pl.ds(me, 1)], recv_sem).start()
    pltpu.make_async_copy(own_line, unused.at[pl.ds(0, 1)], send_sem).start()
    pltpu.make_async_copy(got, got, recv_sem).wait()
    pltpu.make_async_copy(got, got, send_sem).wait()
    out[...] = got[...]


def ids_call(enc_ids, dec_ids, target_ids):
    seqs = lax.axis_size(SEQ)
    lanes = -(-(enc_ids.shape[1] + 2 * dec_ids.shape[1]) // LANES) * LANES
    return pl.pallas_call(
        ids_kernel,
        out_shape=jax.ShapeDtypeStruct((seqs, lanes), jnp.int32),
        in_specs=[pl.BlockSpec(memory_space=pltpu.VMEM)] * 3,
        out_specs=pl.BlockSpec(memory_space=pltpu.VMEM),
        scratch_shapes=[
            pltpu.VMEM((enc_ids.shape[0], lanes), jnp.int32),
            pltpu.VMEM((seqs, lanes), jnp.int32),
            pltpu.VMEM((8, lanes), jnp.int32),
            pltpu.SemaphoreType.DMA,
            pltpu.SemaphoreType.DMA,
        ],
        compiler_params=pltpu.CompilerParams(collective_id=2, has_side_effects=True),
        name="ids_of_one_example",
    )(enc_ids, dec_ids, target_ids)


GROUP = 16


def lookup_kernel(rows, tokens, lead, enc_dev, tgt_dev, ids, table, out, blocks, spots, sems):
    chip, head = lax.axis_index("chip"), lax.axis_index("head")
    vocab_part = table.shape[0]
    offset = head * vocab_part
    enc_count = 2 * rows
    tgt_all = tgt_dev * ids.shape[0]
    half = tgt_all // 2
    groups = out.shape[0] // GROUP

    def fetch(group, place):
        for k in range(GROUP):
            seq_at, lane_at = place(k)
            local = ids[seq_at, lane_at] - offset
            inside = (local >= 0) & (local < vocab_part)
            safe = jnp.clip(local, 0, vocab_part - 1)
            block = safe // GROUP
            spots[group * GROUP + k] = jnp.where(inside, k * GROUP + safe - block * GROUP, -1)
            pltpu.make_async_copy(
                table.at[pl.ds(pl.multiple_of(block * GROUP, GROUP), GROUP)],
                blocks.at[group * GROUP + k],
                sems.at[group],
            ).start()

    def fetch_enc(group, carry):
        def place(k):
            item = group * GROUP + k
            slot = item // rows
            at = (PROMPT - lead) + tokens * (2 * chip + slot) + (item - slot * rows)
            seq_at = at // enc_dev
            return seq_at, at - seq_at * enc_dev

        fetch(group, place)
        return carry

    def fetch_tgt(base, start, lane):
        def body(group, carry):
            def place(k):
                item = (group - base) * GROUP + k + start
                seq_at = item // tgt_dev
                return seq_at, lane + item - seq_at * tgt_dev

            fetch(group, place)
            return carry

        return body

    first, second = enc_count // GROUP, (enc_count + tgt_all) // GROUP
    lax.fori_loop(0, first, fetch_enc, 0)
    lax.fori_loop(first, second, fetch_tgt(first, 0, enc_dev), 0)
    lax.fori_loop(second, groups, fetch_tgt(second, chip * half, enc_dev + tgt_dev), 0)

    across = lax.broadcasted_iota(jnp.int32, (GROUP, GROUP * GROUP), 1)
    down = lax.broadcasted_iota(jnp.int32, (GROUP, GROUP * GROUP), 0)

    def select(group, carry):
        at = pl.ds(pl.multiple_of(group * GROUP, GROUP), GROUP)
        pltpu.make_async_copy(blocks.at[at], blocks.at[at], sems.at[group]).wait()
        want = jnp.full((GROUP, GROUP * GROUP), -1, jnp.int32)
        for k in range(GROUP):
            want = jnp.where(down == k, spots[group * GROUP + k], want)
        chosen = jnp.where(across == want, 1.0, 0.0).astype(BF)
        out[at] = dot_nn(chosen, blocks[at].reshape(GROUP * GROUP, out.shape[1])).astype(BF)
        return carry

    lax.fori_loop(0, groups, select, 0)


def lookup_call(ids, table, rows, tokens, lead, enc_dev, tgt_dev):
    count = 2 * rows + tgt_dev * ids.shape[0] * 3 // 2
    width = table.shape[1]
    return pl.pallas_call(
        functools.partial(lookup_kernel, rows, tokens, lead, enc_dev, tgt_dev),
        out_shape=jax.ShapeDtypeStruct((count, width), BF),
        in_specs=[pl.BlockSpec(memory_space=pltpu.SMEM), pl.BlockSpec(memory_space=pl.ANY)],
        out_specs=pl.BlockSpec(memory_space=pltpu.VMEM),
        scratch_shapes=[
            pltpu.VMEM((count, GROUP, width), BF),
            pltpu.SMEM((count,), jnp.int32),
            pltpu.SemaphoreType.DMA((count // GROUP,)),
        ],
        compiler_params=pltpu.CompilerParams(vmem_limit_bytes=32 * 1024 * 1024),
        name="embedding_rows",
    )(ids, table)


def sum_kernel(share, block, out, parts, unused, total, gathered, send_sem, recv_sem, out_sem, in_sem):
    grp, ex, chip, head = (lax.axis_index(name) for name in EVERYONE)
    n_grp, n_ex, n_chip, n_head = (lax.axis_size(name) for name in EVERYONE)
    lead = PROMPT // QUARTERS
    count = lead + 1
    team = n_grp * n_ex
    everyone = team * n_chip * n_head
    owners = -(-count // share)
    mine = grp * n_ex + ex
    quarter = chip * n_head + head
    whole = mine * QUARTERS + quarter

    def device(index):
        member, part = index // QUARTERS, lax.rem(index, QUARTERS)
        return {
            "grp": member // n_ex,
            "ex": lax.rem(member, n_ex),
            "chip": part // n_head,
            "head": lax.rem(part, n_head),
        }

    barrier = pltpu.get_barrier_semaphore()

    def greet(step, carry):
        peer = device(lax.rem(whole + step, everyone))
        pl.semaphore_signal(barrier, inc=1, device_id=peer, device_id_type=MESH)
        return carry

    lax.fori_loop(1, everyone, greet, 0)
    pl.semaphore_wait(barrier, everyone - 1)

    def line(ref, at, size=share):
        return ref.at[pl.ds(at * size, size)]

    def give(step, carry):
        owner = lax.rem(mine + step, team)
        outside = (owner < owners) & (step > 0)

        @pl.when(outside)
        def _():
            pltpu.make_async_remote_copy(
                src_ref=line(block, owner),
                dst_ref=line(parts, mine),
                send_sem=send_sem,
                recv_sem=recv_sem,
                device_id={"grp": owner // n_ex, "ex": lax.rem(owner, n_ex)},
                device_id_type=MESH,
            ).start()

        @pl.when(jnp.logical_not(outside))
        def _():
            pltpu.make_async_copy(line(block, 0), line(unused, owner), send_sem).start()

        return carry

    lax.fori_loop(0, team, give, 0)
    owning = mine < owners

    @pl.when(owning)
    def _():
        pltpu.make_async_copy(line(block, mine), line(parts, mine), recv_sem).start()
        pltpu.make_async_copy(parts, parts, recv_sem).wait()
        if share == 1:
            total[0:1] = jnp.sum(parts[...], axis=0, keepdims=True)
        else:
            total[0:share] = jnp.sum(parts[...].reshape(team, share, parts.shape[1]), axis=0)
        for k in range(share):
            row = mine * share + k
            place = jnp.where(row < lead, quarter * lead + row, PROMPT + quarter)
            source = line(total, k, 1)

            def spread(step, carry):
                pltpu.make_async_remote_copy(
                    src_ref=source,
                    dst_ref=line(gathered, place, 1),
                    send_sem=out_sem,
                    recv_sem=in_sem,
                    device_id=device(lax.rem(whole + step, everyone)),
                    device_id_type=MESH,
                ).start()
                return carry

            lax.fori_loop(1, everyone, spread, 0)
            pltpu.make_async_copy(source, line(gathered, place, 1), in_sem).start()
            pltpu.make_async_copy(source, line(unused, team * share + k, 1), out_sem).start()

    def wait_rows(count, sem):
        span = gathered.at[pl.ds(0, count)]
        pltpu.make_async_copy(span, span, sem).wait()

    wait_rows(QUARTERS * owners * share, in_sem)
    wait_rows(team * share, send_sem)

    @pl.when(owning)
    def _():
        wait_rows(everyone * share, out_sem)

    out[...] = gathered[0 : out.shape[0]]


def sum_call(block):
    team = lax.axis_size(("grp", "ex"))
    count = PROMPT // QUARTERS + 1
    share = -(-count // team)
    width = block.shape[1]
    rows = PROMPT + QUARTERS
    return pl.pallas_call(
        functools.partial(sum_kernel, share),
        out_shape=jax.ShapeDtypeStruct((rows, width), F32),
        in_specs=[pl.BlockSpec(memory_space=pltpu.VMEM)],
        out_specs=pl.BlockSpec(memory_space=pltpu.VMEM),
        scratch_shapes=[
            pltpu.VMEM((team * share, width), F32),
            pltpu.VMEM((team * share + max(8, share), width), F32),
            pltpu.VMEM((max(8, share), width), F32),
            pltpu.VMEM((max(rows, lax.axis_size(EVERYONE) * share), width), F32),
            pltpu.SemaphoreType.DMA,
            pltpu.SemaphoreType.DMA,
            pltpu.SemaphoreType.DMA,
            pltpu.SemaphoreType.DMA,
        ],
        compiler_params=pltpu.CompilerParams(collective_id=3, has_side_effects=True),
        name="sum_of_prompt_gradients",
    )(block)


def lamb_kernel(summed, first_old, second_old, prompt, loss, grad_norm, norms, first_new, second_new, prompt_new):
    grad = summed[0:PROMPT]
    loss[0] = jnp.sum(summed[PROMPT : PROMPT + QUARTERS, 0:1])
    norm = jnp.sqrt(jnp.sum(grad * grad))
    grad_norm[0] = norm
    clipped = grad * (clip_bound / jnp.maximum(norm, clip_bound))
    first_next = beta_first * first_old[...] + (1.0 - beta_first) * clipped
    second_next = beta_second * second_old[...] + (1.0 - beta_second) * clipped * clipped
    first_new[...] = first_next
    second_new[...] = second_next
    scaled_first = first_next / (1.0 - beta_first**STEP)
    scaled_second = second_next / (1.0 - beta_second**STEP)
    param = prompt[...]
    update = scaled_first / (jnp.sqrt(scaled_second) + adam_eps) + decay_rate * param
    param_norm = jnp.sqrt(jnp.sum(param * param))
    update_norm = jnp.sqrt(jnp.sum(update * update))
    norms[0] = param_norm
    norms[1] = update_norm
    prompt_new[...] = param - learn_rate * (param_norm / update_norm) * update


def lamb_call(summed, first_old, second_old, prompt):
    smem, vmem = pl.BlockSpec(memory_space=pltpu.SMEM), pl.BlockSpec(memory_space=pltpu.VMEM)
    like = jax.ShapeDtypeStruct(prompt.shape, F32)
    return pl.pallas_call(
        lamb_kernel,
        out_shape=(
            jax.ShapeDtypeStruct((1,), F32),
            jax.ShapeDtypeStruct((1,), F32),
            jax.ShapeDtypeStruct((2,), F32),
            like,
            like,
            like,
        ),
        in_specs=[vmem] * 4,
        out_specs=(smem, smem, smem, vmem, vmem, vmem),
        name="lamb",
    )(summed, first_old, second_old, prompt)


def shards(
    enc_ids,
    lengths,
    dec_ids,
    target_ids,
    loss_mask,
    embedding,
    prompt,
    first_moment,
    second_moment,
    gains,
    enc_qkv,
    enc_wo,
    enc_w1,
    enc_w2,
    dec_qkv,
    dec_wo,
    cross_q,
    cross_kv,
    cross_wo,
    dec_w1,
    dec_w2,
):
    width = embedding.shape[1]
    own = dec_wo.shape[0]
    enc_dev, tgt_dev = enc_ids.shape[1], dec_ids.shape[1]
    total_len = enc_dev * lax.axis_size(SEQ)
    lead = PROMPT // QUARTERS
    tokens = (total_len - PROMPT) // QUARTERS
    rows = total_len // QUARTERS
    ids = ids_call(enc_ids, dec_ids, target_ids)
    picked = lookup_call(ids, embedding, rows, tokens, lead, enc_dev, tgt_dev)
    block = main_call(
        lengths,
        (prompt, loss_mask, gains),
        (
            picked,
            enc_qkv,
            enc_wo,
            enc_w1,
            enc_w2,
            dec_qkv.reshape(width, 3 * own),
            dec_wo,
            cross_q,
            cross_kv.reshape(width, 2 * own),
            cross_wo,
            dec_w1,
            dec_w2,
            embedding,
        ),
    )
    summed = sum_call(block)
    loss, grad_norm, norms, first_new, second_new, prompt_new = lamb_call(summed, first_moment, second_moment, prompt)
    return loss.reshape(()), grad_norm.reshape(()), norms, first_new, second_new, prompt_new


def solution(mesh):
    finer = Mesh(
        mesh.devices.reshape(mesh.shape["grp"], mesh.shape["seq"] // 2, 2, mesh.shape["head"]),
        ("grp", "ex", "chip", "head"),
    )
    placed = (
        P("grp", SEQ),
        P("grp"),
        P("grp", SEQ),
        P("grp", SEQ),
        P("grp", None),
        P("head", None),
        P(),
        P(),
        P(),
        P(),
        P(),
        P(),
        P(),
        P(),
        P(None, None, "head"),
        P("head", None),
        P(None, "head"),
        P(None, None, "head"),
        P("head", None),
        P(None, "head"),
        P("head", None),
    )
    return jax.shard_map(
        shards,
        mesh=finer,
        in_specs=placed,
        out_specs=(P(), P(), P(), P(), P(), P()),
        check_vma=False,
    )
```

```python
import functools

import jax
import jax.numpy as jnp
from jax import lax
from jax.experimental import pallas as pl
from jax.experimental.pallas import tpu as pltpu
from jax.sharding import Mesh
from jax.sharding import PartitionSpec as P

HD = 64
PROMPT = 100
STEP = 5
QUARTERS = 4
SEQ = ("ex", "chip")
CLUSTER = ("chip", "head")
EVERYONE = ("grp", "ex", "chip", "head")
NEG = -1000000000.0

norm_eps = 1e-06
beta_first = 0.5
beta_second = 0.5
adam_eps = 1e-12
decay_rate = 0.01
learn_rate = 0.3
clip_bound = 0.0001


MESH = pl.DeviceIdType.MESH
BF = jnp.bfloat16
F32 = jnp.float32
LEAD_PAD = 32
CHUNK = 1024
RING = 4
LANES = 128


def dot_nn(left, right):
    return lax.dot_general(left, right, (((1,), (0,)), ((), ())), preferred_element_type=F32)


def dot_nt(left, right):
    return lax.dot_general(left, right, (((1,), (1,)), ((), ())), preferred_element_type=F32)


def dot_tn(left, right):
    return lax.dot_general(left, right, (((0,), (0,)), ((), ())), preferred_element_type=F32)


def rms(value, gain):
    return value * lax.rsqrt(jnp.mean(value * value, axis=-1, keepdims=True) + norm_eps) * gain


def rms_grad(value, gain, grad):
    scale = lax.rsqrt(jnp.mean(value * value, axis=-1, keepdims=True) + norm_eps)
    scaled = grad * gain
    inner = jnp.mean(scaled * value, axis=-1, keepdims=True)
    return scale * scaled - value * (scale * scale * scale * inner)


GELU_A = 0.7978845608028654
GELU_B = 0.044715


def gelu(value):
    return 0.5 * value * (1.0 + jnp.tanh(GELU_A * (value + GELU_B * (value * value * value))))


def gelu_grad(value, grad):
    square = value * value
    bend = jnp.tanh(GELU_A * (value + GELU_B * (square * value)))
    slope = 0.5 * (1.0 + bend) + 0.5 * value * (1.0 - bend * bend) * (GELU_A * (1.0 + 3.0 * GELU_B * square))
    return grad * slope


def tiles(count, size, body):
    for index in range(count):
        body(pl.ds(index * size, size))


def main_kernel(
    lengths, picked, prompt, loss_mask, gains,
    enc_qkv, enc_wo, enc_w1, enc_w2, dec_qkv, dec_wo, cross_q, cross_kv, cross_wo, dec_w1, dec_w2, embedding,
    out,
    w_qkv, w_o, w_1, w_2, w_dqkv, w_do, w_cq, w_ckv, w_co, w_d1, w_d2, ring,
    lead, enc_my, enc_in, dec_my, dec_in,
    x0, h1, h2, go, spare, n1, q_s, kv, o_f, o_b, s_f, p_b, lse_e, sum_e, nb, u, act,
    eo, ckv, dckv, gp_s, gp_r, gown, d_o, dkv, dkv_r, gj, dl,
    y0, a1, m_b, sqkv, so, dx_s, dx_r, cq, cp, cp_b, st_p, st_r, co_r, co, co_b,
    lg, px_s, px_r, a2, a3, du, dact, f_b, tgt, acc, acc_b, acc_r, vl_s, vl_r, gffn, gco, st_g,
    blk, s1_r, s2_r, all_r,
    load_sem, ring_sem, send_sem, recv_sem,
):
    width = x0.shape[1]
    rows = x0.shape[0]
    half = f_b.shape[0]
    own = co.shape[1]
    pairs_e, pairs_d = width // LANES, own // LANES
    head, chip = lax.axis_index("head"), lax.axis_index("chip")
    mate, across = 1 - head, 1 - chip
    me, slot_mate = 2 * chip + head, 2 * chip + mate
    slot_across, slot_diag = 2 * across + head, 2 * across + mate
    to_mate, to_across = {"head": mate}, {"chip": across}
    to_diag = {"chip": across, "head": mate}

    grp, ex = lax.axis_index("grp"), lax.axis_index("ex")
    n_grp, n_ex = lax.axis_size("grp"), lax.axis_size("ex")

    def ex_peer(step):
        return {"ex": lax.rem(ex + step, n_ex)}

    def plane_peer(step):
        place = lax.rem(grp * QUARTERS + me + step, n_grp * QUARTERS)
        member = lax.div(place, QUARTERS)
        side = lax.div(place - member * QUARTERS, 2)
        return {"grp": member, "chip": side, "head": place - member * QUARTERS - 2 * side}

    barrier = pltpu.get_barrier_semaphore()
    friends = [plane_peer(step) for step in range(1, n_grp * QUARTERS)] + [ex_peer(step) for step in range(1, n_ex)]
    for peer in friends:
        pl.semaphore_signal(barrier, inc=1, device_id=peer, device_id_type=MESH)

    def load(index, source, target):
        copy = pltpu.make_async_copy(source, target, load_sem.at[index])
        copy.start()
        return copy

    my_rows = pl.ds(pl.multiple_of(head * rows, rows), rows)
    mate_rows = pl.ds(pl.multiple_of(mate * rows, rows), rows)
    dec_rows = pl.ds(2 * rows, dec_my.shape[0])
    load_x = load(0, picked.at[my_rows], enc_my)
    load_y = load(1, picked.at[dec_rows], dec_my)
    load_qkv = load(2, enc_qkv, w_qkv)
    load_dqkv = load(3, dec_qkv, w_dqkv)
    load_do = load(4, dec_wo, w_do)
    load_cq = load(5, cross_q, w_cq)
    load_o = load(6, enc_wo, w_o)
    load_1 = load(7, enc_w1, w_1)
    load_2 = load(8, enc_w2, w_2)
    load_ckv = load(9, cross_kv, w_ckv)
    load_co = load(10, cross_wo, w_co)
    load_d1 = load(11, dec_w1, w_d1)
    load_d2 = load(12, dec_w2, w_d2)
    leads = PROMPT // QUARTERS

    vocab = embedding.shape[0]
    full = vocab // CHUNK
    tail = vocab - full * CHUNK

    def chunk_copy(index, slot):
        at = pl.ds(pl.multiple_of(index * CHUNK, CHUNK), CHUNK)
        return pltpu.make_async_copy(embedding.at[at], ring.at[slot], ring_sem.at[slot])

    def tail_copy():
        slot = full % RING
        return pltpu.make_async_copy(
            embedding.at[pl.ds(full * CHUNK, tail)], ring.at[slot, pl.ds(0, tail)], ring_sem.at[slot]
        )

    for index in range(RING):
        chunk_copy(index, index).start()

    pl.semaphore_wait(barrier, len(friends))
    sends = []

    def send(index, source, target, peer):
        copy = pltpu.make_async_remote_copy(
            src_ref=source,
            dst_ref=target,
            send_sem=send_sem.at[index],
            recv_sem=recv_sem.at[index],
            device_id=peer,
            device_id_type=MESH,
        )
        copy.start()
        sends.append(copy)
        return copy

    got_x = send(0, picked.at[mate_rows], enc_in, to_mate)
    got_y = send(1, picked.at[dec_rows], dec_in, to_mate)

    lane = lax.broadcasted_iota(jnp.int32, (1, LANES), 1)
    low_lane = lane < HD
    low_b = jnp.where(low_lane, 1.0, 0.0).astype(BF)
    high_b = jnp.where(low_lane, 0.0, 1.0).astype(BF)
    sides = (low_b, high_b)
    gain = [gains[k : k + 1, :] for k in range(7)]
    gain[6] = gain[6] * width ** (-0.5)
    length = lengths[ex]
    tokens = kv.shape[1] - leads

    def allowed(slots, span, first):
        at = lax.broadcasted_iota(jnp.int32, (1, slots * span), 1)
        slot = at // span
        inner = at - slot * span
        return (inner < leads) | (tokens * (slot + first) + inner - leads < length)

    ok = allowed(4, rows, 0)
    okc = allowed(2, rows, 2 * chip)
    okl = allowed(4, LEAD_PAD, 0)
    mask_row = loss_mask[pl.ds(ex, 1), :].astype(F32)
    lane_at = lax.broadcasted_iota(jnp.int32, (half, mask_row.shape[1]), 1)
    row_of = lax.broadcasted_iota(jnp.int32, (half, mask_row.shape[1]), 0)
    own_mask = jnp.where(lane_at == row_of + chip * half, jnp.broadcast_to(mask_row, lane_at.shape), 0.0)
    share = jnp.sum(own_mask, axis=-1, keepdims=True) / jnp.sum(mask_row, axis=-1, keepdims=True)

    load_x.wait()
    got_x.wait_recv()
    for block in range(rows // 64):
        part = pl.ds(block * 64, 64)
        value = enc_my[part].astype(F32) + enc_in[part].astype(F32)
        if block == 0:
            spot = lax.broadcasted_iota(jnp.int32, (64, width), 0)
            for slot in range(QUARTERS):
                lead[0:leads] = jnp.where(me == slot, prompt[slot * leads : (slot + 1) * leads], lead[0:leads])
            value = jnp.where(spot < leads, lead[...], value)
        x0[part] = value
        n1[me, part] = rms(value, gain[0]).astype(BF)
    got_n = send(2, n1.at[me], n1.at[me], to_across)
    got_m = send(3, n1.at[me], n1.at[me], to_mate)

    load_qkv.wait()

    def key_value(slot):
        def body(at):
            cols = pl.ds(width + at.start, at.size)
            kv[slot, :, at] = dot_nn(n1[slot], w_qkv[:, cols]).astype(BF)

        tiles(2 * width // 256, 256, body)

    def query(at):
        q_s[:, at] = (dot_nn(n1[me], w_qkv[:, at]).astype(BF) * HD ** (-0.5)).astype(BF)

    key_value(me)
    tiles(width // 256, 256, query)
    got_m.wait_recv()
    key_value(slot_mate)

    load_y.wait()
    got_y.wait_recv()
    all_tgt = y0.shape[0]
    value = dec_my[0:all_tgt].astype(F32) + dec_in[0:all_tgt].astype(F32)
    y0[...] = value
    m_b[...] = rms(value, gain[3]).astype(BF)
    tgt[...] = dec_my[all_tgt : all_tgt + half].astype(F32) + dec_in[all_tgt : all_tgt + half].astype(F32)
    load_dqkv.wait()

    for part in range(3):
        sqkv[:, part * own : (part + 1) * own] = dot_nn(m_b[...], w_dqkv[part]).astype(BF)
    row_at = lax.broadcasted_iota(jnp.int32, (all_tgt, all_tgt), 0)
    col_at = lax.broadcasted_iota(jnp.int32, (all_tgt, all_tgt), 1)
    for pair in range(pairs_d):
        lo = pair * LANES
        q2 = sqkv[:, lo : lo + LANES]
        k2 = sqkv[:, own + lo : own + lo + LANES]
        v2 = sqkv[:, 2 * own + lo : 2 * own + lo + LANES]
        outs = []
        for side in sides:
            scores = dot_nt(q2 * side, k2) * HD ** (-0.5)
            scores = jnp.where(col_at <= row_at, scores, NEG)
            top = jnp.max(scores, axis=-1, keepdims=True)
            probs = jnp.exp(scores - top)
            total = jnp.sum(probs, axis=-1, keepdims=True)
            outs.append(dot_nn(probs.astype(BF), v2) / total)
        so[:, lo : lo + LANES] = jnp.where(low_lane, outs[0], outs[1]).astype(BF)
    load_do.wait()

    def self_out(at):
        dx_s[:, at] = dot_nn(so[...], w_do[:, at]).astype(BF)

    tiles(width // 256, 256, self_out)
    got_d = send(4, dx_s, dx_r, to_mate)

    got_n.wait_recv()
    got_f = send(5, n1.at[slot_across], n1.at[slot_across], to_mate)
    key_value(slot_across)

    got_d.wait_recv()
    value = y0[...] + (dx_s[...].astype(F32) + dx_r[...].astype(F32))
    a1[...] = value
    m_b[...] = rms(value, gain[4]).astype(BF)
    load_cq.wait()
    cq[...] = (dot_nn(m_b[...], w_cq[...]).astype(BF) * HD ** (-0.5)).astype(BF)

    got_f.wait_recv()
    key_value(slot_diag)

    keys = 4 * rows

    def pair_lanes(at, base):
        return pl.ds(base + at * LANES, LANES)

    def attend_pair(pair):
        at = pair_lanes(pair, 0)
        q2 = q_s[:, at]
        k2 = kv[:, :, at].reshape(keys, LANES)
        v2 = kv[:, :, pair_lanes(pair, width)].reshape(keys, LANES)
        outs = []
        for index, side in enumerate(sides):
            s_f[index] = dot_nt(q2 * side, k2)
            for block in range(rows // 32):
                part = pl.ds(block * 32, 32)
                scores = jnp.where(ok, s_f[index, part], NEG)
                top = jnp.max(scores, axis=-1, keepdims=True)
                probs = jnp.exp(scores - top)
                total = jnp.sum(probs, axis=-1, keepdims=True)
                p_b[index, part] = probs.astype(BF)
                sum_e[index, part] = jnp.broadcast_to(total, (32, LANES))
                lse = jnp.broadcast_to(top + jnp.log(total), (32, LANES))
                if index == 0:
                    lse_e[pair, part] = lse
                else:
                    lse_e[pair, part] = jnp.where(low_lane, lse_e[pair, part], lse)
            outs.append(dot_nn(p_b[index], v2) / sum_e[index])
        both = jnp.where(low_lane, outs[0], outs[1])
        o_f[:, at] = both
        o_b[:, at] = both.astype(BF)

    for pair in range(pairs_e):
        attend_pair(pair)
    load_o.wait()

    def out_cols(at):
        h1[:, at] = x0[:, at] + dot_nn(o_b[...], w_o[:, at])

    tiles(width // 256, 256, out_cols)

    def norm_two(at):
        nb[at] = rms(h1[at], gain[1]).astype(BF)

    tiles(rows // 64, 64, norm_two)
    load_1.wait()

    def hidden(at):
        value = dot_nn(nb[...], w_1[:, at])
        u[:, at] = value
        act[:, at] = gelu(value).astype(BF)

    tiles(u.shape[1] // 256, 256, hidden)
    load_2.wait()

    def hidden_out(at):
        h2[:, at] = h1[:, at] + dot_nn(act[...], w_2[:, at])

    tiles(width // 256, 256, hidden_out)

    def norm_out(at):
        eo[head, at] = rms(h2[at], gain[2]).astype(BF)

    tiles(rows // 64, 64, norm_out)
    got_e = send(6, eo.at[head], eo.at[head], to_mate)
    load_ckv.wait()

    def cross_keys(slot):
        def body(at):
            ckv[slot, :, at] = dot_nn(eo[slot], w_ckv[:, at]).astype(BF)

        tiles(2 * own // 256, 256, body)

    cross_keys(head)
    got_e.wait_recv()
    cross_keys(mate)


    def cross_pair(pair):
        lo = pair * LANES
        k2 = ckv[:, :, lo : lo + LANES].reshape(2 * rows, LANES)
        v2 = ckv[:, :, own + lo : own + lo + LANES].reshape(2 * rows, LANES)
        return lo, cq[:, lo : lo + LANES], k2, v2

    stats = jnp.zeros((all_tgt, LANES), F32)
    for pair in range(pairs_d):
        lo, q2, k2, v2 = cross_pair(pair)
        outs = []
        for index, side in enumerate(sides):
            scores = jnp.where(okc, dot_nt(q2 * side, k2), NEG)
            top = jnp.max(scores, axis=-1, keepdims=True)
            probs = jnp.exp(scores - top)
            total = jnp.sum(probs, axis=-1, keepdims=True)
            outs.append(dot_nn(probs.astype(BF), v2) / total)
            stats = jnp.where(lane == 2 * pair + index, top + jnp.log(total), stats)
        both = jnp.where(low_lane, outs[0], outs[1])
        cp[:, lo : lo + LANES] = both
        cp_b[:, lo : lo + LANES] = both.astype(BF)
    st_p[...] = stats
    mine_t = pl.ds(pl.multiple_of(chip * half, half), half)
    theirs_t = pl.ds(pl.multiple_of(across * half, half), half)
    got_c = send(7, cp_b.at[theirs_t], co_r, to_across)
    got_s = send(8, st_p.at[theirs_t], st_r, to_across)
    got_c.wait_recv()
    got_s.wait_recv()
    l_own, l_oth = st_p[mine_t], st_r[...]
    top = jnp.maximum(l_own, l_oth)
    lse_c = top + jnp.log(jnp.exp(l_own - top) + jnp.exp(l_oth - top))
    w_own, w_oth = jnp.exp(l_own - lse_c), jnp.exp(l_oth - lse_c)

    def side_cols(array, pair):
        return jnp.where(
            low_lane, array[:, 2 * pair : 2 * pair + 1], array[:, 2 * pair + 1 : 2 * pair + 2]
        )

    for pair in range(pairs_d):
        lo = pair * LANES
        both = cp[mine_t, lo : lo + LANES] * side_cols(w_own, pair)
        both = both + co_r[:, lo : lo + LANES].astype(F32) * side_cols(w_oth, pair)
        co[:, lo : lo + LANES] = both
        co_b[:, lo : lo + LANES] = both.astype(BF)

    def exchange(index, value):
        slot = index - 9
        px_s[slot] = value.astype(BF)
        got = send(index, px_s.at[slot], px_r.at[slot], to_mate)
        got.wait_recv()
        return px_s[slot].astype(F32) + px_r[slot].astype(F32)

    load_co.wait()
    a2[...] = a1[mine_t] + exchange(9, dot_nn(co_b[...], w_co[...]))
    m_b[0:half] = rms(a2[...], gain[5]).astype(BF)
    load_d1.wait()

    def dec_hidden(at):
        value = dot_nn(m_b[0:half], w_d1[:, at])
        du[:, at] = value
        dact[:, at] = gelu(value).astype(BF)

    tiles(du.shape[1] // 512, 512, dec_hidden)
    load_d2.wait()
    a3[...] = a2[...] + exchange(10, dot_nn(dact[...], w_d2[...]))
    f_b[...] = rms(a3[...], gain[6]).astype(BF)

    acc[...] = jnp.zeros_like(acc)

    def vocab_step(logits, table, top, total):
        new_top = jnp.maximum(top, jnp.max(logits, axis=-1, keepdims=True))
        fade = jnp.exp(top - new_top)
        probs = jnp.exp(logits - new_top)
        acc[...] = acc[...] * fade + dot_nn(probs.astype(BF), table)
        return new_top, total * fade + jnp.sum(probs, axis=-1, keepdims=True)

    carry = (jnp.full((half, 1), NEG, F32), jnp.zeros((half, 1), F32))
    chunk_copy(0, 0).wait()
    lg[0] = dot_nt(f_b[...], ring[0])
    for index in range(full):
        slot, after = index % RING, (index + 1) % RING
        if index + 1 < full:
            chunk_copy(index + 1, after).wait()
            lg[(index + 1) % 2] = dot_nt(f_b[...], ring[after])
        elif tail:
            tail_copy().wait()
            lg[(index + 1) % 2, :, 0:tail] = dot_nt(f_b[...], ring[after, 0:tail])
        carry = vocab_step(lg[index % 2], ring[slot], *carry)
        if index + RING < full:
            chunk_copy(index + RING, slot).start()
        elif index + RING == full and tail:
            tail_copy().start()
    if tail:
        carry = vocab_step(lg[full % 2, :, 0:tail], ring[full % RING, 0:tail], *carry)
    top, total = carry
    acc_b[...] = (acc[...] / total).astype(BF)
    vl_s[...] = jnp.broadcast_to(top + jnp.log(total), vl_s.shape)
    got_a = send(11, acc_b, acc_r, to_mate)
    got_v = send(12, vl_s, vl_r, to_mate)
    pick = jnp.sum(f_b[...].astype(F32) * tgt[...], axis=-1, keepdims=True)
    got_a.wait_recv()
    got_v.wait_recv()
    l_own, l_oth = vl_s[:, 0:1], vl_r[:, 0:1]
    top = jnp.maximum(l_own, l_oth)
    lse_v = top + jnp.log(jnp.exp(l_own - top) + jnp.exp(l_oth - top))
    loss = jnp.sum(share * (lse_v - pick), axis=0, keepdims=True) * jnp.where(head == 0, 1.0, 0.0)
    mean_row = acc_b[...].astype(F32) * jnp.exp(l_own - lse_v) + acc_r[...].astype(F32) * jnp.exp(l_oth - lse_v)
    gffn[...] = rms_grad(a3[...], gain[6], share * (mean_row - tgt[...]))

    m_b[0:half] = gffn[...].astype(BF)

    def dec_hidden_grad(at):
        value = dot_nt(m_b[0:half], w_d2[at])
        dact[:, at] = gelu_grad(du[:, at], value).astype(BF)

    tiles(du.shape[1] // 512, 512, dec_hidden_grad)
    slope = exchange(13, dot_nt(dact[...], w_d1[...]))
    gcross = gffn[...] + rms_grad(a2[...], gain[5], slope)
    gco[chip] = dot_nt(gcross.astype(BF), w_co[...]).astype(BF)
    stats = lse_c
    for pair in range(pairs_d):
        lo = pair * LANES
        value = gco[chip, :, lo : lo + LANES].astype(F32) * co[:, lo : lo + LANES]
        for index in range(2):
            picked_side = jnp.where(low_lane == (index == 0), value, 0.0)
            delta = jnp.sum(picked_side, axis=-1, keepdims=True)
            stats = jnp.where(lane == HD + 2 * pair + index, delta, stats)
    st_g[chip] = stats
    got_g = send(14, gco.at[chip], gco.at[chip], to_across)
    got_t = send(15, st_g.at[chip], st_g.at[chip], to_across)
    got_g.wait_recv()
    got_t.wait_recv()

    stats = st_g[...].reshape(all_tgt, LANES)
    for pair in range(pairs_d):
        lo, q2, k2, v2 = cross_pair(pair)
        do2 = gco[:, :, lo : lo + LANES].reshape(all_tgt, LANES)
        dks, dvs = [], []
        for index, side in enumerate(sides):
            column = 2 * pair + index
            scores = jnp.where(okc, dot_nt(q2 * side, k2), NEG)
            probs = jnp.exp(scores - stats[:, column : column + 1])
            dp = dot_nt(do2 * side, v2)
            ds = (probs * (dp - stats[:, HD + column : HD + column + 1])).astype(BF)
            dks.append(dot_tn(ds, q2))
            dvs.append(dot_tn(probs.astype(BF), do2))
        dckv[:, :, lo : lo + LANES] = jnp.where(low_lane, *dks).astype(BF).reshape(2, rows, LANES)
        dckv[:, :, own + lo : own + lo + LANES] = jnp.where(low_lane, *dvs).astype(BF).reshape(2, rows, LANES)

    def pair_grad_mate(at):
        gp_s[:, at] = dot_nt(dckv[mate], w_ckv[at]).astype(BF)

    tiles(width // 256, 256, pair_grad_mate)
    got_p = send(16, gp_s, gp_r, to_mate)

    def pair_grad_mine(at):
        gown[:, at] = dot_nt(dckv[head], w_ckv[at])

    tiles(width // 256, 256, pair_grad_mine)
    got_p.wait_recv()

    def out_grad(at):
        value = rms_grad(h2[at], gain[2], gown[at].astype(BF).astype(F32) + gp_r[at].astype(F32))
        go[at] = value
        nb[at] = value.astype(BF)

    tiles(rows // 64, 64, out_grad)

    def hidden_grad(at):
        act[:, at] = gelu_grad(u[:, at], dot_nt(nb[...], w_2[at])).astype(BF)

    tiles(u.shape[1] // 256, 256, hidden_grad)

    def norm_two_grad(at):
        spare[:, at] = dot_nt(act[...], w_1[at])

    tiles(width // 256, 256, norm_two_grad)

    def one_grad(at):
        value = go[at] + rms_grad(h1[at], gain[1], spare[at])
        go[at] = value
        nb[at] = value.astype(BF)

    tiles(rows // 64, 64, one_grad)

    def attn_grad(at):
        d_o[:, at] = dot_nt(nb[...], w_o[at]).astype(BF)

    tiles(width // 256, 256, attn_grad)

    lead_keys = 4 * LEAD_PAD

    quad = 2 * LANES
    heads_in = quad // HD
    quad_lane = lax.broadcasted_iota(jnp.int32, (1, quad), 1)
    quad_of = [(quad_lane >= k * HD) & (quad_lane < (k + 1) * HD) for k in range(heads_in)]
    quad_b = [jnp.where(inside, 1.0, 0.0).astype(BF) for inside in quad_of]

    def lead_pair(pair):
        at = pair_lanes(pair, 0)
        q2, do2 = q_s[:, at], d_o[:, at]
        k2 = kv[:, 0:LEAD_PAD, at].reshape(lead_keys, LANES)
        v2 = kv[:, 0:LEAD_PAD, pair_lanes(pair, width)].reshape(lead_keys, LANES)
        value = do2.astype(F32) * o_f[:, at]
        dks, dvs, deltas = [], [], []
        for index, side in enumerate(sides):
            delta = jnp.sum(jnp.where(low_lane == (index == 0), value, 0.0), axis=-1, keepdims=True)
            deltas.append(delta)
            lse = lse_e[pair, :, index * HD : index * HD + 1]
            scores = jnp.where(okl, dot_nt(q2 * side, k2), NEG)
            probs = jnp.exp(scores - lse)
            ds = (probs * (dot_nt(do2 * side, v2) - delta)).astype(BF)
            dks.append(dot_tn(ds, q2))
            dvs.append(dot_tn(probs.astype(BF), do2))
        lo = (pair % 2) * LANES
        shape = (4, LEAD_PAD, LANES)
        dkv[pair // 2, :, :, lo : lo + LANES] = jnp.where(low_lane, *dks).astype(BF).reshape(shape)
        dkv[pair // 2, :, :, quad + lo : quad + lo + LANES] = jnp.where(low_lane, *dvs).astype(BF).reshape(shape)
        dl[pair] = jnp.where(low_lane, *[d[0:LEAD_PAD] for d in deltas])

    def stack(value):
        return jnp.concatenate([value * side for side in quad_b], axis=0)

    def column(ref, group, rows_at):
        return jnp.concatenate(
            [ref[2 * group + k // 2, rows_at, (k % 2) * HD : (k % 2) * HD + 1] for k in range(heads_in)], axis=0
        )

    def query_quad(group):
        at = slice(group * quad, (group + 1) * quad)
        vat = slice(width + group * quad, width + (group + 1) * quad)
        lead_rows = slice(0, LEAD_PAD)
        k4 = kv[:, :, at].reshape(keys, quad)
        v4 = kv[:, :, vat].reshape(keys, quad)
        scores = jnp.where(ok, dot_nt(stack(q_s[lead_rows, at]), k4), NEG)
        probs = jnp.exp(scores - column(lse_e, group, lead_rows))
        ds = (probs * (dot_nt(stack(d_o[lead_rows, at]), v4) - column(dl, group, lead_rows))).astype(BF)
        wide = dot_nn(ds, k4)
        value = jnp.zeros((LEAD_PAD, quad), F32)
        for k in range(heads_in):
            value = jnp.where(quad_of[k], wide[k * LEAD_PAD : (k + 1) * LEAD_PAD], value)
        gj[:, at] = (value * HD ** (-0.5)).astype(BF)

    got_k = []
    for group in range(width // quad):
        lead_pair(2 * group)
        lead_pair(2 * group + 1)
        first = 17 + 3 * group
        got_k += [
            send(first, dkv.at[group, slot_across], dkv_r.at[group, 1], to_across),
            send(first + 1, dkv.at[group, slot_diag], dkv_r.at[group, 2], to_diag),
            send(first + 2, dkv.at[group, slot_mate], dkv_r.at[group, 0], to_mate),
        ]
        query_quad(group)
    for group in range(width // quad):
        summed = dkv[group, me].astype(F32)
        for index in range(3):
            got_k[3 * group + (2, 0, 1)[index]].wait_recv()
            summed = summed + dkv_r[group, index].astype(F32)
        lo = group * quad
        gj[:, width + lo : width + lo + quad] = summed[:, :quad].astype(BF)
        gj[:, 2 * width + lo : 2 * width + lo + quad] = summed[:, quad:].astype(BF)

    def start_grad(at):
        spare[0:LEAD_PAD, at] = dot_nt(gj[...], w_qkv[at])

    tiles(width // 256, 256, start_grad)
    top_rows = slice(0, LEAD_PAD)
    value = go[top_rows] + rms_grad(x0[top_rows], gain[0], spare[top_rows])
    spot = lax.broadcasted_iota(jnp.int32, (LEAD_PAD, width), 0)
    extra = jnp.where(spot == leads, loss, 0.0)
    blk[...] = jnp.where(spot < leads, value, extra)

    piece = LEAD_PAD // n_grp

    def piece_of(member):
        return pl.ds(pl.multiple_of(member * piece, piece), piece)

    slot = 17 + 3 * (width // quad)
    got = []
    for step in range(1, n_grp):
        other = lax.rem(grp + step, n_grp)
        got.append(send(slot, blk.at[piece_of(other)], s1_r.at[step], {"grp": other}))
        slot += 1
    value = blk[piece_of(grp)]
    for step in range(1, n_grp):
        got[step - 1].wait_recv()
        value = value + s1_r[step]
    s2_r[ex] = value
    got = []
    for step in range(1, n_ex):
        got.append(send(slot, s2_r.at[ex], s2_r.at[ex], ex_peer(step)))
        slot += 1
    for copy in got:
        copy.wait_recv()
    value = s2_r[0]
    for member in range(1, n_ex):
        value = value + s2_r[member]
    all_r[me, grp] = value
    got = []
    for step in range(1, n_grp * QUARTERS):
        got.append(send(slot, all_r.at[me, grp], all_r.at[me, grp], plane_peer(step)))
        slot += 1
    for copy in got:
        copy.wait_recv()
    out[...] = all_r[...].reshape(out.shape)
    for copy in sends:
        copy.wait_send()


def main_call(lengths, vmem, hbm):
    half = vmem[1].shape[1] // 2
    rows = (hbm[0].shape[0] - 3 * half) // 2
    wq, wo, w1, w2, dqkv, dwo, cqw, ckvw, cwo, dw1, dw2, emb = hbm[1:]
    width, own, ff, dff, tgt_all = wo.shape[0], dwo.shape[0], w1.shape[1], dw1.shape[1], 2 * half
    pairs_e = width // LANES

    def v(shape, kind=F32):
        return pltpu.VMEM(shape, kind)

    scratch = [v(w.shape, BF) for w in hbm[1:12]]
    scratch += [v((RING, CHUNK, width), BF)]
    scratch += [v((64, width))]
    scratch += [v((rows, width), BF), v((rows, width), BF), v((tgt_all + half, width), BF), v((tgt_all + half, width), BF)]
    scratch += [v((rows, width)) for _ in range(5)]
    scratch += [v((4, rows, width), BF), v((rows, width), BF), v((4, rows, 2 * width), BF)]
    scratch += [v((rows, width)), v((rows, width), BF), v((2, rows, 4 * rows)), v((2, rows, 4 * rows), BF)]
    scratch += [v((pairs_e, rows, LANES)), v((2, rows, LANES)), v((rows, width), BF)]
    scratch += [v((rows, ff)), v((rows, ff), BF)]
    scratch += [v((2, rows, width), BF), v((2, rows, 2 * own), BF), v((2, rows, 2 * own), BF)]
    scratch += [v((rows, width), BF), v((rows, width), BF), v((rows, width)), v((rows, width), BF)]
    groups = width // (2 * LANES)
    scratch += [v((groups, 4, LEAD_PAD, 4 * LANES), BF), v((groups, 3, LEAD_PAD, 4 * LANES), BF), v((LEAD_PAD, 3 * width), BF)]
    scratch += [v((pairs_e, LEAD_PAD, LANES))]
    scratch += [v((tgt_all, width)), v((tgt_all, width)), v((tgt_all, width), BF), v((tgt_all, 3 * own), BF)]
    scratch += [v((tgt_all, own), BF), v((tgt_all, width), BF), v((tgt_all, width), BF), v((tgt_all, own), BF)]
    scratch += [v((tgt_all, own)), v((tgt_all, own), BF), v((tgt_all, LANES)), v((half, LANES))]
    scratch += [v((half, own), BF), v((half, own)), v((half, own), BF)]
    scratch += [v((2, half, CHUNK))]
    scratch += [v((5, half, width), BF), v((5, half, width), BF)]
    scratch += [v((half, width)), v((half, width)), v((half, dff)), v((half, dff), BF), v((half, width), BF)]
    scratch += [v((half, width)), v((half, width)), v((half, width), BF), v((half, width), BF)]
    scratch += [v((half, LANES)), v((half, LANES)), v((half, width)), v((2, half, own), BF), v((2, half, LANES))]
    n_grp, n_ex = lax.axis_size("grp"), lax.axis_size("ex")
    piece = LEAD_PAD // n_grp
    scratch += [v((LEAD_PAD, width)), v((n_grp, piece, width)), v((n_ex, piece, width))]
    scratch += [v((QUARTERS, n_grp, piece, width))]
    exchanges = 17 + 3 * groups + (n_grp - 1) + (n_ex - 1) + (n_grp * QUARTERS - 1)
    scratch += [
        pltpu.SemaphoreType.DMA((13,)),
        pltpu.SemaphoreType.DMA((RING,)),
        pltpu.SemaphoreType.DMA((exchanges,)),
        pltpu.SemaphoreType.DMA((exchanges,)),
    ]
    any_spec, vmem_spec = pl.BlockSpec(memory_space=pl.ANY), pl.BlockSpec(memory_space=pltpu.VMEM)
    return pl.pallas_call(
        main_kernel,
        out_shape=jax.ShapeDtypeStruct((QUARTERS, LEAD_PAD, width), F32),
        in_specs=[pl.BlockSpec(memory_space=pltpu.SMEM), any_spec] + [vmem_spec] * len(vmem) + [any_spec] * len(hbm[1:]),
        out_specs=vmem_spec,
        scratch_shapes=scratch,
        compiler_params=pltpu.CompilerParams(
            collective_id=1, has_side_effects=True, vmem_limit_bytes=62 * 1024 * 1024
        ),
        name="step_of_one_example",
    )(lengths, hbm[0], *vmem, *hbm[1:])


def log2(size):
    return size.bit_length() - 1


def ids_kernel(enc_ids, dec_ids, target_ids, out, lines, got, unused, send_sem, recv_sem):
    ex, chip = lax.axis_index("ex"), lax.axis_index("chip")
    chips = lax.axis_size("chip")
    seqs = lax.axis_size(SEQ)
    me = ex * chips + chip
    enc_dev, tgt_dev = enc_ids.shape[1], dec_ids.shape[1]


    def peer_of(step):
        peer = lax.rem(me + step, seqs)
        row = lax.div(peer, chips)
        return row, {"ex": row, "chip": peer - row * chips}

    barrier = pltpu.get_barrier_semaphore()
    for step in range(1, seqs):
        pl.semaphore_signal(barrier, inc=1, device_id=peer_of(step)[1], device_id_type=MESH)
    lines[:, 0:enc_dev] = enc_ids[...]
    lines[:, enc_dev : enc_dev + tgt_dev] = dec_ids[...]
    lines[:, enc_dev + tgt_dev : enc_dev + 2 * tgt_dev] = target_ids[...]
    lines[:, enc_dev + 2 * tgt_dev :] = jnp.zeros((lines.shape[0], lines.shape[1] - enc_dev - 2 * tgt_dev), jnp.int32)
    pl.semaphore_wait(barrier, seqs - 1)

    for step in range(1, seqs):
        row, peer = peer_of(step)
        pltpu.make_async_remote_copy(
            src_ref=lines.at[pl.ds(row, 1)],
            dst_ref=got.at[pl.ds(me, 1)],
            send_sem=send_sem,
            recv_sem=recv_sem,
            device_id=peer,
            device_id_type=MESH,
        ).start()
    own_line = lines.at[pl.ds(ex, 1)]
    pltpu.make_async_copy(own_line, got.at[pl.ds(me, 1)], recv_sem).start()
    pltpu.make_async_copy(own_line, unused.at[pl.ds(0, 1)], send_sem).start()
    pltpu.make_async_copy(got, got, recv_sem).wait()
    pltpu.make_async_copy(got, got, send_sem).wait()
    out[...] = got[...]


def ids_call(enc_ids, dec_ids, target_ids):
    seqs = lax.axis_size(SEQ)
    lanes = -(-(enc_ids.shape[1] + 2 * dec_ids.shape[1]) // LANES) * LANES
    return pl.pallas_call(
        ids_kernel,
        out_shape=jax.ShapeDtypeStruct((seqs, lanes), jnp.int32),
        in_specs=[pl.BlockSpec(memory_space=pltpu.VMEM)] * 3,
        out_specs=pl.BlockSpec(memory_space=pltpu.VMEM),
        scratch_shapes=[
            pltpu.VMEM((enc_ids.shape[0], lanes), jnp.int32),
            pltpu.VMEM((seqs, lanes), jnp.int32),
            pltpu.VMEM((8, lanes), jnp.int32),
            pltpu.SemaphoreType.DMA,
            pltpu.SemaphoreType.DMA,
        ],
        compiler_params=pltpu.CompilerParams(collective_id=2, has_side_effects=True),
        name="ids_of_one_example",
    )(enc_ids, dec_ids, target_ids)


GROUP = 16


AHEAD = 8


def lookup_kernel(rows, tokens, lead, enc_dev, tgt_dev, ids, table, out, blocks, spots, sems):
    chip, head = lax.axis_index("chip"), lax.axis_index("head")
    vocab_part = table.shape[0]
    enc_count = 2 * rows
    tgt_all = tgt_dev * ids.shape[0]
    half = tgt_all // 2
    groups = out.shape[0] // GROUP
    first, second = enc_count // GROUP, (enc_count + tgt_all) // GROUP

    def fetch(group):
        enc = group < first
        slot = (group * GROUP) >> log2(rows)
        enc_base = (PROMPT - lead) + tokens * (2 * chip + slot) + ((group * GROUP) & (rows - 1))
        dec_base = (group - jnp.where(group < second, first, second)) * GROUP
        dec_base = dec_base + jnp.where(group < second, 0, chip * half)
        base = jnp.where(enc, enc_base, dec_base)
        shift = jnp.where(enc, log2(enc_dev), log2(tgt_dev))
        mask = jnp.where(enc, enc_dev - 1, tgt_dev - 1)
        lane = jnp.where(enc, 0, jnp.where(group < second, enc_dev, enc_dev + tgt_dev))
        for k in range(GROUP):
            token = ids[(base + k) >> shift, lane + ((base + k) & mask)]
            upper = jnp.where(token >= vocab_part, 1, 0)
            local = token - upper * vocab_part
            spots[group * GROUP + k] = k * GROUP + (local & (GROUP - 1)) + ((upper + head - 2 * upper * head) * 4096)
            at = pl.multiple_of((local >> log2(GROUP)) << log2(GROUP), GROUP)
            pltpu.make_async_copy(
                table.at[pl.ds(at, GROUP)], blocks.at[group * GROUP + k], sems.at[group]
            ).start()

    across = lax.broadcasted_iota(jnp.int32, (8, LANES), 1)
    down = lax.broadcasted_iota(jnp.int32, (8, LANES), 0)

    def select(group):
        at = pl.ds(pl.multiple_of(group * GROUP, GROUP), GROUP)
        pltpu.make_async_copy(blocks.at[at], blocks.at[at], sems.at[group]).wait()
        chosen = []
        for part in range(GROUP // 8):
            want = jnp.full((8, LANES), -1, jnp.int32)
            for k in range(8):
                want = jnp.where(down == k, spots[group * GROUP + part * 8 + k], want)
            hits = [jnp.where(across + base == want, 1.0, 0.0) for base in range(0, GROUP * GROUP, LANES)]
            chosen.append(jnp.concatenate(hits, axis=1))
        chosen = jnp.concatenate(chosen, axis=0).astype(BF)
        out[at] = dot_nn(chosen, blocks[at].reshape(GROUP * GROUP, out.shape[1])).astype(BF)

    def loop(start, stop, *steps):
        def body(group, carry):
            for step in steps:
                step(group)
            return carry

        lax.fori_loop(start, stop, body, 0)

    loop(0, AHEAD, fetch)
    loop(AHEAD, groups, fetch, lambda group: select(group - AHEAD))
    loop(groups - AHEAD, groups, select)


def lookup_call(ids, table, rows, tokens, lead, enc_dev, tgt_dev):
    count = 2 * rows + tgt_dev * ids.shape[0] * 3 // 2
    width = table.shape[1]
    return pl.pallas_call(
        functools.partial(lookup_kernel, rows, tokens, lead, enc_dev, tgt_dev),
        out_shape=jax.ShapeDtypeStruct((count, width), BF),
        in_specs=[pl.BlockSpec(memory_space=pltpu.SMEM), pl.BlockSpec(memory_space=pl.ANY)],
        out_specs=pl.BlockSpec(memory_space=pltpu.VMEM),
        scratch_shapes=[
            pltpu.VMEM((count, GROUP, width), BF),
            pltpu.SMEM((count,), jnp.int32),
            pltpu.SemaphoreType.DMA((count // GROUP,)),
        ],
        compiler_params=pltpu.CompilerParams(vmem_limit_bytes=32 * 1024 * 1024),
        name="embedding_rows",
    )(ids, table)


def lamb_kernel(summed, first_old, second_old, prompt, loss, grad_norm, norms, first_new, second_new, prompt_new, work):
    lead = PROMPT // QUARTERS
    for quarter in range(QUARTERS):
        work[quarter * lead : (quarter + 1) * lead] = summed[quarter, 0:lead]
    grad = work[...]
    total = summed[0, lead : lead + 1, 0:1]
    for quarter in range(1, QUARTERS):
        total = total + summed[quarter, lead : lead + 1, 0:1]
    loss[0] = jnp.sum(total)
    norm = jnp.sqrt(jnp.sum(grad * grad))
    grad_norm[0] = norm
    clipped = grad * (clip_bound / jnp.maximum(norm, clip_bound))
    first_next = beta_first * first_old[...] + (1.0 - beta_first) * clipped
    second_next = beta_second * second_old[...] + (1.0 - beta_second) * clipped * clipped
    first_new[...] = first_next
    second_new[...] = second_next
    scaled_first = first_next / (1.0 - beta_first**STEP)
    scaled_second = second_next / (1.0 - beta_second**STEP)
    param = prompt[...]
    update = scaled_first / (jnp.sqrt(scaled_second) + adam_eps) + decay_rate * param
    param_norm = jnp.sqrt(jnp.sum(param * param))
    update_norm = jnp.sqrt(jnp.sum(update * update))
    norms[0] = param_norm
    norms[1] = update_norm
    prompt_new[...] = param - learn_rate * (param_norm / update_norm) * update


def lamb_call(summed, first_old, second_old, prompt):
    smem, vmem = pl.BlockSpec(memory_space=pltpu.SMEM), pl.BlockSpec(memory_space=pltpu.VMEM)
    like = jax.ShapeDtypeStruct(prompt.shape, F32)
    return pl.pallas_call(
        lamb_kernel,
        out_shape=(
            jax.ShapeDtypeStruct((1,), F32),
            jax.ShapeDtypeStruct((1,), F32),
            jax.ShapeDtypeStruct((2,), F32),
            like,
            like,
            like,
        ),
        in_specs=[vmem] * 4,
        out_specs=(smem, smem, smem, vmem, vmem, vmem),
        scratch_shapes=[pltpu.VMEM(prompt.shape, F32)],
        name="lamb",
    )(summed, first_old, second_old, prompt)


def shards(
    enc_ids,
    lengths,
    dec_ids,
    target_ids,
    loss_mask,
    embedding,
    prompt,
    first_moment,
    second_moment,
    gains,
    enc_qkv,
    enc_wo,
    enc_w1,
    enc_w2,
    dec_qkv,
    dec_wo,
    cross_q,
    cross_kv,
    cross_wo,
    dec_w1,
    dec_w2,
):
    width = embedding.shape[1]
    own = dec_wo.shape[0]
    enc_dev, tgt_dev = enc_ids.shape[1], dec_ids.shape[1]
    total_len = enc_dev * lax.axis_size(SEQ)
    lead = PROMPT // QUARTERS
    tokens = (total_len - PROMPT) // QUARTERS
    rows = total_len // QUARTERS
    ids = ids_call(enc_ids, dec_ids, target_ids)
    picked = lookup_call(ids, embedding, rows, tokens, lead, enc_dev, tgt_dev)
    summed = main_call(
        lengths,
        (prompt, loss_mask, gains),
        (
            picked,
            enc_qkv,
            enc_wo,
            enc_w1,
            enc_w2,
            jnp.transpose(dec_qkv, (1, 0, 2)),
            dec_wo,
            cross_q,
            cross_kv.reshape(width, 2 * own),
            cross_wo,
            dec_w1,
            dec_w2,
            embedding,
        ),
    )
    loss, grad_norm, norms, first_new, second_new, prompt_new = lamb_call(summed, first_moment, second_moment, prompt)
    return loss.reshape(()), grad_norm.reshape(()), norms, first_new, second_new, prompt_new


def solution(mesh):
    finer = Mesh(
        mesh.devices.reshape(mesh.shape["grp"], mesh.shape["seq"] // 2, 2, mesh.shape["head"]),
        ("grp", "ex", "chip", "head"),
    )
    placed = (
        P("grp", SEQ),
        P("grp"),
        P("grp", SEQ),
        P("grp", SEQ),
        P("grp", None),
        P("head", None),
        P(),
        P(),
        P(),
        P(),
        P(),
        P(),
        P(),
        P(),
        P(None, None, "head"),
        P("head", None),
        P(None, "head"),
        P(None, None, "head"),
        P("head", None),
        P(None, "head"),
        P("head", None),
    )
    return jax.shard_map(
        shards,
        mesh=finer,
        in_specs=placed,
        out_specs=(P(), P(), P(), P(), P(), P()),
        check_vma=False,
    )
```

```python
import functools

import jax
import jax.numpy as jnp
from jax import lax
from jax.experimental import pallas as pl
from jax.experimental.pallas import tpu as pltpu
from jax.sharding import Mesh
from jax.sharding import PartitionSpec as P

HD = 64
PROMPT = 100
STEP = 5
QUARTERS = 4
SEQ = ("ex", "chip")
CLUSTER = ("chip", "head")
EVERYONE = ("grp", "ex", "chip", "head")
NEG = -1000000000.0

norm_eps = 1e-06
beta_first = 0.5
beta_second = 0.5
adam_eps = 1e-12
decay_rate = 0.01
learn_rate = 0.3
clip_bound = 0.0001


MESH = pl.DeviceIdType.MESH
BF = jnp.bfloat16
F32 = jnp.float32
LEAD_PAD = 32
CHUNK = 1024
RING = 4
LANES = 128


def dot_nn(left, right):
    return lax.dot_general(left, right, (((1,), (0,)), ((), ())), preferred_element_type=F32)


def dot_nt(left, right):
    return lax.dot_general(left, right, (((1,), (1,)), ((), ())), preferred_element_type=F32)


def dot_tn(left, right):
    return lax.dot_general(left, right, (((0,), (0,)), ((), ())), preferred_element_type=F32)


def rms(value, gain):
    return value * lax.rsqrt(jnp.mean(value * value, axis=-1, keepdims=True) + norm_eps) * gain


def rms_grad(value, gain, grad):
    scale = lax.rsqrt(jnp.mean(value * value, axis=-1, keepdims=True) + norm_eps)
    scaled = grad * gain
    inner = jnp.mean(scaled * value, axis=-1, keepdims=True)
    return scale * scaled - value * (scale * scale * scale * inner)


GELU_A = 0.7978845608028654
GELU_B = 0.044715


def gelu(value):
    return 0.5 * value * (1.0 + jnp.tanh(GELU_A * (value + GELU_B * (value * value * value))))


def gelu_grad(value, grad):
    square = value * value
    bend = jnp.tanh(GELU_A * (value + GELU_B * (square * value)))
    slope = 0.5 * (1.0 + bend) + 0.5 * value * (1.0 - bend * bend) * (GELU_A * (1.0 + 3.0 * GELU_B * square))
    return grad * slope


def tiles(count, size, body):
    for index in range(count):
        body(pl.ds(index * size, size))


def each(count, unroll, body):
    def step(index, carry):
        body(index)
        return carry

    if unroll == count:
        for index in range(count):
            body(index)
    else:
        lax.fori_loop(0, count, step, 0, unroll=unroll)


def lanes_at(index, size, base=0):
    if isinstance(index, int):
        return pl.ds(base + index * size, size)
    return pl.ds(pl.multiple_of(base + index * size, LANES), size)


UNROLL = {"attend": 1, "self": 1, "cross": 1, "cross_back": 1, "lead": 1, "vocab": 2}


def main_kernel(
    lengths, picked, prompt, loss_mask, gains,
    enc_qkv, enc_wo, enc_w1, enc_w2, dec_qkv, dec_wo, cross_q, cross_kv, cross_wo, dec_w1, dec_w2, embedding,
    out,
    w_qkv, w_o, w_1, w_2, w_dqkv, w_do, w_cq, w_ckv, w_co, w_d1, w_d2, ring,
    lead, enc_my, enc_in, dec_my, dec_in,
    x0, h1, h2, go, spare, n1, q_s, kv, o_f, o_b, s_f, p_b, lse_e, fade_e, scale_e, stat_e, nb, u, act,
    eo, ckv, dckv, gp_s, gp_r, gown, d_o, dkv, dkv_r, gj, dl,
    y0, a1, m_b, sqkv, so, dx_s, dx_r, cq, cp, cp_b, st_p, st_r, co_r, co, co_b,
    lg, px_s, px_r, a2, a3, du, dact, f_b, tgt, acc, acc_b, acc_r, vl_s, vl_r, gffn, gco, st_g,
    blk, s1_r, s2_r, all_r,
    load_sem, ring_sem, send_sem, recv_sem,
):
    width = x0.shape[1]
    rows = x0.shape[0]
    half = f_b.shape[0]
    own = co.shape[1]
    pairs_e, pairs_d = width // LANES, own // LANES
    head, chip = lax.axis_index("head"), lax.axis_index("chip")
    mate, across = 1 - head, 1 - chip
    me, slot_mate = 2 * chip + head, 2 * chip + mate
    slot_across, slot_diag = 2 * across + head, 2 * across + mate
    to_mate, to_across = {"head": mate}, {"chip": across}
    to_diag = {"chip": across, "head": mate}

    grp, ex = lax.axis_index("grp"), lax.axis_index("ex")
    n_grp, n_ex = lax.axis_size("grp"), lax.axis_size("ex")

    def ex_peer(step):
        return {"ex": lax.rem(ex + step, n_ex)}

    def plane_peer(step):
        place = lax.rem(grp * QUARTERS + me + step, n_grp * QUARTERS)
        member = lax.div(place, QUARTERS)
        side = lax.div(place - member * QUARTERS, 2)
        return {"grp": member, "chip": side, "head": place - member * QUARTERS - 2 * side}

    barrier = pltpu.get_barrier_semaphore()
    friends = [plane_peer(step) for step in range(1, n_grp * QUARTERS)] + [ex_peer(step) for step in range(1, n_ex)]
    for peer in friends:
        pl.semaphore_signal(barrier, inc=1, device_id=peer, device_id_type=MESH)

    def load(index, source, target):
        copy = pltpu.make_async_copy(source, target, load_sem.at[index])
        copy.start()
        return copy

    my_rows = pl.ds(pl.multiple_of(head * rows, rows), rows)
    mate_rows = pl.ds(pl.multiple_of(mate * rows, rows), rows)
    dec_rows = pl.ds(2 * rows, dec_my.shape[0])
    load_x = load(0, picked.at[my_rows], enc_my)
    load_y = load(1, picked.at[dec_rows], dec_my)
    load_qkv = load(2, enc_qkv, w_qkv)
    load_dqkv = load(3, dec_qkv, w_dqkv)
    load_do = load(4, dec_wo, w_do)
    load_cq = load(5, cross_q, w_cq)
    load_o = load(6, enc_wo, w_o)
    load_1 = load(7, enc_w1, w_1)
    load_2 = load(8, enc_w2, w_2)
    load_ckv = load(9, cross_kv, w_ckv)
    load_co = load(10, cross_wo, w_co)
    load_d1 = load(11, dec_w1, w_d1)
    load_d2 = load(12, dec_w2, w_d2)
    leads = PROMPT // QUARTERS

    vocab = embedding.shape[0]
    full = vocab // CHUNK
    tail = vocab - full * CHUNK

    def chunk_copy(index, slot):
        at = pl.ds(pl.multiple_of(index * CHUNK, CHUNK), CHUNK)
        return pltpu.make_async_copy(embedding.at[at], ring.at[slot], ring_sem.at[slot])

    def tail_copy():
        slot = full % RING
        return pltpu.make_async_copy(
            embedding.at[pl.ds(full * CHUNK, tail)], ring.at[slot, pl.ds(0, tail)], ring_sem.at[slot]
        )

    for index in range(RING):
        chunk_copy(index, index).start()

    pl.semaphore_wait(barrier, len(friends))
    sends = []
    block_sem = 17 + 3 * (width // (2 * LANES))

    def send(index, source, target, peer):
        copy = pltpu.make_async_remote_copy(
            src_ref=source,
            dst_ref=target,
            send_sem=send_sem.at[index],
            recv_sem=recv_sem.at[index],
            device_id=peer,
            device_id_type=MESH,
        )
        copy.start()
        sends.append(copy)
        return copy

    blocks = rows // 64
    got_x = []
    for block in range(blocks):
        source = picked.at[pl.ds(pl.multiple_of(mate * rows + block * 64, 64), 64)]
        got_x.append(send(block_sem + block, source, enc_in.at[pl.ds(block * 64, 64)], to_mate))
    got_y = send(1, picked.at[dec_rows], dec_in, to_mate)

    lane = lax.broadcasted_iota(jnp.int32, (1, LANES), 1)
    low_lane = lane < HD
    low_b = jnp.where(low_lane, 1.0, 0.0).astype(BF)
    high_b = jnp.where(low_lane, 0.0, 1.0).astype(BF)
    sides = (low_b, high_b)
    gain = [gains[k : k + 1, :] for k in range(7)]
    gain[6] = gain[6] * width ** (-0.5)
    length = lengths[ex]
    tokens = kv.shape[1] - leads

    def allowed(slots, span, first):
        at = lax.broadcasted_iota(jnp.int32, (1, slots * span), 1)
        slot = at // span
        inner = at - slot * span
        return (inner < leads) | (tokens * (slot + first) + inner - leads < length)

    ok = allowed(4, rows, 0)
    okc = allowed(2, rows, 2 * chip)
    okf = allowed(2, rows, 2 * across)
    okl = allowed(4, LEAD_PAD, 0)
    mask_row = loss_mask[pl.ds(ex, 1), :].astype(F32)
    lane_at = lax.broadcasted_iota(jnp.int32, (half, mask_row.shape[1]), 1)
    row_of = lax.broadcasted_iota(jnp.int32, (half, mask_row.shape[1]), 0)
    own_mask = jnp.where(lane_at == row_of + chip * half, jnp.broadcast_to(mask_row, lane_at.shape), 0.0)
    share = jnp.sum(own_mask, axis=-1, keepdims=True) / jnp.sum(mask_row, axis=-1, keepdims=True)

    load_x.wait()
    got_n, got_m = [], []
    for block in range(blocks):
        part = pl.ds(block * 64, 64)
        got_x[block].wait_recv()
        value = enc_my[part].astype(F32) + enc_in[part].astype(F32)
        if block == 0:
            spot = lax.broadcasted_iota(jnp.int32, (64, width), 0)
            for slot in range(QUARTERS):
                lead[0:leads] = jnp.where(me == slot, prompt[slot * leads : (slot + 1) * leads], lead[0:leads])
            value = jnp.where(spot < leads, lead[...], value)
        x0[part] = value
        n1[me, part] = rms(value, gain[0]).astype(BF)
        mine_n = n1.at[me, part]
        got_n.append(send(block_sem + blocks + block, mine_n, mine_n, to_across))
        got_m.append(send(block_sem + 2 * blocks + block, mine_n, mine_n, to_mate))

    load_qkv.wait()

    def query(at):
        q_s[:, at] = (dot_nn(n1[me], w_qkv[:, at]).astype(BF) * HD ** (-0.5)).astype(BF)

    tiles(width // 256, 256, query)

    load_y.wait()
    got_y.wait_recv()
    all_tgt = y0.shape[0]
    value = dec_my[0:all_tgt].astype(F32) + dec_in[0:all_tgt].astype(F32)
    y0[...] = value
    m_b[...] = rms(value, gain[3]).astype(BF)
    tgt[...] = dec_my[all_tgt : all_tgt + half].astype(F32) + dec_in[all_tgt : all_tgt + half].astype(F32)
    load_dqkv.wait()

    for part in range(3):
        sqkv[:, part * own : (part + 1) * own] = dot_nn(m_b[...], w_dqkv[part]).astype(BF)
    row_at = lax.broadcasted_iota(jnp.int32, (all_tgt, all_tgt), 0)
    col_at = lax.broadcasted_iota(jnp.int32, (all_tgt, all_tgt), 1)
    def self_pair(pair):
        q2 = sqkv[:, lanes_at(pair, LANES)]
        k2 = sqkv[:, lanes_at(pair, LANES, own)]
        v2 = sqkv[:, lanes_at(pair, LANES, 2 * own)]
        outs = []
        for side in sides:
            scores = dot_nt(q2 * side, k2) * HD ** (-0.5)
            scores = jnp.where(col_at <= row_at, scores, NEG)
            top = jnp.max(scores, axis=-1, keepdims=True)
            probs = jnp.exp(scores - top)
            total = jnp.sum(probs, axis=-1, keepdims=True)
            outs.append(dot_nn(probs.astype(BF), v2) / total)
        so[:, lanes_at(pair, LANES)] = jnp.where(low_lane, outs[0], outs[1]).astype(BF)

    each(pairs_d, UNROLL["self"], self_pair)
    load_do.wait()

    def self_out(at):
        dx_s[:, at] = dot_nn(so[...], w_do[:, at]).astype(BF)

    tiles(width // 256, 256, self_out)

    got_d = send(4, dx_s, dx_r, to_mate)
    def forward(block):
        part = n1.at[slot_across, pl.ds(block * 64, 64)]
        return pltpu.make_async_remote_copy(
            src_ref=part,
            dst_ref=part,
            send_sem=send_sem.at[block_sem + 3 * blocks + block],
            recv_sem=recv_sem.at[block_sem + 3 * blocks + block],
            device_id=to_mate,
            device_id_type=MESH,
        )

    def key_value(turn):
        slot = jnp.where(turn < 2, 2 * chip, 2 * across) + jnp.where(turn % 2 == 0, head, mate)

        @pl.when(turn == 1)
        def _():
            for copy in got_m:
                copy.wait_recv()

        @pl.when(turn == 2)
        def _():
            for block in range(blocks):
                got_n[block].wait_recv()
                forward(block).start()

        @pl.when(turn == 3)
        def _():
            for block in range(blocks):
                forward(block).wait_recv()

        for index in range(2 * width // 256):
            at = pl.ds(index * 256, 256)
            kv[slot, :, at] = dot_nn(n1[slot], w_qkv[:, pl.ds(width + index * 256, 256)]).astype(BF)

    def between():
        got_d.wait_recv()
        value = y0[...] + (dx_s[...].astype(F32) + dx_r[...].astype(F32))
        a1[...] = value
        m_b[...] = rms(value, gain[4]).astype(BF)
        load_cq.wait()
        cq[...] = (dot_nn(m_b[...], w_cq[...]).astype(BF) * HD ** (-0.5)).astype(BF)

    def key_values(first, last):
        def body(turn, carry):
            key_value(turn)
            return carry

        lax.fori_loop(first, last, body, 0)

    between()

    keys = 4 * rows

    def scores_of(pair, side, index, slots, allowed_keys):
        k2 = kv[slots, :, lanes_at(pair, LANES)].reshape(2 * rows, LANES)
        v2 = kv[slots, :, lanes_at(pair, LANES, width)].reshape(2 * rows, LANES)
        s_f[index] = dot_nt(q_s[:, lanes_at(pair, LANES)] * side, k2)
        return v2

    def near_pair(pair):
        slots = pl.ds(2 * chip, 2)
        outs = []
        for index, side in enumerate(sides):
            v2 = scores_of(pair, side, index, slots, okc)
            for block in range(rows // 32):
                part = pl.ds(block * 32, 32)
                scores = jnp.where(okc, s_f[index, part], NEG)
                top = jnp.max(scores, axis=-1, keepdims=True)
                probs = jnp.exp(scores - top)
                p_b[index, part] = probs.astype(BF)
                total = jnp.sum(probs, axis=-1, keepdims=True)
                u[part, lanes_at(index * pairs_e + pair, LANES)] = jnp.broadcast_to(total, (32, LANES))
                u[part, lanes_at(index * pairs_e + pair, LANES, 2 * width)] = jnp.broadcast_to(top, (32, LANES))
            outs.append(dot_nn(p_b[index], v2))
        o_f[:, lanes_at(pair, LANES)] = jnp.where(low_lane, outs[0], outs[1])

    def far_pair(pair):
        slots = pl.ds(2 * across, 2)
        outs = []
        for index, side in enumerate(sides):
            v2 = scores_of(pair, side, index, slots, okf)
            for block in range(rows // 32):
                part = pl.ds(block * 32, 32)
                scores = jnp.where(okf, s_f[index, part], NEG)
                near_top = u[part, lanes_at(index * pairs_e + pair, LANES, 2 * width)]
                own_top = jnp.max(scores, axis=-1, keepdims=True)
                top = jnp.maximum(jnp.broadcast_to(own_top, (32, LANES)), near_top)
                probs = jnp.exp(scores - jnp.concatenate([top] * (2 * rows // LANES), axis=1))
                fade = jnp.exp(near_top - top)
                total = jnp.broadcast_to(jnp.sum(probs, axis=-1, keepdims=True), (32, LANES))
                total = total + u[part, lanes_at(index * pairs_e + pair, LANES)] * fade
                p_b[index, part] = probs.astype(BF)
                fade_e[index, part] = fade
                scale_e[index, part] = 1.0 / total
                stat_e[index, part] = top + jnp.log(total)
            wide = dot_nn(p_b[index], v2) + o_f[:, lanes_at(pair, LANES)] * fade_e[index]
            outs.append(wide * scale_e[index])
        lse_e[pair] = jnp.where(low_lane, stat_e[0], stat_e[1])
        both = jnp.where(low_lane, outs[0], outs[1])
        o_f[:, lanes_at(pair, LANES)] = both
        o_b[:, lanes_at(pair, LANES)] = both.astype(BF)

    key_values(0, 2)
    each(pairs_e, UNROLL["attend"], near_pair)
    key_values(2, 4)
    sends.extend(forward(block) for block in range(blocks))
    each(pairs_e, UNROLL["attend"], far_pair)
    load_o.wait()

    def out_cols(at):
        h1[:, at] = x0[:, at] + dot_nn(o_b[...], w_o[:, at])

    tiles(width // 256, 256, out_cols)

    def norm_two(at):
        nb[at] = rms(h1[at], gain[1]).astype(BF)

    tiles(rows // 64, 64, norm_two)
    load_1.wait()

    def hidden(at):
        value = dot_nn(nb[...], w_1[:, at])
        u[:, at] = value
        act[:, at] = gelu(value).astype(BF)

    tiles(u.shape[1] // 256, 256, hidden)
    load_2.wait()

    def hidden_out(at):
        h2[:, at] = h1[:, at] + dot_nn(act[...], w_2[:, at])

    tiles(width // 256, 256, hidden_out)

    def norm_out(at):
        eo[head, at] = rms(h2[at], gain[2]).astype(BF)

    tiles(rows // 64, 64, norm_out)
    got_e = send(6, eo.at[head], eo.at[head], to_mate)
    load_ckv.wait()

    def cross_keys(slot):
        def body(at):
            ckv[slot, :, at] = dot_nn(eo[slot], w_ckv[:, at]).astype(BF)

        tiles(2 * own // 256, 256, body)

    cross_keys(head)
    got_e.wait_recv()
    cross_keys(mate)


    def cross_pair(pair):
        k2 = ckv[:, :, lanes_at(pair, LANES)].reshape(2 * rows, LANES)
        v2 = ckv[:, :, lanes_at(pair, LANES, own)].reshape(2 * rows, LANES)
        return cq[:, lanes_at(pair, LANES)], k2, v2

    st_p[...] = jnp.zeros_like(st_p)

    def cross_attend(pair):
        q2, k2, v2 = cross_pair(pair)
        stats = st_p[...]
        outs = []
        for index, side in enumerate(sides):
            scores = jnp.where(okc, dot_nt(q2 * side, k2), NEG)
            top = jnp.max(scores, axis=-1, keepdims=True)
            probs = jnp.exp(scores - top)
            total = jnp.sum(probs, axis=-1, keepdims=True)
            outs.append(dot_nn(probs.astype(BF), v2) / total)
            stats = jnp.where(lane == 2 * pair + index, top + jnp.log(total), stats)
        both = jnp.where(low_lane, outs[0], outs[1])
        cp[:, lanes_at(pair, LANES)] = both
        cp_b[:, lanes_at(pair, LANES)] = both.astype(BF)
        st_p[...] = stats

    each(pairs_d, UNROLL["cross"], cross_attend)
    mine_t = pl.ds(pl.multiple_of(chip * half, half), half)
    theirs_t = pl.ds(pl.multiple_of(across * half, half), half)
    got_c = send(7, cp_b.at[theirs_t], co_r, to_across)
    got_s = send(8, st_p.at[theirs_t], st_r, to_across)
    got_c.wait_recv()
    got_s.wait_recv()
    l_own, l_oth = st_p[mine_t], st_r[...]
    top = jnp.maximum(l_own, l_oth)
    lse_c = top + jnp.log(jnp.exp(l_own - top) + jnp.exp(l_oth - top))
    w_own, w_oth = jnp.exp(l_own - lse_c), jnp.exp(l_oth - lse_c)

    def side_cols(array, pair):
        return jnp.where(
            low_lane, array[:, 2 * pair : 2 * pair + 1], array[:, 2 * pair + 1 : 2 * pair + 2]
        )

    for pair in range(pairs_d):
        lo = pair * LANES
        both = cp[mine_t, lo : lo + LANES] * side_cols(w_own, pair)
        both = both + co_r[:, lo : lo + LANES].astype(F32) * side_cols(w_oth, pair)
        co[:, lo : lo + LANES] = both
        co_b[:, lo : lo + LANES] = both.astype(BF)

    def exchange(index, value):
        slot = index - 9
        px_s[slot] = value.astype(BF)
        got = send(index, px_s.at[slot], px_r.at[slot], to_mate)
        got.wait_recv()
        return px_s[slot].astype(F32) + px_r[slot].astype(F32)

    load_co.wait()
    a2[...] = a1[mine_t] + exchange(9, dot_nn(co_b[...], w_co[...]))
    m_b[0:half] = rms(a2[...], gain[5]).astype(BF)
    load_d1.wait()

    def dec_hidden(at):
        value = dot_nn(m_b[0:half], w_d1[:, at])
        du[:, at] = value
        dact[:, at] = gelu(value).astype(BF)

    tiles(du.shape[1] // 512, 512, dec_hidden)
    load_d2.wait()
    a3[...] = a2[...] + exchange(10, dot_nn(dact[...], w_d2[...]))
    f_b[...] = rms(a3[...], gain[6]).astype(BF)

    acc[...] = jnp.zeros_like(acc)

    def vocab_step(logits, table, top, total):
        new_top = jnp.maximum(top, jnp.max(logits, axis=-1, keepdims=True))
        fade = jnp.exp(top - new_top)
        probs = jnp.exp(logits - new_top)
        acc[...] = acc[...] * fade + dot_nn(probs.astype(BF), table)
        return new_top, total * fade + jnp.sum(probs, axis=-1, keepdims=True)

    def refill(index, slot):
        @pl.when(index + RING < full)
        def _():
            chunk_copy(index + RING, slot).start()

        if tail:

            @pl.when(index + RING == full)
            def _():
                tail_copy().start()

    span = UNROLL["vocab"]
    chunk_copy(0, 0).wait()
    lg[0] = dot_nt(f_b[...], ring[0])

    def vocab_chunks(turn, carry):
        first = span * turn
        slots = [lax.rem(first + k, RING) for k in range(span + 1)]
        for k in range(span):
            chunk_copy(first + k + 1, slots[k + 1]).wait()
            lg[(k + 1) % 2] = dot_nt(f_b[...], ring[slots[k + 1]])
            carry = vocab_step(lg[k % 2], ring[slots[k]], *carry)
            refill(first + k, slots[k])
        return carry

    carry = (jnp.full((half, 1), NEG, F32), jnp.zeros((half, 1), F32))
    turns = (full - 1) // span
    carry = lax.fori_loop(0, turns, vocab_chunks, carry)
    for index in range(span * turns, full):
        slot, after = index % RING, (index + 1) % RING
        if index + 1 < full:
            chunk_copy(index + 1, after).wait()
            lg[(index + 1) % 2] = dot_nt(f_b[...], ring[after])
        elif tail:
            tail_copy().wait()
            lg[(index + 1) % 2, :, 0:tail] = dot_nt(f_b[...], ring[after, 0:tail])
        carry = vocab_step(lg[index % 2], ring[slot], *carry)
        refill(index, slot)
    if tail:
        carry = vocab_step(lg[full % 2, :, 0:tail], ring[full % RING, 0:tail], *carry)
    top, total = carry
    acc_b[...] = (acc[...] / total).astype(BF)
    vl_s[...] = jnp.broadcast_to(top + jnp.log(total), vl_s.shape)
    got_a = send(11, acc_b, acc_r, to_mate)
    got_v = send(12, vl_s, vl_r, to_mate)
    pick = jnp.sum(f_b[...].astype(F32) * tgt[...], axis=-1, keepdims=True)
    got_a.wait_recv()
    got_v.wait_recv()
    l_own, l_oth = vl_s[:, 0:1], vl_r[:, 0:1]
    top = jnp.maximum(l_own, l_oth)
    lse_v = top + jnp.log(jnp.exp(l_own - top) + jnp.exp(l_oth - top))
    loss = jnp.sum(share * (lse_v - pick), axis=0, keepdims=True) * jnp.where(head == 0, 1.0, 0.0)
    mean_row = acc_b[...].astype(F32) * jnp.exp(l_own - lse_v) + acc_r[...].astype(F32) * jnp.exp(l_oth - lse_v)
    gffn[...] = rms_grad(a3[...], gain[6], share * (mean_row - tgt[...]))

    m_b[0:half] = gffn[...].astype(BF)

    def dec_hidden_grad(at):
        value = dot_nt(m_b[0:half], w_d2[at])
        dact[:, at] = gelu_grad(du[:, at], value).astype(BF)

    tiles(du.shape[1] // 512, 512, dec_hidden_grad)
    slope = exchange(13, dot_nt(dact[...], w_d1[...]))
    gcross = gffn[...] + rms_grad(a2[...], gain[5], slope)
    gco[chip] = dot_nt(gcross.astype(BF), w_co[...]).astype(BF)
    stats = lse_c
    for pair in range(pairs_d):
        lo = pair * LANES
        value = gco[chip, :, lo : lo + LANES].astype(F32) * co[:, lo : lo + LANES]
        for index in range(2):
            picked_side = jnp.where(low_lane == (index == 0), value, 0.0)
            delta = jnp.sum(picked_side, axis=-1, keepdims=True)
            stats = jnp.where(lane == HD + 2 * pair + index, delta, stats)
    st_g[chip] = stats
    got_g = send(14, gco.at[chip], gco.at[chip], to_across)
    got_t = send(15, st_g.at[chip], st_g.at[chip], to_across)
    got_g.wait_recv()
    got_t.wait_recv()

    def cross_back(pair):
        q2, k2, v2 = cross_pair(pair)
        do2 = gco[:, :, lanes_at(pair, LANES)].reshape(all_tgt, LANES)
        stats = st_g[...].reshape(all_tgt, LANES)
        dks, dvs = [], []
        for index, side in enumerate(sides):
            column = 2 * pair + index
            lse = jnp.sum(jnp.where(lane == column, stats, 0.0), axis=-1, keepdims=True)
            delta = jnp.sum(jnp.where(lane == HD + column, stats, 0.0), axis=-1, keepdims=True)
            scores = jnp.where(okc, dot_nt(q2 * side, k2), NEG)
            probs = jnp.exp(scores - lse)
            dp = dot_nt(do2 * side, v2)
            ds = (probs * (dp - delta)).astype(BF)
            dks.append(dot_tn(ds, q2))
            dvs.append(dot_tn(probs.astype(BF), do2))
        shape = (2, rows, LANES)
        dckv[:, :, lanes_at(pair, LANES)] = jnp.where(low_lane, *dks).astype(BF).reshape(shape)
        dckv[:, :, lanes_at(pair, LANES, own)] = jnp.where(low_lane, *dvs).astype(BF).reshape(shape)

    each(pairs_d, UNROLL["cross_back"], cross_back)
    def pair_grad_mate(at):
        gp_s[:, at] = dot_nt(dckv[mate], w_ckv[at]).astype(BF)

    tiles(width // 256, 256, pair_grad_mate)
    got_p = send(16, gp_s, gp_r, to_mate)

    def pair_grad_mine(at):
        gown[:, at] = dot_nt(dckv[head], w_ckv[at])

    tiles(width // 256, 256, pair_grad_mine)
    got_p.wait_recv()

    def out_grad(at):
        value = rms_grad(h2[at], gain[2], gown[at].astype(BF).astype(F32) + gp_r[at].astype(F32))
        go[at] = value
        nb[at] = value.astype(BF)

    tiles(rows // 64, 64, out_grad)

    def hidden_grad(at):
        act[:, at] = gelu_grad(u[:, at], dot_nt(nb[...], w_2[at])).astype(BF)

    tiles(u.shape[1] // 256, 256, hidden_grad)

    def norm_two_grad(at):
        spare[:, at] = dot_nt(act[...], w_1[at])

    tiles(width // 256, 256, norm_two_grad)

    def one_grad(at):
        value = go[at] + rms_grad(h1[at], gain[1], spare[at])
        go[at] = value
        nb[at] = value.astype(BF)

    tiles(rows // 64, 64, one_grad)

    def attn_grad(at):
        d_o[:, at] = dot_nt(nb[...], w_o[at]).astype(BF)

    tiles(width // 256, 256, attn_grad)

    lead_keys = 4 * LEAD_PAD

    quad = 2 * LANES
    heads_in = quad // HD
    quad_lane = lax.broadcasted_iota(jnp.int32, (1, quad), 1)
    quad_of = [(quad_lane >= k * HD) & (quad_lane < (k + 1) * HD) for k in range(heads_in)]
    quad_b = [jnp.where(inside, 1.0, 0.0).astype(BF) for inside in quad_of]

    def lead_pair(group, part):
        pair = 2 * group + part
        at = lanes_at(pair, LANES)
        q2, do2 = q_s[:, at], d_o[:, at]
        k2 = kv[:, 0:LEAD_PAD, at].reshape(lead_keys, LANES)
        v2 = kv[:, 0:LEAD_PAD, lanes_at(pair, LANES, width)].reshape(lead_keys, LANES)
        value = do2.astype(F32) * o_f[:, at]
        dks, dvs, deltas = [], [], []
        for index, side in enumerate(sides):
            delta = jnp.sum(jnp.where(low_lane == (index == 0), value, 0.0), axis=-1, keepdims=True)
            deltas.append(delta)
            lse = lse_e[pair, :, index * HD : index * HD + 1]
            scores = jnp.where(okl, dot_nt(q2 * side, k2), NEG)
            probs = jnp.exp(scores - lse)
            ds = (probs * (dot_nt(do2 * side, v2) - delta)).astype(BF)
            dks.append(dot_tn(ds, q2))
            dvs.append(dot_tn(probs.astype(BF), do2))
        lo = part * LANES
        shape = (4, LEAD_PAD, LANES)
        dkv[group, :, :, lo : lo + LANES] = jnp.where(low_lane, *dks).astype(BF).reshape(shape)
        dkv[group, :, :, quad + lo : quad + lo + LANES] = jnp.where(low_lane, *dvs).astype(BF).reshape(shape)
        dl[pair] = jnp.where(low_lane, *[d[0:LEAD_PAD] for d in deltas])

    def stack(value):
        return jnp.concatenate([value * side for side in quad_b], axis=0)

    def column(ref, group, rows_at):
        return jnp.concatenate(
            [ref[2 * group + k // 2, rows_at, (k % 2) * HD : (k % 2) * HD + 1] for k in range(heads_in)], axis=0
        )

    def query_quad(group):
        at, vat = lanes_at(group, quad), lanes_at(group, quad, width)
        lead_rows = slice(0, LEAD_PAD)
        k4 = kv[:, :, at].reshape(keys, quad)
        v4 = kv[:, :, vat].reshape(keys, quad)
        scores = jnp.where(ok, dot_nt(stack(q_s[lead_rows, at]), k4), NEG)
        probs = jnp.exp(scores - column(lse_e, group, lead_rows))
        ds = (probs * (dot_nt(stack(d_o[lead_rows, at]), v4) - column(dl, group, lead_rows))).astype(BF)
        wide = dot_nn(ds, k4)
        value = jnp.zeros((LEAD_PAD, quad), F32)
        for k in range(heads_in):
            value = jnp.where(quad_of[k], wide[k * LEAD_PAD : (k + 1) * LEAD_PAD], value)
        gj[:, at] = (value * HD ** (-0.5)).astype(BF)

    def key_copies(group):
        plan = ((slot_across, 1, to_across), (slot_diag, 2, to_diag), (slot_mate, 0, to_mate))
        copies = []
        for k, (slot, place, peer) in enumerate(plan):
            copies.append(
                pltpu.make_async_remote_copy(
                    src_ref=dkv.at[group, slot],
                    dst_ref=dkv_r.at[group, place],
                    send_sem=send_sem.at[17 + 3 * group + k],
                    recv_sem=recv_sem.at[17 + 3 * group + k],
                    device_id=peer,
                    device_id_type=MESH,
                )
            )
        return copies

    def lead_group(group):
        lead_pair(group, 0)
        lead_pair(group, 1)
        for copy in key_copies(group):
            copy.start()

    each(width // quad, UNROLL["lead"], lead_group)
    each(width // quad, UNROLL["lead"], query_quad)
    for group in range(width // quad):
        summed = dkv[group, me].astype(F32)
        copies = key_copies(group)
        for index in range(3):
            copies[(2, 0, 1)[index]].wait_recv()
            summed = summed + dkv_r[group, index].astype(F32)
        sends.extend(copies)
        lo = group * quad
        gj[:, width + lo : width + lo + quad] = summed[:, :quad].astype(BF)
        gj[:, 2 * width + lo : 2 * width + lo + quad] = summed[:, quad:].astype(BF)

    def start_grad(at):
        spare[0:LEAD_PAD, at] = dot_nt(gj[...], w_qkv[at])

    tiles(width // 256, 256, start_grad)
    top_rows = slice(0, LEAD_PAD)
    value = go[top_rows] + rms_grad(x0[top_rows], gain[0], spare[top_rows])
    spot = lax.broadcasted_iota(jnp.int32, (LEAD_PAD, width), 0)
    extra = jnp.where(spot == leads, loss, 0.0)
    blk[...] = jnp.where(spot < leads, value, extra)

    piece = LEAD_PAD // n_grp
    fold = 16 // piece if piece < 16 else 1
    narrow = width // fold
    base = leads - leads % piece
    line_at = lax.broadcasted_iota(jnp.int32, (piece, width), 0)

    def folded(value, member):
        first = leads - base
        lines = value[first : first + 1] + value[first + 1 : first + 2] + value[first + 2 : first + 3]
        for k in range(3):
            high = lines.astype(BF).astype(F32)
            value = jnp.where((line_at == first + k) & (member * piece == base), high, value)
            lines = lines - high
        parts = [value[:, k * narrow : (k + 1) * narrow] for k in range(fold)]
        return jnp.concatenate(parts, axis=0).astype(BF) if fold > 1 else value.astype(BF)

    def unfolded(value):
        value = value.astype(F32)
        parts = [value[k * piece : (k + 1) * piece] for k in range(fold)]
        return jnp.concatenate(parts, axis=1) if fold > 1 else value

    slot = block_sem + 4 * blocks
    got = []
    for step in range(n_grp):
        member = lax.rem(grp + step, n_grp)
        rows_at = pl.ds(pl.multiple_of(member * piece, piece), piece)
        if step:
            got.append(send(slot, blk.at[rows_at], s1_r.at[step], {"grp": member}))
            slot += 1
    value = blk[pl.ds(pl.multiple_of(grp * piece, piece), piece)]
    for step in range(1, n_grp):
        got[step - 1].wait_recv()
        value = value + s1_r[step]
    s2_r[ex] = value
    got = []
    for step in range(1, n_ex):
        got.append(send(slot, s2_r.at[ex], s2_r.at[ex], ex_peer(step)))
        slot += 1
    for copy in got:
        copy.wait_recv()
    value = s2_r[0]
    for member in range(1, n_ex):
        value = value + s2_r[member]
    all_r[me, grp] = folded(value, grp)
    got = []
    for step in range(1, n_grp * QUARTERS):
        got.append(send(slot, all_r.at[me, grp], all_r.at[me, grp], plane_peer(step)))
        slot += 1
    for copy in got:
        copy.wait_recv()
    for quarter in range(QUARTERS):
        for member in range(n_grp):
            out[quarter, member * piece : (member + 1) * piece] = unfolded(all_r[quarter, member])
    for copy in sends:
        copy.wait_send()


def main_call(lengths, vmem, hbm):
    half = vmem[1].shape[1] // 2
    rows = (hbm[0].shape[0] - 3 * half) // 2
    wq, wo, w1, w2, dqkv, dwo, cqw, ckvw, cwo, dw1, dw2, emb = hbm[1:]
    width, own, ff, dff, tgt_all = wo.shape[0], dwo.shape[0], w1.shape[1], dw1.shape[1], 2 * half
    pairs_e = width // LANES

    def v(shape, kind=F32):
        return pltpu.VMEM(shape, kind)

    scratch = [v(w.shape, BF) for w in hbm[1:12]]
    scratch += [v((RING, CHUNK, width), BF)]
    scratch += [v((64, width))]
    scratch += [v((rows, width), BF), v((rows, width), BF), v((tgt_all + half, width), BF), v((tgt_all + half, width), BF)]
    scratch += [v((rows, width)) for _ in range(5)]
    scratch += [v((4, rows, width), BF), v((rows, width), BF), v((4, rows, 2 * width), BF)]
    scratch += [v((rows, width)), v((rows, width), BF), v((2, rows, 2 * rows)), v((2, rows, 2 * rows), BF)]
    scratch += [v((pairs_e, rows, LANES))]
    scratch += [v((2, rows, LANES)), v((2, rows, LANES)), v((2, rows, LANES)), v((rows, width), BF)]
    scratch += [v((rows, ff)), v((rows, ff), BF)]
    scratch += [v((2, rows, width), BF), v((2, rows, 2 * own), BF), v((2, rows, 2 * own), BF)]
    scratch += [v((rows, width), BF), v((rows, width), BF), v((rows, width)), v((rows, width), BF)]
    groups = width // (2 * LANES)
    scratch += [v((groups, 4, LEAD_PAD, 4 * LANES), BF), v((groups, 3, LEAD_PAD, 4 * LANES), BF), v((LEAD_PAD, 3 * width), BF)]
    scratch += [v((pairs_e, LEAD_PAD, LANES))]
    scratch += [v((tgt_all, width)), v((tgt_all, width)), v((tgt_all, width), BF), v((tgt_all, 3 * own), BF)]
    scratch += [v((tgt_all, own), BF), v((tgt_all, width), BF), v((tgt_all, width), BF), v((tgt_all, own), BF)]
    scratch += [v((tgt_all, own)), v((tgt_all, own), BF), v((tgt_all, LANES)), v((half, LANES))]
    scratch += [v((half, own), BF), v((half, own)), v((half, own), BF)]
    scratch += [v((2, half, CHUNK))]
    scratch += [v((5, half, width), BF), v((5, half, width), BF)]
    scratch += [v((half, width)), v((half, width)), v((half, dff)), v((half, dff), BF), v((half, width), BF)]
    scratch += [v((half, width)), v((half, width)), v((half, width), BF), v((half, width), BF)]
    scratch += [v((half, LANES)), v((half, LANES)), v((half, width)), v((2, half, own), BF), v((2, half, LANES))]
    n_grp, n_ex = lax.axis_size("grp"), lax.axis_size("ex")
    piece = LEAD_PAD // n_grp
    fold = 16 // piece if piece < 16 else 1
    folded = (piece * fold, width // fold)
    scratch += [v((LEAD_PAD, width)), v((n_grp, piece, width)), v((n_ex, piece, width))]
    scratch += [v((QUARTERS, n_grp, *folded), BF)]
    exchanges = 17 + 3 * groups + 4 * (rows // 64) + (n_grp - 1) + (n_ex - 1) + (n_grp * QUARTERS - 1)
    scratch += [
        pltpu.SemaphoreType.DMA((13,)),
        pltpu.SemaphoreType.DMA((RING,)),
        pltpu.SemaphoreType.DMA((exchanges,)),
        pltpu.SemaphoreType.DMA((exchanges,)),
    ]
    any_spec, vmem_spec = pl.BlockSpec(memory_space=pl.ANY), pl.BlockSpec(memory_space=pltpu.VMEM)
    return pl.pallas_call(
        main_kernel,
        out_shape=jax.ShapeDtypeStruct((QUARTERS, LEAD_PAD, width), F32),
        in_specs=[pl.BlockSpec(memory_space=pltpu.SMEM), any_spec] + [vmem_spec] * len(vmem) + [any_spec] * len(hbm[1:]),
        out_specs=vmem_spec,
        scratch_shapes=scratch,
        compiler_params=pltpu.CompilerParams(
            collective_id=1, has_side_effects=True, vmem_limit_bytes=62 * 1024 * 1024
        ),
        name="step_of_one_example",
    )(lengths, hbm[0], *vmem, *hbm[1:])


def log2(size):
    return size.bit_length() - 1


def ids_kernel(enc_ids, dec_ids, target_ids, out, lines, got, unused, send_sem, recv_sem):
    ex, chip = lax.axis_index("ex"), lax.axis_index("chip")
    chips = lax.axis_size("chip")
    seqs = lax.axis_size(SEQ)
    me = ex * chips + chip
    enc_dev, tgt_dev = enc_ids.shape[1], dec_ids.shape[1]


    def peer_of(step):
        peer = lax.rem(me + step, seqs)
        row = lax.div(peer, chips)
        return row, {"ex": row, "chip": peer - row * chips}

    barrier = pltpu.get_barrier_semaphore()
    for step in range(1, seqs):
        pl.semaphore_signal(barrier, inc=1, device_id=peer_of(step)[1], device_id_type=MESH)
    lines[:, 0:enc_dev] = enc_ids[...]
    lines[:, enc_dev : enc_dev + tgt_dev] = dec_ids[...]
    lines[:, enc_dev + tgt_dev : enc_dev + 2 * tgt_dev] = target_ids[...]
    lines[:, enc_dev + 2 * tgt_dev :] = jnp.zeros((lines.shape[0], lines.shape[1] - enc_dev - 2 * tgt_dev), jnp.int32)
    pl.semaphore_wait(barrier, seqs - 1)

    for step in range(1, seqs):
        row, peer = peer_of(step)
        pltpu.make_async_remote_copy(
            src_ref=lines.at[pl.ds(row, 1)],
            dst_ref=got.at[pl.ds(me, 1)],
            send_sem=send_sem,
            recv_sem=recv_sem,
            device_id=peer,
            device_id_type=MESH,
        ).start()
    own_line = lines.at[pl.ds(ex, 1)]
    pltpu.make_async_copy(own_line, got.at[pl.ds(me, 1)], recv_sem).start()
    pltpu.make_async_copy(own_line, unused.at[pl.ds(0, 1)], send_sem).start()
    pltpu.make_async_copy(got, got, recv_sem).wait()
    pltpu.make_async_copy(got, got, send_sem).wait()
    out[...] = got[...]


def ids_call(enc_ids, dec_ids, target_ids):
    seqs = lax.axis_size(SEQ)
    lanes = -(-(enc_ids.shape[1] + 2 * dec_ids.shape[1]) // LANES) * LANES
    return pl.pallas_call(
        ids_kernel,
        out_shape=jax.ShapeDtypeStruct((seqs, lanes), jnp.int32),
        in_specs=[pl.BlockSpec(memory_space=pltpu.VMEM)] * 3,
        out_specs=pl.BlockSpec(memory_space=pltpu.VMEM),
        scratch_shapes=[
            pltpu.VMEM((enc_ids.shape[0], lanes), jnp.int32),
            pltpu.VMEM((seqs, lanes), jnp.int32),
            pltpu.VMEM((8, lanes), jnp.int32),
            pltpu.SemaphoreType.DMA,
            pltpu.SemaphoreType.DMA,
        ],
        compiler_params=pltpu.CompilerParams(collective_id=2, has_side_effects=True),
        name="ids_of_one_example",
    )(enc_ids, dec_ids, target_ids)


GROUP = 16


AHEAD = 8


def lookup_kernel(rows, tokens, lead, enc_dev, tgt_dev, ids, table, out, blocks, spots, sems):
    chip, head = lax.axis_index("chip"), lax.axis_index("head")
    vocab_part = table.shape[0]
    enc_count = 2 * rows
    tgt_all = tgt_dev * ids.shape[0]
    half = tgt_all // 2
    groups = out.shape[0] // GROUP
    first, second = enc_count // GROUP, (enc_count + tgt_all) // GROUP

    def fetch(group):
        enc = group < first
        slot = (group * GROUP) >> log2(rows)
        enc_base = (PROMPT - lead) + tokens * (2 * chip + slot) + ((group * GROUP) & (rows - 1))
        dec_base = (group - jnp.where(group < second, first, second)) * GROUP
        dec_base = dec_base + jnp.where(group < second, 0, chip * half)
        base = jnp.where(enc, enc_base, dec_base)
        shift = jnp.where(enc, log2(enc_dev), log2(tgt_dev))
        mask = jnp.where(enc, enc_dev - 1, tgt_dev - 1)
        lane = jnp.where(enc, 0, jnp.where(group < second, enc_dev, enc_dev + tgt_dev))
        for k in range(GROUP):
            token = ids[(base + k) >> shift, lane + ((base + k) & mask)]
            upper = jnp.where(token >= vocab_part, 1, 0)
            local = token - upper * vocab_part
            spots[group * GROUP + k] = k * GROUP + (local & (GROUP - 1)) + ((upper + head - 2 * upper * head) * 4096)
            at = pl.multiple_of((local >> log2(GROUP)) << log2(GROUP), GROUP)
            pltpu.make_async_copy(
                table.at[pl.ds(at, GROUP)], blocks.at[group * GROUP + k], sems.at[group]
            ).start()

    across = lax.broadcasted_iota(jnp.int32, (8, LANES), 1)
    down = lax.broadcasted_iota(jnp.int32, (8, LANES), 0)

    def select(group):
        at = pl.ds(pl.multiple_of(group * GROUP, GROUP), GROUP)
        pltpu.make_async_copy(blocks.at[at], blocks.at[at], sems.at[group]).wait()
        chosen = []
        for part in range(GROUP // 8):
            want = jnp.full((8, LANES), -1, jnp.int32)
            for k in range(8):
                want = jnp.where(down == k, spots[group * GROUP + part * 8 + k], want)
            hits = [jnp.where(across + base == want, 1.0, 0.0) for base in range(0, GROUP * GROUP, LANES)]
            chosen.append(jnp.concatenate(hits, axis=1))
        chosen = jnp.concatenate(chosen, axis=0).astype(BF)
        out[at] = dot_nn(chosen, blocks[at].reshape(GROUP * GROUP, out.shape[1])).astype(BF)

    def loop(start, stop, *steps):
        def body(group, carry):
            for step in steps:
                step(group)
            return carry

        lax.fori_loop(start, stop, body, 0)

    loop(0, AHEAD, fetch)
    loop(AHEAD, groups, fetch, lambda group: select(group - AHEAD))
    loop(groups - AHEAD, groups, select)


def lookup_call(ids, table, rows, tokens, lead, enc_dev, tgt_dev):
    count = 2 * rows + tgt_dev * ids.shape[0] * 3 // 2
    width = table.shape[1]
    return pl.pallas_call(
        functools.partial(lookup_kernel, rows, tokens, lead, enc_dev, tgt_dev),
        out_shape=jax.ShapeDtypeStruct((count, width), BF),
        in_specs=[pl.BlockSpec(memory_space=pltpu.SMEM), pl.BlockSpec(memory_space=pl.ANY)],
        out_specs=pl.BlockSpec(memory_space=pltpu.VMEM),
        scratch_shapes=[
            pltpu.VMEM((count, GROUP, width), BF),
            pltpu.SMEM((count,), jnp.int32),
            pltpu.SemaphoreType.DMA((count // GROUP,)),
        ],
        compiler_params=pltpu.CompilerParams(vmem_limit_bytes=32 * 1024 * 1024),
        name="embedding_rows",
    )(ids, table)


def lamb_kernel(summed, first_old, second_old, prompt, loss, grad_norm, norms, first_new, second_new, prompt_new, work):
    lead = PROMPT // QUARTERS
    for quarter in range(QUARTERS):
        work[quarter * lead : (quarter + 1) * lead] = summed[quarter, 0:lead]
    grad = work[...]
    total = summed[0, lead : lead + 3, 0:1]
    for quarter in range(1, QUARTERS):
        total = total + summed[quarter, lead : lead + 3, 0:1]
    loss[0] = jnp.sum(total)
    norm = jnp.sqrt(jnp.sum(grad * grad))
    grad_norm[0] = norm
    clipped = grad * (clip_bound / jnp.maximum(norm, clip_bound))
    first_next = beta_first * first_old[...] + (1.0 - beta_first) * clipped
    second_next = beta_second * second_old[...] + (1.0 - beta_second) * clipped * clipped
    first_new[...] = first_next
    second_new[...] = second_next
    scaled_first = first_next / (1.0 - beta_first**STEP)
    scaled_second = second_next / (1.0 - beta_second**STEP)
    param = prompt[...]
    update = scaled_first / (jnp.sqrt(scaled_second) + adam_eps) + decay_rate * param
    param_norm = jnp.sqrt(jnp.sum(param * param))
    update_norm = jnp.sqrt(jnp.sum(update * update))
    norms[0] = param_norm
    norms[1] = update_norm
    prompt_new[...] = param - learn_rate * (param_norm / update_norm) * update


def lamb_call(summed, first_old, second_old, prompt):
    smem, vmem = pl.BlockSpec(memory_space=pltpu.SMEM), pl.BlockSpec(memory_space=pltpu.VMEM)
    like = jax.ShapeDtypeStruct(prompt.shape, F32)
    return pl.pallas_call(
        lamb_kernel,
        out_shape=(
            jax.ShapeDtypeStruct((1,), F32),
            jax.ShapeDtypeStruct((1,), F32),
            jax.ShapeDtypeStruct((2,), F32),
            like,
            like,
            like,
        ),
        in_specs=[vmem] * 4,
        out_specs=(smem, smem, smem, vmem, vmem, vmem),
        scratch_shapes=[pltpu.VMEM(prompt.shape, F32)],
        name="lamb",
    )(summed, first_old, second_old, prompt)


def shards(
    enc_ids,
    lengths,
    dec_ids,
    target_ids,
    loss_mask,
    embedding,
    prompt,
    first_moment,
    second_moment,
    gains,
    enc_qkv,
    enc_wo,
    enc_w1,
    enc_w2,
    dec_qkv,
    dec_wo,
    cross_q,
    cross_kv,
    cross_wo,
    dec_w1,
    dec_w2,
):
    width = embedding.shape[1]
    own = dec_wo.shape[0]
    enc_dev, tgt_dev = enc_ids.shape[1], dec_ids.shape[1]
    total_len = enc_dev * lax.axis_size(SEQ)
    lead = PROMPT // QUARTERS
    tokens = (total_len - PROMPT) // QUARTERS
    rows = total_len // QUARTERS
    ids = ids_call(enc_ids, dec_ids, target_ids)
    picked = lookup_call(ids, embedding, rows, tokens, lead, enc_dev, tgt_dev)
    summed = main_call(
        lengths,
        (prompt, loss_mask, gains),
        (
            picked,
            enc_qkv,
            enc_wo,
            enc_w1,
            enc_w2,
            jnp.transpose(dec_qkv, (1, 0, 2)),
            dec_wo,
            cross_q,
            cross_kv.reshape(width, 2 * own),
            cross_wo,
            dec_w1,
            dec_w2,
            embedding,
        ),
    )
    loss, grad_norm, norms, first_new, second_new, prompt_new = lamb_call(summed, first_moment, second_moment, prompt)
    return loss.reshape(()), grad_norm.reshape(()), norms, first_new, second_new, prompt_new


def solution(mesh):
    finer = Mesh(
        mesh.devices.reshape(mesh.shape["grp"], mesh.shape["seq"] // 2, 2, mesh.shape["head"]),
        ("grp", "ex", "chip", "head"),
    )
    placed = (
        P("grp", SEQ),
        P("grp"),
        P("grp", SEQ),
        P("grp", SEQ),
        P("grp", None),
        P("head", None),
        P(),
        P(),
        P(),
        P(),
        P(),
        P(),
        P(),
        P(),
        P(None, None, "head"),
        P("head", None),
        P(None, "head"),
        P(None, None, "head"),
        P("head", None),
        P(None, "head"),
        P("head", None),
    )
    return jax.shard_map(
        shards,
        mesh=finer,
        in_specs=placed,
        out_specs=(P(), P(), P(), P(), P(), P()),
        check_vma=False,
    )
```

```python
import functools

import jax
import jax.numpy as jnp
from jax import lax
from jax.experimental import pallas as pl
from jax.experimental.pallas import tpu as pltpu
from jax.sharding import Mesh
from jax.sharding import PartitionSpec as P

HD = 64
PROMPT = 100
STEP = 5
QUARTERS = 4
SEQ = ("ex", "chip")
CLUSTER = ("chip", "head")
EVERYONE = ("grp", "ex", "chip", "head")
NEG = -1000000000.0

norm_eps = 1e-06
beta_first = 0.5
beta_second = 0.5
adam_eps = 1e-12
decay_rate = 0.01
learn_rate = 0.3
clip_bound = 0.0001


MESH = pl.DeviceIdType.MESH
BF = jnp.bfloat16
F32 = jnp.float32
LEAD_PAD = 32
CHUNK = 1024
RING = 4
LANES = 128


def dot_nn(left, right):
    return lax.dot_general(left, right, (((1,), (0,)), ((), ())), preferred_element_type=F32)


def dot_nt(left, right):
    return lax.dot_general(left, right, (((1,), (1,)), ((), ())), preferred_element_type=F32)


def dot_tn(left, right):
    return lax.dot_general(left, right, (((0,), (0,)), ((), ())), preferred_element_type=F32)


def rms(value, gain):
    return value * lax.rsqrt(jnp.mean(value * value, axis=-1, keepdims=True) + norm_eps) * gain


def rms_grad(value, gain, grad):
    scale = lax.rsqrt(jnp.mean(value * value, axis=-1, keepdims=True) + norm_eps)
    scaled = grad * gain
    inner = jnp.mean(scaled * value, axis=-1, keepdims=True)
    return scale * scaled - value * (scale * scale * scale * inner)


GELU_A = 0.7978845608028654
GELU_B = 0.044715


def gelu(value):
    return 0.5 * value * (1.0 + jnp.tanh(GELU_A * (value + GELU_B * (value * value * value))))


def gelu_slope(value):
    square = value * value
    bend = jnp.tanh(GELU_A * (value + GELU_B * (square * value)))
    return 0.5 * (1.0 + bend) + 0.5 * value * (1.0 - bend * bend) * (GELU_A * (1.0 + 3.0 * GELU_B * square))


def tiles(count, size, body):
    for index in range(count):
        body(pl.ds(index * size, size))


def each(count, unroll, body):
    def step(index, carry):
        body(index)
        return carry

    if unroll == count:
        for index in range(count):
            body(index)
    else:
        lax.fori_loop(0, count, step, 0, unroll=unroll)


def lanes_at(index, size, base=0):
    if isinstance(index, int):
        return pl.ds(base + index * size, size)
    return pl.ds(pl.multiple_of(base + index * size, LANES), size)


UNROLL = {"attend": 1, "self": 1, "cross": 3, "cross_back": 3, "lead": 1, "vocab": 2}


def main_kernel(
    lengths, picked, prompt, loss_mask, gains,
    enc_qkv, enc_wo, enc_w1, enc_w2, dec_qkv, dec_wo, cross_q, cross_kv, cross_wo, dec_w1, dec_w2, embedding,
    out,
    w_qkv, w_o, w_1, w_2, w_dqkv, w_do, w_cq, w_ckv, w_co, w_d1, w_d2, ring,
    lead, enc_my, enc_in, dec_my, dec_in,
    x0, h1, h2, go, spare, n1, q_s, kv, o_f, o_b, s_f, p_b, lse_e, fade_e, scale_e, stat_e, nb, u, act,
    eo, ckv, dckv, gp_s, gp_r, gown, d_o, dkv, dkv_r, gj, dl,
    y0, a1, m_b, sqkv, so, dx_s, dx_r, cq, cp, cp_b, st_p, st_r, co_r, co, co_b,
    lg, px_s, px_r, a2, a3, du, dact, f_b, tgt, acc, acc_b, acc_r, vl_s, vl_r, gffn, gco, st_g,
    blk, s1_r, s2_r, all_r,
    load_sem, ring_sem, send_sem, recv_sem,
):
    width = x0.shape[1]
    rows = x0.shape[0]
    half = f_b.shape[0]
    own = co.shape[1]
    pairs_e, pairs_d = width // LANES, own // LANES
    head, chip = lax.axis_index("head"), lax.axis_index("chip")
    mate, across = 1 - head, 1 - chip
    me, slot_mate = 2 * chip + head, 2 * chip + mate
    slot_across, slot_diag = 2 * across + head, 2 * across + mate
    to_mate, to_across = {"head": mate}, {"chip": across}
    to_diag = {"chip": across, "head": mate}

    grp, ex = lax.axis_index("grp"), lax.axis_index("ex")
    n_grp, n_ex = lax.axis_size("grp"), lax.axis_size("ex")

    def ex_peer(step):
        return {"ex": lax.rem(ex + step, n_ex)}

    def plane_peer(step):
        place = lax.rem(grp * QUARTERS + me + step, n_grp * QUARTERS)
        member = lax.div(place, QUARTERS)
        side = lax.div(place - member * QUARTERS, 2)
        return {"grp": member, "chip": side, "head": place - member * QUARTERS - 2 * side}

    barrier = pltpu.get_barrier_semaphore()
    friends = [plane_peer(step) for step in range(1, n_grp * QUARTERS)] + [ex_peer(step) for step in range(1, n_ex)]
    for peer in friends:
        pl.semaphore_signal(barrier, inc=1, device_id=peer, device_id_type=MESH)

    def load(index, source, target):
        copy = pltpu.make_async_copy(source, target, load_sem.at[index])
        copy.start()
        return copy

    my_rows = pl.ds(pl.multiple_of(head * rows, rows), rows)
    mate_rows = pl.ds(pl.multiple_of(mate * rows, rows), rows)
    dec_rows = pl.ds(2 * rows, dec_my.shape[0])
    load_x = load(0, picked.at[my_rows], enc_my)
    load_y = load(1, picked.at[dec_rows], dec_my)
    load_qkv = load(2, enc_qkv, w_qkv)
    load_dqkv = load(3, dec_qkv, w_dqkv)
    load_do = load(4, dec_wo, w_do)
    load_cq = load(5, cross_q, w_cq)
    load_o = load(6, enc_wo, w_o)
    load_1 = load(7, enc_w1, w_1)
    load_2 = load(8, enc_w2, w_2)
    load_ckv = load(9, cross_kv, w_ckv)
    load_co = load(10, cross_wo, w_co)
    load_d1 = load(11, dec_w1, w_d1)
    load_d2 = load(12, dec_w2, w_d2)
    leads = PROMPT // QUARTERS

    vocab = embedding.shape[0]
    full = vocab // CHUNK
    tail = vocab - full * CHUNK

    def chunk_copy(index, slot):
        at = pl.ds(pl.multiple_of(index * CHUNK, CHUNK), CHUNK)
        return pltpu.make_async_copy(embedding.at[at], ring.at[slot], ring_sem.at[slot])

    def tail_copy():
        slot = full % RING
        return pltpu.make_async_copy(
            embedding.at[pl.ds(full * CHUNK, tail)], ring.at[slot, pl.ds(0, tail)], ring_sem.at[slot]
        )

    for index in range(RING):
        chunk_copy(index, index).start()

    pl.semaphore_wait(barrier, len(friends))
    sends = []
    block_sem = 17 + 3 * (width // (2 * LANES))

    def send(index, source, target, peer):
        copy = pltpu.make_async_remote_copy(
            src_ref=source,
            dst_ref=target,
            send_sem=send_sem.at[index],
            recv_sem=recv_sem.at[index],
            device_id=peer,
            device_id_type=MESH,
        )
        copy.start()
        sends.append(copy)
        return copy

    blocks = rows // 64
    got_x = []
    for block in range(blocks):
        source = picked.at[pl.ds(pl.multiple_of(mate * rows + block * 64, 64), 64)]
        got_x.append(send(block_sem + block, source, enc_in.at[pl.ds(block * 64, 64)], to_mate))
    got_y = send(1, picked.at[dec_rows], dec_in, to_mate)

    lane = lax.broadcasted_iota(jnp.int32, (1, LANES), 1)
    low_lane = lane < HD
    low_b = jnp.where(low_lane, 1.0, 0.0).astype(BF)
    high_b = jnp.where(low_lane, 0.0, 1.0).astype(BF)
    sides = (low_b, high_b)
    gain = [gains[k : k + 1, :] for k in range(7)]
    gain[6] = gain[6] * width ** (-0.5)
    length = lengths[ex]
    tokens = kv.shape[1] - leads

    def allowed(slots, span, first):
        at = lax.broadcasted_iota(jnp.int32, (1, slots * span), 1)
        slot = at // span
        inner = at - slot * span
        return (inner < leads) | (tokens * (slot + first) + inner - leads < length)

    ok = allowed(4, rows, 0)
    okc = allowed(2, rows, 2 * chip)
    okf = allowed(2, rows, 2 * across)
    okl = allowed(4, LEAD_PAD, 0)
    mask_row = loss_mask[pl.ds(ex, 1), :].astype(F32)
    lane_at = lax.broadcasted_iota(jnp.int32, (half, mask_row.shape[1]), 1)
    row_of = lax.broadcasted_iota(jnp.int32, (half, mask_row.shape[1]), 0)
    own_mask = jnp.where(lane_at == row_of + chip * half, jnp.broadcast_to(mask_row, lane_at.shape), 0.0)
    share = jnp.sum(own_mask, axis=-1, keepdims=True) / jnp.sum(mask_row, axis=-1, keepdims=True)

    load_x.wait()
    got_n, got_m = [], []
    for block in range(blocks):
        part = pl.ds(block * 64, 64)
        got_x[block].wait_recv()
        value = enc_my[part].astype(F32) + enc_in[part].astype(F32)
        if block == 0:
            spot = lax.broadcasted_iota(jnp.int32, (64, width), 0)
            for slot in range(QUARTERS):
                lead[0:leads] = jnp.where(me == slot, prompt[slot * leads : (slot + 1) * leads], lead[0:leads])
            value = jnp.where(spot < leads, lead[...], value)
        x0[part] = value
        n1[me, part] = rms(value, gain[0]).astype(BF)
        mine_n = n1.at[me, part]
        got_n.append(send(block_sem + blocks + block, mine_n, mine_n, to_across))
        got_m.append(send(block_sem + 2 * blocks + block, mine_n, mine_n, to_mate))

    load_qkv.wait()

    def query(at):
        q_s[:, at] = (dot_nn(n1[me], w_qkv[:, at]).astype(BF) * HD ** (-0.5)).astype(BF)

    tiles(width // 256, 256, query)

    load_y.wait()
    got_y.wait_recv()
    all_tgt = y0.shape[0]
    value = dec_my[0:all_tgt].astype(F32) + dec_in[0:all_tgt].astype(F32)
    y0[...] = value
    m_b[...] = rms(value, gain[3]).astype(BF)
    tgt[...] = dec_my[all_tgt : all_tgt + half].astype(F32) + dec_in[all_tgt : all_tgt + half].astype(F32)
    load_dqkv.wait()

    for part in range(3):
        sqkv[:, part * own : (part + 1) * own] = dot_nn(m_b[...], w_dqkv[part]).astype(BF)
    row_at = lax.broadcasted_iota(jnp.int32, (all_tgt, all_tgt), 0)
    col_at = lax.broadcasted_iota(jnp.int32, (all_tgt, all_tgt), 1)
    def self_pair(pair):
        q2 = sqkv[:, lanes_at(pair, LANES)]
        k2 = sqkv[:, lanes_at(pair, LANES, own)]
        v2 = sqkv[:, lanes_at(pair, LANES, 2 * own)]
        outs = []
        for side in sides:
            scores = dot_nt(q2 * side, k2) * HD ** (-0.5)
            scores = jnp.where(col_at <= row_at, scores, NEG)
            top = jnp.max(scores, axis=-1, keepdims=True)
            probs = jnp.exp(scores - top)
            total = jnp.sum(probs, axis=-1, keepdims=True)
            outs.append(dot_nn(probs.astype(BF), v2) / total)
        so[:, lanes_at(pair, LANES)] = jnp.where(low_lane, outs[0], outs[1]).astype(BF)

    each(pairs_d, UNROLL["self"], self_pair)
    load_do.wait()

    def self_out(at):
        dx_s[:, at] = dot_nn(so[...], w_do[:, at]).astype(BF)

    tiles(width // 256, 256, self_out)

    got_d = send(4, dx_s, dx_r, to_mate)
    def forward(block):
        part = n1.at[slot_across, pl.ds(block * 64, 64)]
        return pltpu.make_async_remote_copy(
            src_ref=part,
            dst_ref=part,
            send_sem=send_sem.at[block_sem + 3 * blocks + block],
            recv_sem=recv_sem.at[block_sem + 3 * blocks + block],
            device_id=to_mate,
            device_id_type=MESH,
        )

    def key_value(turn):
        slot = jnp.where(turn < 2, 2 * chip, 2 * across) + jnp.where(turn % 2 == 0, head, mate)

        @pl.when(turn == 1)
        def _():
            for copy in got_m:
                copy.wait_recv()

        @pl.when(turn == 2)
        def _():
            for block in range(blocks):
                got_n[block].wait_recv()
                forward(block).start()

        @pl.when(turn == 3)
        def _():
            for block in range(blocks):
                forward(block).wait_recv()

        for index in range(2 * width // 256):
            at = pl.ds(index * 256, 256)
            kv[slot, :, at] = dot_nn(n1[slot], w_qkv[:, pl.ds(width + index * 256, 256)]).astype(BF)

    def between():
        got_d.wait_recv()
        value = y0[...] + (dx_s[...].astype(F32) + dx_r[...].astype(F32))
        a1[...] = value
        m_b[...] = rms(value, gain[4]).astype(BF)
        load_cq.wait()
        cq[...] = (dot_nn(m_b[...], w_cq[...]).astype(BF) * HD ** (-0.5)).astype(BF)

    def key_values(first, last):
        def body(turn, carry):
            key_value(turn)
            return carry

        lax.fori_loop(first, last, body, 0)

    between()

    keys = 4 * rows

    def scores_of(pair, side, index, slots, allowed_keys):
        k2 = kv[slots, :, lanes_at(pair, LANES)].reshape(2 * rows, LANES)
        v2 = kv[slots, :, lanes_at(pair, LANES, width)].reshape(2 * rows, LANES)
        s_f[index] = dot_nt(q_s[:, lanes_at(pair, LANES)] * side, k2)
        return v2

    def near_pair(pair):
        slots = pl.ds(2 * chip, 2)
        outs = []
        for index, side in enumerate(sides):
            v2 = scores_of(pair, side, index, slots, okc)
            for block in range(rows // 32):
                part = pl.ds(block * 32, 32)
                scores = jnp.where(okc, s_f[index, part], NEG)
                top = jnp.max(scores, axis=-1, keepdims=True)
                probs = jnp.exp(scores - top)
                p_b[index, part] = probs.astype(BF)
                total = jnp.sum(probs, axis=-1, keepdims=True)
                u[part, lanes_at(index * pairs_e + pair, LANES)] = jnp.broadcast_to(total, (32, LANES))
                u[part, lanes_at(index * pairs_e + pair, LANES, 2 * width)] = jnp.broadcast_to(top, (32, LANES))
            outs.append(dot_nn(p_b[index], v2))
        o_f[:, lanes_at(pair, LANES)] = jnp.where(low_lane, outs[0], outs[1])

    def far_pair(pair):
        slots = pl.ds(2 * across, 2)
        outs = []
        for index, side in enumerate(sides):
            v2 = scores_of(pair, side, index, slots, okf)
            for block in range(rows // 32):
                part = pl.ds(block * 32, 32)
                scores = jnp.where(okf, s_f[index, part], NEG)
                near_top = u[part, lanes_at(index * pairs_e + pair, LANES, 2 * width)]
                own_top = jnp.max(scores, axis=-1, keepdims=True)
                top = jnp.maximum(jnp.broadcast_to(own_top, (32, LANES)), near_top)
                probs = jnp.exp(scores - jnp.concatenate([top] * (2 * rows // LANES), axis=1))
                fade = jnp.exp(near_top - top)
                total = jnp.broadcast_to(jnp.sum(probs, axis=-1, keepdims=True), (32, LANES))
                total = total + u[part, lanes_at(index * pairs_e + pair, LANES)] * fade
                p_b[index, part] = probs.astype(BF)
                fade_e[index, part] = fade
                scale_e[index, part] = 1.0 / total
                stat_e[index, part] = top + jnp.log(total)
            wide = dot_nn(p_b[index], v2) + o_f[:, lanes_at(pair, LANES)] * fade_e[index]
            outs.append(wide * scale_e[index])
        lse_e[pair] = jnp.where(low_lane, stat_e[0], stat_e[1])
        both = jnp.where(low_lane, outs[0], outs[1])
        o_f[:, lanes_at(pair, LANES)] = both
        o_b[:, lanes_at(pair, LANES)] = both.astype(BF)

    key_values(0, 2)
    each(pairs_e, UNROLL["attend"], near_pair)
    key_values(2, 4)
    sends.extend(forward(block) for block in range(blocks))
    each(pairs_e, UNROLL["attend"], far_pair)
    load_o.wait()

    def out_cols(at):
        h1[:, at] = x0[:, at] + dot_nn(o_b[...], w_o[:, at])

    tiles(width // 256, 256, out_cols)

    def norm_two(at):
        nb[at] = rms(h1[at], gain[1]).astype(BF)

    tiles(rows // 64, 64, norm_two)
    load_1.wait()

    def hidden(at):
        value = dot_nn(nb[...], w_1[:, at])
        u[:, at] = value
        act[:, at] = gelu(value).astype(BF)

    tiles(u.shape[1] // 256, 256, hidden)
    load_2.wait()

    def hidden_out(at):
        h2[:, at] = h1[:, at] + dot_nn(act[...], w_2[:, at])

    tiles(width // 256, 256, hidden_out)

    def norm_out(at):
        eo[head, at] = rms(h2[at], gain[2]).astype(BF)

    tiles(rows // 64, 64, norm_out)
    got_e = send(6, eo.at[head], eo.at[head], to_mate)
    load_ckv.wait()

    def cross_keys(slot):
        def body(at):
            ckv[slot, :, at] = dot_nn(eo[slot], w_ckv[:, at]).astype(BF)

        tiles(2 * own // 256, 256, body)

    cross_keys(head)
    got_e.wait_recv()
    cross_keys(mate)


    def cross_pair(pair):
        k2 = ckv[:, :, lanes_at(pair, LANES)].reshape(2 * rows, LANES)
        v2 = ckv[:, :, lanes_at(pair, LANES, own)].reshape(2 * rows, LANES)
        return cq[:, lanes_at(pair, LANES)], k2, v2

    st_p[...] = jnp.zeros_like(st_p)

    def cross_attend(pair):
        q2, k2, v2 = cross_pair(pair)
        stats = st_p[...]
        outs = []
        for index, side in enumerate(sides):
            scores = jnp.where(okc, dot_nt(q2 * side, k2), NEG)
            top = jnp.max(scores, axis=-1, keepdims=True)
            probs = jnp.exp(scores - top)
            total = jnp.sum(probs, axis=-1, keepdims=True)
            outs.append(dot_nn(probs.astype(BF), v2) / total)
            stats = jnp.where(lane == 2 * pair + index, top + jnp.log(total), stats)
        both = jnp.where(low_lane, outs[0], outs[1])
        cp[:, lanes_at(pair, LANES)] = both
        cp_b[:, lanes_at(pair, LANES)] = both.astype(BF)
        st_p[...] = stats

    each(pairs_d, UNROLL["cross"], cross_attend)
    mine_t = pl.ds(pl.multiple_of(chip * half, half), half)
    theirs_t = pl.ds(pl.multiple_of(across * half, half), half)
    got_c = send(7, cp_b.at[theirs_t], co_r, to_across)
    got_s = send(8, st_p.at[theirs_t], st_r, to_across)
    ff_tiles = u.shape[1] // 256

    def slopes(first, last):
        def some_cols(index, carry):
            at = pl.ds(pl.multiple_of(index * 256, 256), 256)
            u[:, at] = gelu_slope(u[:, at])
            return carry

        lax.fori_loop(first, last, some_cols, 0)

    slopes(0, ff_tiles // 2)
    got_c.wait_recv()
    got_s.wait_recv()
    l_own, l_oth = st_p[mine_t], st_r[...]
    top = jnp.maximum(l_own, l_oth)
    lse_c = top + jnp.log(jnp.exp(l_own - top) + jnp.exp(l_oth - top))
    w_own, w_oth = jnp.exp(l_own - lse_c), jnp.exp(l_oth - lse_c)

    def side_cols(array, pair):
        return jnp.where(
            low_lane, array[:, 2 * pair : 2 * pair + 1], array[:, 2 * pair + 1 : 2 * pair + 2]
        )

    for pair in range(pairs_d):
        lo = pair * LANES
        both = cp[mine_t, lo : lo + LANES] * side_cols(w_own, pair)
        both = both + co_r[:, lo : lo + LANES].astype(F32) * side_cols(w_oth, pair)
        co[:, lo : lo + LANES] = both
        co_b[:, lo : lo + LANES] = both.astype(BF)

    def exchange(index, value, meanwhile=None):
        slot = index - 9
        px_s[slot] = value.astype(BF)
        got = send(index, px_s.at[slot], px_r.at[slot], to_mate)
        if meanwhile is not None:
            meanwhile()
        got.wait_recv()
        return px_s[slot].astype(F32) + px_r[slot].astype(F32)

    load_co.wait()
    a2[...] = a1[mine_t] + exchange(9, dot_nn(co_b[...], w_co[...]))
    m_b[0:half] = rms(a2[...], gain[5]).astype(BF)
    load_d1.wait()

    def dec_hidden(at):
        value = dot_nn(m_b[0:half], w_d1[:, at])
        du[:, at] = value
        dact[:, at] = gelu(value).astype(BF)

    tiles(du.shape[1] // 512, 512, dec_hidden)
    load_d2.wait()

    def dec_slope():
        du[...] = gelu_slope(du[...])

    a3[...] = a2[...] + exchange(10, dot_nn(dact[...], w_d2[...]), dec_slope)
    f_b[...] = rms(a3[...], gain[6]).astype(BF)

    acc[...] = jnp.zeros_like(acc)

    def vocab_step(logits, table, top, total):
        new_top = jnp.maximum(top, jnp.max(logits, axis=-1, keepdims=True))
        fade = jnp.exp(top - new_top)
        probs = jnp.exp(logits - new_top)
        acc[...] = acc[...] * fade + dot_nn(probs.astype(BF), table)
        return new_top, total * fade + jnp.sum(probs, axis=-1, keepdims=True)

    def refill(index, slot):
        @pl.when(index + RING < full)
        def _():
            chunk_copy(index + RING, slot).start()

        if tail:

            @pl.when(index + RING == full)
            def _():
                tail_copy().start()

    span = UNROLL["vocab"]
    chunk_copy(0, 0).wait()
    lg[0] = dot_nt(f_b[...], ring[0])

    def vocab_chunks(turn, carry):
        first = span * turn
        slots = [lax.rem(first + k, RING) for k in range(span + 1)]
        for k in range(span):
            chunk_copy(first + k + 1, slots[k + 1]).wait()
            lg[(k + 1) % 2] = dot_nt(f_b[...], ring[slots[k + 1]])
            carry = vocab_step(lg[k % 2], ring[slots[k]], *carry)
            refill(first + k, slots[k])
        return carry

    carry = (jnp.full((half, 1), NEG, F32), jnp.zeros((half, 1), F32))
    turns = (full - 1) // span
    carry = lax.fori_loop(0, turns, vocab_chunks, carry)
    for index in range(span * turns, full):
        slot, after = index % RING, (index + 1) % RING
        if index + 1 < full:
            chunk_copy(index + 1, after).wait()
            lg[(index + 1) % 2] = dot_nt(f_b[...], ring[after])
        elif tail:
            tail_copy().wait()
            lg[(index + 1) % 2, :, 0:tail] = dot_nt(f_b[...], ring[after, 0:tail])
        carry = vocab_step(lg[index % 2], ring[slot], *carry)
        refill(index, slot)
    if tail:
        carry = vocab_step(lg[full % 2, :, 0:tail], ring[full % RING, 0:tail], *carry)
    top, total = carry
    acc_b[...] = (acc[...] / total).astype(BF)
    vl_s[...] = jnp.broadcast_to(top + jnp.log(total), vl_s.shape)
    got_a = send(11, acc_b, acc_r, to_mate)
    got_v = send(12, vl_s, vl_r, to_mate)
    pick = jnp.sum(f_b[...].astype(F32) * tgt[...], axis=-1, keepdims=True)
    got_a.wait_recv()
    got_v.wait_recv()
    l_own, l_oth = vl_s[:, 0:1], vl_r[:, 0:1]
    top = jnp.maximum(l_own, l_oth)
    lse_v = top + jnp.log(jnp.exp(l_own - top) + jnp.exp(l_oth - top))
    loss = jnp.sum(share * (lse_v - pick), axis=0, keepdims=True) * jnp.where(head == 0, 1.0, 0.0)
    mean_row = acc_b[...].astype(F32) * jnp.exp(l_own - lse_v) + acc_r[...].astype(F32) * jnp.exp(l_oth - lse_v)
    gffn[...] = rms_grad(a3[...], gain[6], share * (mean_row - tgt[...]))

    m_b[0:half] = gffn[...].astype(BF)

    def dec_hidden_grad(at):
        value = dot_nt(m_b[0:half], w_d2[at])
        dact[:, at] = (du[:, at] * value).astype(BF)

    tiles(du.shape[1] // 512, 512, dec_hidden_grad)
    slope = exchange(13, dot_nt(dact[...], w_d1[...]))
    gcross = gffn[...] + rms_grad(a2[...], gain[5], slope)
    gco[chip] = dot_nt(gcross.astype(BF), w_co[...]).astype(BF)
    stats = lse_c
    for pair in range(pairs_d):
        lo = pair * LANES
        value = gco[chip, :, lo : lo + LANES].astype(F32) * co[:, lo : lo + LANES]
        for index in range(2):
            picked_side = jnp.where(low_lane == (index == 0), value, 0.0)
            delta = jnp.sum(picked_side, axis=-1, keepdims=True)
            stats = jnp.where(lane == HD + 2 * pair + index, delta, stats)
    st_g[chip] = stats
    got_g = send(14, gco.at[chip], gco.at[chip], to_across)
    got_t = send(15, st_g.at[chip], st_g.at[chip], to_across)
    slopes(ff_tiles // 2, ff_tiles)
    got_g.wait_recv()
    got_t.wait_recv()

    def cross_back(pair):
        q2, k2, v2 = cross_pair(pair)
        do2 = gco[:, :, lanes_at(pair, LANES)].reshape(all_tgt, LANES)
        stats = st_g[...].reshape(all_tgt, LANES)
        dks, dvs = [], []
        for index, side in enumerate(sides):
            column = 2 * pair + index
            lse = jnp.sum(jnp.where(lane == column, stats, 0.0), axis=-1, keepdims=True)
            delta = jnp.sum(jnp.where(lane == HD + column, stats, 0.0), axis=-1, keepdims=True)
            scores = jnp.where(okc, dot_nt(q2 * side, k2), NEG)
            probs = jnp.exp(scores - lse)
            dp = dot_nt(do2 * side, v2)
            ds = (probs * (dp - delta)).astype(BF)
            dks.append(dot_tn(ds, q2))
            dvs.append(dot_tn(probs.astype(BF), do2))
        shape = (2, rows, LANES)
        dckv[:, :, lanes_at(pair, LANES)] = jnp.where(low_lane, *dks).astype(BF).reshape(shape)
        dckv[:, :, lanes_at(pair, LANES, own)] = jnp.where(low_lane, *dvs).astype(BF).reshape(shape)

    each(pairs_d, UNROLL["cross_back"], cross_back)
    def pair_grad_mate(at):
        gp_s[:, at] = dot_nt(dckv[mate], w_ckv[at]).astype(BF)

    tiles(width // 256, 256, pair_grad_mate)
    got_p = send(16, gp_s, gp_r, to_mate)

    def pair_grad_mine(at):
        gown[:, at] = dot_nt(dckv[head], w_ckv[at])

    tiles(width // 256, 256, pair_grad_mine)
    got_p.wait_recv()

    def out_grad(at):
        value = rms_grad(h2[at], gain[2], gown[at].astype(BF).astype(F32) + gp_r[at].astype(F32))
        go[at] = value
        nb[at] = value.astype(BF)

    tiles(rows // 64, 64, out_grad)

    def hidden_grad(at):
        act[:, at] = (u[:, at] * dot_nt(nb[...], w_2[at])).astype(BF)

    tiles(u.shape[1] // 256, 256, hidden_grad)

    def norm_two_grad(at):
        spare[:, at] = dot_nt(act[...], w_1[at])

    tiles(width // 256, 256, norm_two_grad)

    def one_grad(at):
        value = go[at] + rms_grad(h1[at], gain[1], spare[at])
        go[at] = value
        nb[at] = value.astype(BF)

    tiles(rows // 64, 64, one_grad)

    def attn_grad(at):
        d_o[:, at] = dot_nt(nb[...], w_o[at]).astype(BF)

    tiles(width // 256, 256, attn_grad)

    lead_keys = 4 * LEAD_PAD

    quad = 2 * LANES
    heads_in = quad // HD
    quad_lane = lax.broadcasted_iota(jnp.int32, (1, quad), 1)
    quad_of = [(quad_lane >= k * HD) & (quad_lane < (k + 1) * HD) for k in range(heads_in)]
    quad_b = [jnp.where(inside, 1.0, 0.0).astype(BF) for inside in quad_of]

    def lead_pair(group, part):
        pair = 2 * group + part
        at = lanes_at(pair, LANES)
        q2, do2 = q_s[:, at], d_o[:, at]
        k2 = kv[:, 0:LEAD_PAD, at].reshape(lead_keys, LANES)
        v2 = kv[:, 0:LEAD_PAD, lanes_at(pair, LANES, width)].reshape(lead_keys, LANES)
        value = do2.astype(F32) * o_f[:, at]
        dks, dvs, deltas = [], [], []
        for index, side in enumerate(sides):
            delta = jnp.sum(jnp.where(low_lane == (index == 0), value, 0.0), axis=-1, keepdims=True)
            deltas.append(delta)
            lse = lse_e[pair, :, index * HD : index * HD + 1]
            scores = jnp.where(okl, dot_nt(q2 * side, k2), NEG)
            probs = jnp.exp(scores - lse)
            ds = (probs * (dot_nt(do2 * side, v2) - delta)).astype(BF)
            dks.append(dot_tn(ds, q2))
            dvs.append(dot_tn(probs.astype(BF), do2))
        lo = part * LANES
        shape = (4, LEAD_PAD, LANES)
        dkv[group, :, :, lo : lo + LANES] = jnp.where(low_lane, *dks).astype(BF).reshape(shape)
        dkv[group, :, :, quad + lo : quad + lo + LANES] = jnp.where(low_lane, *dvs).astype(BF).reshape(shape)
        dl[pair] = jnp.where(low_lane, *[d[0:LEAD_PAD] for d in deltas])

    def stack(value):
        return jnp.concatenate([value * side for side in quad_b], axis=0)

    def column(ref, group, rows_at):
        return jnp.concatenate(
            [ref[2 * group + k // 2, rows_at, (k % 2) * HD : (k % 2) * HD + 1] for k in range(heads_in)], axis=0
        )

    def query_quad(group):
        at, vat = lanes_at(group, quad), lanes_at(group, quad, width)
        lead_rows = slice(0, LEAD_PAD)
        k4 = kv[:, :, at].reshape(keys, quad)
        v4 = kv[:, :, vat].reshape(keys, quad)
        scores = jnp.where(ok, dot_nt(stack(q_s[lead_rows, at]), k4), NEG)
        probs = jnp.exp(scores - column(lse_e, group, lead_rows))
        ds = (probs * (dot_nt(stack(d_o[lead_rows, at]), v4) - column(dl, group, lead_rows))).astype(BF)
        wide = dot_nn(ds, k4)
        value = jnp.zeros((LEAD_PAD, quad), F32)
        for k in range(heads_in):
            value = jnp.where(quad_of[k], wide[k * LEAD_PAD : (k + 1) * LEAD_PAD], value)
        gj[:, at] = (value * HD ** (-0.5)).astype(BF)

    def key_copies(group):
        plan = ((slot_across, 1, to_across), (slot_diag, 2, to_diag), (slot_mate, 0, to_mate))
        copies = []
        for k, (slot, place, peer) in enumerate(plan):
            copies.append(
                pltpu.make_async_remote_copy(
                    src_ref=dkv.at[group, slot],
                    dst_ref=dkv_r.at[group, place],
                    send_sem=send_sem.at[17 + 3 * group + k],
                    recv_sem=recv_sem.at[17 + 3 * group + k],
                    device_id=peer,
                    device_id_type=MESH,
                )
            )
        return copies

    def lead_group(group):
        lead_pair(group, 0)
        lead_pair(group, 1)
        for copy in key_copies(group):
            copy.start()

    each(width // quad, UNROLL["lead"], lead_group)
    each(width // quad, UNROLL["lead"], query_quad)
    for group in range(width // quad):
        summed = dkv[group, me].astype(F32)
        copies = key_copies(group)
        for index in range(3):
            copies[(2, 0, 1)[index]].wait_recv()
            summed = summed + dkv_r[group, index].astype(F32)
        sends.extend(copies)
        lo = group * quad
        gj[:, width + lo : width + lo + quad] = summed[:, :quad].astype(BF)
        gj[:, 2 * width + lo : 2 * width + lo + quad] = summed[:, quad:].astype(BF)

    def start_grad(at):
        spare[0:LEAD_PAD, at] = dot_nt(gj[...], w_qkv[at])

    tiles(width // 256, 256, start_grad)
    top_rows = slice(0, LEAD_PAD)
    value = go[top_rows] + rms_grad(x0[top_rows], gain[0], spare[top_rows])
    spot = lax.broadcasted_iota(jnp.int32, (LEAD_PAD, width), 0)
    extra = jnp.where(spot == leads, loss, 0.0)
    blk[...] = jnp.where(spot < leads, value, extra)

    piece = LEAD_PAD // n_grp
    slot = block_sem + 4 * blocks
    got = []
    for step in range(n_grp):
        member = lax.rem(grp + step, n_grp)
        rows_at = pl.ds(pl.multiple_of(member * piece, piece), piece)
        if step:
            got.append(send(slot, blk.at[rows_at], s1_r.at[step], {"grp": member}))
            slot += 1
    value = blk[pl.ds(pl.multiple_of(grp * piece, piece), piece)]
    for step in range(1, n_grp):
        got[step - 1].wait_recv()
        value = value + s1_r[step]
    s2_r[ex] = value
    got = []
    for step in range(1, n_ex):
        got.append(send(slot, s2_r.at[ex], s2_r.at[ex], ex_peer(step)))
        slot += 1
    for copy in got:
        copy.wait_recv()
    value = s2_r[0]
    for member in range(1, n_ex):
        value = value + s2_r[member]
    all_r[me, grp] = value
    got = []
    for step in range(1, n_grp * QUARTERS):
        got.append(send(slot, all_r.at[me, grp], all_r.at[me, grp], plane_peer(step)))
        slot += 1
    for copy in got:
        copy.wait_recv()
    out[...] = all_r[...].reshape(out.shape)
    for copy in sends:
        copy.wait_send()


def main_call(lengths, vmem, hbm):
    half = vmem[1].shape[1] // 2
    rows = (hbm[0].shape[0] - 3 * half) // 2
    wq, wo, w1, w2, dqkv, dwo, cqw, ckvw, cwo, dw1, dw2, emb = hbm[1:]
    width, own, ff, dff, tgt_all = wo.shape[0], dwo.shape[0], w1.shape[1], dw1.shape[1], 2 * half
    pairs_e = width // LANES

    def v(shape, kind=F32):
        return pltpu.VMEM(shape, kind)

    scratch = [v(w.shape, BF) for w in hbm[1:12]]
    scratch += [v((RING, CHUNK, width), BF)]
    scratch += [v((64, width))]
    scratch += [v((rows, width), BF), v((rows, width), BF), v((tgt_all + half, width), BF), v((tgt_all + half, width), BF)]
    scratch += [v((rows, width)) for _ in range(5)]
    scratch += [v((4, rows, width), BF), v((rows, width), BF), v((4, rows, 2 * width), BF)]
    scratch += [v((rows, width)), v((rows, width), BF), v((2, rows, 2 * rows)), v((2, rows, 2 * rows), BF)]
    scratch += [v((pairs_e, rows, LANES))]
    scratch += [v((2, rows, LANES)), v((2, rows, LANES)), v((2, rows, LANES)), v((rows, width), BF)]
    scratch += [v((rows, ff)), v((rows, ff), BF)]
    scratch += [v((2, rows, width), BF), v((2, rows, 2 * own), BF), v((2, rows, 2 * own), BF)]
    scratch += [v((rows, width), BF), v((rows, width), BF), v((rows, width)), v((rows, width), BF)]
    groups = width // (2 * LANES)
    scratch += [v((groups, 4, LEAD_PAD, 4 * LANES), BF), v((groups, 3, LEAD_PAD, 4 * LANES), BF), v((LEAD_PAD, 3 * width), BF)]
    scratch += [v((pairs_e, LEAD_PAD, LANES))]
    scratch += [v((tgt_all, width)), v((tgt_all, width)), v((tgt_all, width), BF), v((tgt_all, 3 * own), BF)]
    scratch += [v((tgt_all, own), BF), v((tgt_all, width), BF), v((tgt_all, width), BF), v((tgt_all, own), BF)]
    scratch += [v((tgt_all, own)), v((tgt_all, own), BF), v((tgt_all, LANES)), v((half, LANES))]
    scratch += [v((half, own), BF), v((half, own)), v((half, own), BF)]
    scratch += [v((2, half, CHUNK))]
    scratch += [v((5, half, width), BF), v((5, half, width), BF)]
    scratch += [v((half, width)), v((half, width)), v((half, dff)), v((half, dff), BF), v((half, width), BF)]
    scratch += [v((half, width)), v((half, width)), v((half, width), BF), v((half, width), BF)]
    scratch += [v((half, LANES)), v((half, LANES)), v((half, width)), v((2, half, own), BF), v((2, half, LANES))]
    n_grp, n_ex = lax.axis_size("grp"), lax.axis_size("ex")
    piece = LEAD_PAD // n_grp
    scratch += [v((LEAD_PAD, width)), v((n_grp, piece, width)), v((n_ex, piece, width))]
    scratch += [v((QUARTERS, n_grp, piece, width))]
    exchanges = 17 + 3 * groups + 4 * (rows // 64) + (n_grp - 1) + (n_ex - 1) + (n_grp * QUARTERS - 1)
    scratch += [
        pltpu.SemaphoreType.DMA((13,)),
        pltpu.SemaphoreType.DMA((RING,)),
        pltpu.SemaphoreType.DMA((exchanges,)),
        pltpu.SemaphoreType.DMA((exchanges,)),
    ]
    any_spec, vmem_spec = pl.BlockSpec(memory_space=pl.ANY), pl.BlockSpec(memory_space=pltpu.VMEM)
    return pl.pallas_call(
        main_kernel,
        out_shape=jax.ShapeDtypeStruct((QUARTERS, LEAD_PAD, width), F32),
        in_specs=[pl.BlockSpec(memory_space=pltpu.SMEM), any_spec] + [vmem_spec] * len(vmem) + [any_spec] * len(hbm[1:]),
        out_specs=vmem_spec,
        scratch_shapes=scratch,
        compiler_params=pltpu.CompilerParams(
            collective_id=1, has_side_effects=True, vmem_limit_bytes=62 * 1024 * 1024
        ),
        name="step_of_one_example",
    )(lengths, hbm[0], *vmem, *hbm[1:])


def log2(size):
    return size.bit_length() - 1


def ids_kernel(enc_ids, dec_ids, target_ids, out, lines, got, unused, send_sem, recv_sem):
    ex, chip = lax.axis_index("ex"), lax.axis_index("chip")
    chips = lax.axis_size("chip")
    seqs = lax.axis_size(SEQ)
    me = ex * chips + chip
    enc_dev, tgt_dev = enc_ids.shape[1], dec_ids.shape[1]


    def peer_of(step):
        peer = lax.rem(me + step, seqs)
        row = lax.div(peer, chips)
        return row, {"ex": row, "chip": peer - row * chips}

    barrier = pltpu.get_barrier_semaphore()
    for step in range(1, seqs):
        pl.semaphore_signal(barrier, inc=1, device_id=peer_of(step)[1], device_id_type=MESH)
    lines[:, 0:enc_dev] = enc_ids[...]
    lines[:, enc_dev : enc_dev + tgt_dev] = dec_ids[...]
    lines[:, enc_dev + tgt_dev : enc_dev + 2 * tgt_dev] = target_ids[...]
    lines[:, enc_dev + 2 * tgt_dev :] = jnp.zeros((lines.shape[0], lines.shape[1] - enc_dev - 2 * tgt_dev), jnp.int32)
    pl.semaphore_wait(barrier, seqs - 1)

    for step in range(1, seqs):
        row, peer = peer_of(step)
        pltpu.make_async_remote_copy(
            src_ref=lines.at[pl.ds(row, 1)],
            dst_ref=got.at[pl.ds(me, 1)],
            send_sem=send_sem,
            recv_sem=recv_sem,
            device_id=peer,
            device_id_type=MESH,
        ).start()
    own_line = lines.at[pl.ds(ex, 1)]
    pltpu.make_async_copy(own_line, got.at[pl.ds(me, 1)], recv_sem).start()
    pltpu.make_async_copy(own_line, unused.at[pl.ds(0, 1)], send_sem).start()
    pltpu.make_async_copy(got, got, recv_sem).wait()
    pltpu.make_async_copy(got, got, send_sem).wait()
    out[...] = got[...]


def ids_call(enc_ids, dec_ids, target_ids):
    seqs = lax.axis_size(SEQ)
    lanes = -(-(enc_ids.shape[1] + 2 * dec_ids.shape[1]) // LANES) * LANES
    return pl.pallas_call(
        ids_kernel,
        out_shape=jax.ShapeDtypeStruct((seqs, lanes), jnp.int32),
        in_specs=[pl.BlockSpec(memory_space=pltpu.VMEM)] * 3,
        out_specs=pl.BlockSpec(memory_space=pltpu.VMEM),
        scratch_shapes=[
            pltpu.VMEM((enc_ids.shape[0], lanes), jnp.int32),
            pltpu.VMEM((seqs, lanes), jnp.int32),
            pltpu.VMEM((8, lanes), jnp.int32),
            pltpu.SemaphoreType.DMA,
            pltpu.SemaphoreType.DMA,
        ],
        compiler_params=pltpu.CompilerParams(collective_id=2, has_side_effects=True),
        name="ids_of_one_example",
    )(enc_ids, dec_ids, target_ids)


GROUP = 16


AHEAD = 8


def lookup_kernel(rows, tokens, lead, enc_dev, tgt_dev, ids, table, out, blocks, spots, sems):
    chip, head = lax.axis_index("chip"), lax.axis_index("head")
    vocab_part = table.shape[0]
    enc_count = 2 * rows
    tgt_all = tgt_dev * ids.shape[0]
    half = tgt_all // 2
    groups = out.shape[0] // GROUP
    first, second = enc_count // GROUP, (enc_count + tgt_all) // GROUP

    def fetch(group):
        enc = group < first
        slot = (group * GROUP) >> log2(rows)
        enc_base = (PROMPT - lead) + tokens * (2 * chip + slot) + ((group * GROUP) & (rows - 1))
        dec_base = (group - jnp.where(group < second, first, second)) * GROUP
        dec_base = dec_base + jnp.where(group < second, 0, chip * half)
        base = jnp.where(enc, enc_base, dec_base)
        shift = jnp.where(enc, log2(enc_dev), log2(tgt_dev))
        mask = jnp.where(enc, enc_dev - 1, tgt_dev - 1)
        lane = jnp.where(enc, 0, jnp.where(group < second, enc_dev, enc_dev + tgt_dev))
        for k in range(GROUP):
            token = ids[(base + k) >> shift, lane + ((base + k) & mask)]
            upper = jnp.where(token >= vocab_part, 1, 0)
            local = token - upper * vocab_part
            spots[group * GROUP + k] = k * GROUP + (local & (GROUP - 1)) + ((upper + head - 2 * upper * head) * 4096)
            at = pl.multiple_of((local >> log2(GROUP)) << log2(GROUP), GROUP)
            pltpu.make_async_copy(
                table.at[pl.ds(at, GROUP)], blocks.at[group * GROUP + k], sems.at[group]
            ).start()

    across = lax.broadcasted_iota(jnp.int32, (8, LANES), 1)
    down = lax.broadcasted_iota(jnp.int32, (8, LANES), 0)

    def select(group):
        at = pl.ds(pl.multiple_of(group * GROUP, GROUP), GROUP)
        pltpu.make_async_copy(blocks.at[at], blocks.at[at], sems.at[group]).wait()
        chosen = []
        for part in range(GROUP // 8):
            want = jnp.full((8, LANES), -1, jnp.int32)
            for k in range(8):
                want = jnp.where(down == k, spots[group * GROUP + part * 8 + k], want)
            hits = [jnp.where(across + base == want, 1.0, 0.0) for base in range(0, GROUP * GROUP, LANES)]
            chosen.append(jnp.concatenate(hits, axis=1))
        chosen = jnp.concatenate(chosen, axis=0).astype(BF)
        out[at] = dot_nn(chosen, blocks[at].reshape(GROUP * GROUP, out.shape[1])).astype(BF)

    def loop(start, stop, *steps):
        def body(group, carry):
            for step in steps:
                step(group)
            return carry

        lax.fori_loop(start, stop, body, 0, unroll=2 if len(steps) > 1 and (stop - start) % 2 == 0 else 1)

    skip = lead // GROUP
    per_slot = rows // GROUP - skip
    needed = groups - 2 * skip

    def real(index):
        return index + skip + jnp.where(index >= per_slot, skip, 0)

    loop(0, AHEAD, lambda index: fetch(real(index)))
    loop(AHEAD, needed, lambda index: fetch(real(index)), lambda index: select(real(index - AHEAD)))
    loop(needed - AHEAD, needed, lambda index: select(real(index)))


def lookup_call(ids, table, rows, tokens, lead, enc_dev, tgt_dev):
    count = 2 * rows + tgt_dev * ids.shape[0] * 3 // 2
    width = table.shape[1]
    return pl.pallas_call(
        functools.partial(lookup_kernel, rows, tokens, lead, enc_dev, tgt_dev),
        out_shape=jax.ShapeDtypeStruct((count, width), BF),
        in_specs=[pl.BlockSpec(memory_space=pltpu.SMEM), pl.BlockSpec(memory_space=pl.ANY)],
        out_specs=pl.BlockSpec(memory_space=pltpu.VMEM),
        scratch_shapes=[
            pltpu.VMEM((count, GROUP, width), BF),
            pltpu.SMEM((count,), jnp.int32),
            pltpu.SemaphoreType.DMA((count // GROUP,)),
        ],
        compiler_params=pltpu.CompilerParams(vmem_limit_bytes=32 * 1024 * 1024),
        name="embedding_rows",
    )(ids, table)


def lamb_kernel(summed, first_old, second_old, prompt, loss, grad_norm, norms, first_new, second_new, prompt_new, work):
    lead = PROMPT // QUARTERS
    for quarter in range(QUARTERS):
        work[quarter * lead : (quarter + 1) * lead] = summed[quarter, 0:lead]
    grad = work[...]
    total = summed[0, lead : lead + 1, 0:1]
    for quarter in range(1, QUARTERS):
        total = total + summed[quarter, lead : lead + 1, 0:1]
    loss[0] = jnp.sum(total)
    norm = jnp.sqrt(jnp.sum(grad * grad))
    grad_norm[0] = norm
    clipped = grad * (clip_bound / jnp.maximum(norm, clip_bound))
    first_next = beta_first * first_old[...] + (1.0 - beta_first) * clipped
    second_next = beta_second * second_old[...] + (1.0 - beta_second) * clipped * clipped
    first_new[...] = first_next
    second_new[...] = second_next
    scaled_first = first_next / (1.0 - beta_first**STEP)
    scaled_second = second_next / (1.0 - beta_second**STEP)
    param = prompt[...]
    update = scaled_first / (jnp.sqrt(scaled_second) + adam_eps) + decay_rate * param
    param_norm = jnp.sqrt(jnp.sum(param * param))
    update_norm = jnp.sqrt(jnp.sum(update * update))
    norms[0] = param_norm
    norms[1] = update_norm
    prompt_new[...] = param - learn_rate * (param_norm / update_norm) * update


def lamb_call(summed, first_old, second_old, prompt):
    smem, vmem = pl.BlockSpec(memory_space=pltpu.SMEM), pl.BlockSpec(memory_space=pltpu.VMEM)
    like = jax.ShapeDtypeStruct(prompt.shape, F32)
    return pl.pallas_call(
        lamb_kernel,
        out_shape=(
            jax.ShapeDtypeStruct((1,), F32),
            jax.ShapeDtypeStruct((1,), F32),
            jax.ShapeDtypeStruct((2,), F32),
            like,
            like,
            like,
        ),
        in_specs=[vmem] * 4,
        out_specs=(smem, smem, smem, vmem, vmem, vmem),
        scratch_shapes=[pltpu.VMEM(prompt.shape, F32)],
        name="lamb",
    )(summed, first_old, second_old, prompt)


def shards(
    enc_ids,
    lengths,
    dec_ids,
    target_ids,
    loss_mask,
    embedding,
    prompt,
    first_moment,
    second_moment,
    gains,
    enc_qkv,
    enc_wo,
    enc_w1,
    enc_w2,
    dec_qkv,
    dec_wo,
    cross_q,
    cross_kv,
    cross_wo,
    dec_w1,
    dec_w2,
):
    width = embedding.shape[1]
    own = dec_wo.shape[0]
    enc_dev, tgt_dev = enc_ids.shape[1], dec_ids.shape[1]
    total_len = enc_dev * lax.axis_size(SEQ)
    lead = PROMPT // QUARTERS
    tokens = (total_len - PROMPT) // QUARTERS
    rows = total_len // QUARTERS
    ids = ids_call(enc_ids, dec_ids, target_ids)
    picked = lookup_call(ids, embedding, rows, tokens, lead, enc_dev, tgt_dev)
    summed = main_call(
        lengths,
        (prompt, loss_mask, gains),
        (
            picked,
            enc_qkv,
            enc_wo,
            enc_w1,
            enc_w2,
            jnp.transpose(dec_qkv, (1, 0, 2)),
            dec_wo,
            cross_q,
            cross_kv.reshape(width, 2 * own),
            cross_wo,
            dec_w1,
            dec_w2,
            embedding,
        ),
    )
    loss, grad_norm, norms, first_new, second_new, prompt_new = lamb_call(summed, first_moment, second_moment, prompt)
    return loss.reshape(()), grad_norm.reshape(()), norms, first_new, second_new, prompt_new


def solution(mesh):
    finer = Mesh(
        mesh.devices.reshape(mesh.shape["grp"], mesh.shape["seq"] // 2, 2, mesh.shape["head"]),
        ("grp", "ex", "chip", "head"),
    )
    placed = (
        P("grp", SEQ),
        P("grp"),
        P("grp", SEQ),
        P("grp", SEQ),
        P("grp", None),
        P("head", None),
        P(),
        P(),
        P(),
        P(),
        P(),
        P(),
        P(),
        P(),
        P(None, None, "head"),
        P("head", None),
        P(None, "head"),
        P(None, None, "head"),
        P("head", None),
        P(None, "head"),
        P("head", None),
    )
    return jax.shard_map(
        shards,
        mesh=finer,
        in_specs=placed,
        out_specs=(P(), P(), P(), P(), P(), P()),
        check_vma=False,
    )
```

```python
import functools

import jax
import jax.numpy as jnp
from jax import lax
from jax.experimental import pallas as pl
from jax.experimental.pallas import tpu as pltpu
from jax.sharding import Mesh
from jax.sharding import PartitionSpec as P

HD = 64
PROMPT = 100
STEP = 5
QUARTERS = 4
SEQ = ("ex", "chip")
CLUSTER = ("chip", "head")
EVERYONE = ("grp", "ex", "chip", "head")
NEG = -1000000000.0

norm_eps = 1e-06
beta_first = 0.5
beta_second = 0.5
adam_eps = 1e-12
decay_rate = 0.01
learn_rate = 0.3
clip_bound = 0.0001


MESH = pl.DeviceIdType.MESH
BF = jnp.bfloat16
F32 = jnp.float32
LEAD_PAD = 32
CHUNK = 1024
RING = 4
LANES = 128


def dot_nn(left, right):
    return lax.dot_general(left, right, (((1,), (0,)), ((), ())), preferred_element_type=F32)


def dot_nt(left, right):
    return lax.dot_general(left, right, (((1,), (1,)), ((), ())), preferred_element_type=F32)


def dot_tn(left, right):
    return lax.dot_general(left, right, (((0,), (0,)), ((), ())), preferred_element_type=F32)


def rms(value, gain):
    return value * lax.rsqrt(jnp.mean(value * value, axis=-1, keepdims=True) + norm_eps) * gain


def rms_grad(value, gain, grad):
    scale = lax.rsqrt(jnp.mean(value * value, axis=-1, keepdims=True) + norm_eps)
    scaled = grad * gain
    inner = jnp.mean(scaled * value, axis=-1, keepdims=True)
    return scale * scaled - value * (scale * scale * scale * inner)


GELU_A = 0.7978845608028654
GELU_B = 0.044715


def gelu(value):
    return 0.5 * value * (1.0 + jnp.tanh(GELU_A * (value + GELU_B * (value * value * value))))


def gelu_slope(value):
    square = value * value
    bend = jnp.tanh(GELU_A * (value + GELU_B * (square * value)))
    return 0.5 * (1.0 + bend) + 0.5 * value * (1.0 - bend * bend) * (GELU_A * (1.0 + 3.0 * GELU_B * square))


def tiles(count, size, body):
    for index in range(count):
        body(pl.ds(index * size, size))


def each(count, unroll, body):
    def step(index, carry):
        body(index)
        return carry

    if unroll == count:
        for index in range(count):
            body(index)
    else:
        lax.fori_loop(0, count, step, 0, unroll=unroll)


def lanes_at(index, size, base=0):
    if isinstance(index, int):
        return pl.ds(base + index * size, size)
    return pl.ds(pl.multiple_of(base + index * size, LANES), size)


UNROLL = {"attend": 2, "self": 1, "cross": 3, "cross_back": 3, "lead": 1, "vocab": 2}


def main_kernel(
    lengths, picked, prompt, loss_mask, gains,
    enc_qkv, enc_wo, enc_w1, enc_w2, dec_qkv, dec_wo, cross_q, cross_kv, cross_wo, dec_w1, dec_w2, embedding,
    out,
    w_qkv, w_o, w_1, w_2, w_dqkv, w_do, w_cq, w_ckv, w_co, w_d1, w_d2, ring,
    lead, enc_my, enc_in, dec_my, dec_in,
    x0, h1, h2, go, spare, n1, q_s, kv, o_f, o_b, s_f, p_b, lse_e, fade_e, scale_e, stat_e, nb, u, act,
    eo, ckv, dckv, gp_s, gp_r, gown, d_o, dkv, dkv_r, gj, dl,
    y0, a1, m_b, sqkv, so, dx_s, dx_r, cq, cp, cp_b, st_p, st_r, co_r, co, co_b,
    lg, px_s, px_r, a2, a3, du, dact, f_b, tgt, acc, acc_b, acc_r, vl_s, vl_r, gffn, gco, st_g,
    blk, s1_r, s2_r, all_r,
    load_sem, ring_sem, send_sem, recv_sem,
):
    width = x0.shape[1]
    rows = x0.shape[0]
    half = f_b.shape[0]
    own = co.shape[1]
    pairs_e, pairs_d = width // LANES, own // LANES
    head, chip = lax.axis_index("head"), lax.axis_index("chip")
    mate, across = 1 - head, 1 - chip
    me, slot_mate = 2 * chip + head, 2 * chip + mate
    slot_across, slot_diag = 2 * across + head, 2 * across + mate
    to_mate, to_across = {"head": mate}, {"chip": across}
    to_diag = {"chip": across, "head": mate}

    grp, ex = lax.axis_index("grp"), lax.axis_index("ex")
    n_grp, n_ex = lax.axis_size("grp"), lax.axis_size("ex")

    def ex_peer(step):
        return {"ex": lax.rem(ex + step, n_ex)}

    def plane_peer(step):
        place = lax.rem(grp * QUARTERS + me + step, n_grp * QUARTERS)
        member = lax.div(place, QUARTERS)
        side = lax.div(place - member * QUARTERS, 2)
        return {"grp": member, "chip": side, "head": place - member * QUARTERS - 2 * side}

    barrier = pltpu.get_barrier_semaphore()
    friends = [plane_peer(step) for step in range(1, n_grp * QUARTERS)] + [ex_peer(step) for step in range(1, n_ex)]
    for peer in friends:
        pl.semaphore_signal(barrier, inc=1, device_id=peer, device_id_type=MESH)

    def load(index, source, target):
        copy = pltpu.make_async_copy(source, target, load_sem.at[index])
        copy.start()
        return copy

    my_rows = pl.ds(pl.multiple_of(head * rows, rows), rows)
    mate_rows = pl.ds(pl.multiple_of(mate * rows, rows), rows)
    dec_rows = pl.ds(2 * rows, dec_my.shape[0])
    load_x = load(0, picked.at[my_rows], enc_my)
    load_y = load(1, picked.at[dec_rows], dec_my)
    load_qkv = load(2, enc_qkv, w_qkv)
    load_dqkv = load(3, dec_qkv, w_dqkv)
    load_do = load(4, dec_wo, w_do)
    load_cq = load(5, cross_q, w_cq)
    load_o = load(6, enc_wo, w_o)
    load_1 = load(7, enc_w1, w_1)
    load_2 = load(8, enc_w2, w_2)
    load_ckv = load(9, cross_kv, w_ckv)
    load_co = load(10, cross_wo, w_co)
    load_d1 = load(11, dec_w1, w_d1)
    load_d2 = load(12, dec_w2, w_d2)
    leads = PROMPT // QUARTERS

    vocab = embedding.shape[0]
    full = vocab // CHUNK
    tail = vocab - full * CHUNK

    def chunk_copy(index, slot):
        at = pl.ds(pl.multiple_of(index * CHUNK, CHUNK), CHUNK)
        return pltpu.make_async_copy(embedding.at[at], ring.at[slot], ring_sem.at[slot])

    def tail_copy():
        slot = full % RING
        return pltpu.make_async_copy(
            embedding.at[pl.ds(full * CHUNK, tail)], ring.at[slot, pl.ds(0, tail)], ring_sem.at[slot]
        )

    for index in range(RING):
        chunk_copy(index, index).start()

    pl.semaphore_wait(barrier, len(friends))
    sends = []
    block_sem = 17 + 3 * (width // (2 * LANES))

    def send(index, source, target, peer):
        copy = pltpu.make_async_remote_copy(
            src_ref=source,
            dst_ref=target,
            send_sem=send_sem.at[index],
            recv_sem=recv_sem.at[index],
            device_id=peer,
            device_id_type=MESH,
        )
        copy.start()
        sends.append(copy)
        return copy

    blocks = rows // 64
    got_x = []
    for block in range(blocks):
        source = picked.at[pl.ds(pl.multiple_of(mate * rows + block * 64, 64), 64)]
        got_x.append(send(block_sem + block, source, enc_in.at[pl.ds(block * 64, 64)], to_mate))
    got_y = send(1, picked.at[dec_rows], dec_in, to_mate)

    lane = lax.broadcasted_iota(jnp.int32, (1, LANES), 1)
    low_lane = lane < HD
    low_b = jnp.where(low_lane, 1.0, 0.0).astype(BF)
    high_b = jnp.where(low_lane, 0.0, 1.0).astype(BF)
    sides = (low_b, high_b)
    gain = [gains[k : k + 1, :] for k in range(7)]
    gain[6] = gain[6] * width ** (-0.5)
    length = lengths[ex]
    tokens = kv.shape[1] - leads

    def allowed(slots, span, first):
        at = lax.broadcasted_iota(jnp.int32, (1, slots * span), 1)
        slot = at // span
        inner = at - slot * span
        return (inner < leads) | (tokens * (slot + first) + inner - leads < length)

    ok = allowed(4, rows, 0)
    okc = allowed(2, rows, 2 * chip)
    okf = allowed(2, rows, 2 * across)
    okl = allowed(4, LEAD_PAD, 0)
    mask_row = loss_mask[pl.ds(ex, 1), :].astype(F32)
    lane_at = lax.broadcasted_iota(jnp.int32, (half, mask_row.shape[1]), 1)
    row_of = lax.broadcasted_iota(jnp.int32, (half, mask_row.shape[1]), 0)
    own_mask = jnp.where(lane_at == row_of + chip * half, jnp.broadcast_to(mask_row, lane_at.shape), 0.0)
    share = jnp.sum(own_mask, axis=-1, keepdims=True) / jnp.sum(mask_row, axis=-1, keepdims=True)

    load_x.wait()
    got_n, got_m = [], []
    for block in range(blocks):
        part = pl.ds(block * 64, 64)
        got_x[block].wait_recv()
        value = enc_my[part].astype(F32) + enc_in[part].astype(F32)
        if block == 0:
            spot = lax.broadcasted_iota(jnp.int32, (64, width), 0)
            for slot in range(QUARTERS):
                lead[0:leads] = jnp.where(me == slot, prompt[slot * leads : (slot + 1) * leads], lead[0:leads])
            value = jnp.where(spot < leads, lead[...], value)
        x0[part] = value
        n1[me, part] = rms(value, gain[0]).astype(BF)
        mine_n = n1.at[me, part]
        got_n.append(send(block_sem + blocks + block, mine_n, mine_n, to_across))
        got_m.append(send(block_sem + 2 * blocks + block, mine_n, mine_n, to_mate))

    load_qkv.wait()

    def query(at):
        q_s[:, at] = (dot_nn(n1[me], w_qkv[:, at]).astype(BF) * HD ** (-0.5)).astype(BF)

    tiles(width // 256, 256, query)

    load_y.wait()
    got_y.wait_recv()
    all_tgt = y0.shape[0]
    value = dec_my[0:all_tgt].astype(F32) + dec_in[0:all_tgt].astype(F32)
    y0[...] = value
    m_b[...] = rms(value, gain[3]).astype(BF)
    tgt[...] = dec_my[all_tgt : all_tgt + half].astype(F32) + dec_in[all_tgt : all_tgt + half].astype(F32)
    load_dqkv.wait()

    for part in range(3):
        sqkv[:, part * own : (part + 1) * own] = dot_nn(m_b[...], w_dqkv[part]).astype(BF)
    row_at = lax.broadcasted_iota(jnp.int32, (all_tgt, all_tgt), 0)
    col_at = lax.broadcasted_iota(jnp.int32, (all_tgt, all_tgt), 1)
    def self_pair(pair):
        q2 = sqkv[:, lanes_at(pair, LANES)]
        k2 = sqkv[:, lanes_at(pair, LANES, own)]
        v2 = sqkv[:, lanes_at(pair, LANES, 2 * own)]
        outs = []
        for side in sides:
            scores = dot_nt(q2 * side, k2) * HD ** (-0.5)
            scores = jnp.where(col_at <= row_at, scores, NEG)
            top = jnp.max(scores, axis=-1, keepdims=True)
            probs = jnp.exp(scores - top)
            total = jnp.sum(probs, axis=-1, keepdims=True)
            outs.append(dot_nn(probs.astype(BF), v2) / total)
        so[:, lanes_at(pair, LANES)] = jnp.where(low_lane, outs[0], outs[1]).astype(BF)

    each(pairs_d, UNROLL["self"], self_pair)
    load_do.wait()

    def self_out(at):
        dx_s[:, at] = dot_nn(so[...], w_do[:, at]).astype(BF)

    tiles(width // 256, 256, self_out)

    got_d = send(4, dx_s, dx_r, to_mate)
    def forward(block):
        part = n1.at[slot_across, pl.ds(block * 64, 64)]
        return pltpu.make_async_remote_copy(
            src_ref=part,
            dst_ref=part,
            send_sem=send_sem.at[block_sem + 3 * blocks + block],
            recv_sem=recv_sem.at[block_sem + 3 * blocks + block],
            device_id=to_mate,
            device_id_type=MESH,
        )

    def key_value(turn):
        slot = jnp.where(turn < 2, 2 * chip, 2 * across) + jnp.where(turn % 2 == 0, head, mate)

        @pl.when(turn == 1)
        def _():
            for copy in got_m:
                copy.wait_recv()

        @pl.when(turn == 2)
        def _():
            for block in range(blocks):
                got_n[block].wait_recv()
                forward(block).start()

        @pl.when(turn == 3)
        def _():
            for block in range(blocks):
                forward(block).wait_recv()

        for index in range(2 * width // 256):
            at = pl.ds(index * 256, 256)
            kv[slot, :, at] = dot_nn(n1[slot], w_qkv[:, pl.ds(width + index * 256, 256)]).astype(BF)

    def between():
        got_d.wait_recv()
        value = y0[...] + (dx_s[...].astype(F32) + dx_r[...].astype(F32))
        a1[...] = value
        m_b[...] = rms(value, gain[4]).astype(BF)
        load_cq.wait()
        cq[...] = (dot_nn(m_b[...], w_cq[...]).astype(BF) * HD ** (-0.5)).astype(BF)

    def key_values(first, last):
        def body(turn, carry):
            key_value(turn)
            return carry

        lax.fori_loop(first, last, body, 0)

    between()

    keys = 4 * rows

    def scores_of(pair, side, index, slots, allowed_keys):
        k2 = kv[slots, :, lanes_at(pair, LANES)].reshape(2 * rows, LANES)
        v2 = kv[slots, :, lanes_at(pair, LANES, width)].reshape(2 * rows, LANES)
        s_f[index] = dot_nt(q_s[:, lanes_at(pair, LANES)] * side, k2)
        return v2

    def near_pair(pair):
        slots = pl.ds(2 * chip, 2)
        outs = []
        for index, side in enumerate(sides):
            v2 = scores_of(pair, side, index, slots, okc)
            for block in range(rows // 32):
                part = pl.ds(block * 32, 32)
                scores = jnp.where(okc, s_f[index, part], NEG)
                top = jnp.max(scores, axis=-1, keepdims=True)
                probs = jnp.exp(scores - top)
                p_b[index, part] = probs.astype(BF)
                total = jnp.sum(probs, axis=-1, keepdims=True)
                u[part, lanes_at(index * pairs_e + pair, LANES)] = jnp.broadcast_to(total, (32, LANES))
                u[part, lanes_at(index * pairs_e + pair, LANES, 2 * width)] = jnp.broadcast_to(top, (32, LANES))
            outs.append(dot_nn(p_b[index], v2))
        o_f[:, lanes_at(pair, LANES)] = jnp.where(low_lane, outs[0], outs[1])

    def far_pair(pair):
        slots = pl.ds(2 * across, 2)
        outs = []
        for index, side in enumerate(sides):
            v2 = scores_of(pair, side, index, slots, okf)
            for block in range(rows // 32):
                part = pl.ds(block * 32, 32)
                scores = jnp.where(okf, s_f[index, part], NEG)
                near_top = u[part, lanes_at(index * pairs_e + pair, LANES, 2 * width)]
                own_top = jnp.max(scores, axis=-1, keepdims=True)
                top = jnp.maximum(jnp.broadcast_to(own_top, (32, LANES)), near_top)
                probs = jnp.exp(scores - jnp.concatenate([top] * (2 * rows // LANES), axis=1))
                fade = jnp.exp(near_top - top)
                total = jnp.broadcast_to(jnp.sum(probs, axis=-1, keepdims=True), (32, LANES))
                total = total + u[part, lanes_at(index * pairs_e + pair, LANES)] * fade
                p_b[index, part] = probs.astype(BF)
                fade_e[index, part] = fade
                scale_e[index, part] = 1.0 / total
                stat_e[index, part] = top + jnp.log(total)
            wide = dot_nn(p_b[index], v2) + o_f[:, lanes_at(pair, LANES)] * fade_e[index]
            outs.append(wide * scale_e[index])
        lse_e[pair] = jnp.where(low_lane, stat_e[0], stat_e[1])
        both = jnp.where(low_lane, outs[0], outs[1])
        o_f[:, lanes_at(pair, LANES)] = both
        o_b[:, lanes_at(pair, LANES)] = both.astype(BF)

    key_values(0, 2)
    each(pairs_e, UNROLL["attend"], near_pair)
    key_values(2, 4)
    sends.extend(forward(block) for block in range(blocks))
    each(pairs_e, UNROLL["attend"], far_pair)
    load_o.wait()

    def out_cols(at):
        h1[:, at] = x0[:, at] + dot_nn(o_b[...], w_o[:, at])

    tiles(width // 256, 256, out_cols)

    def norm_two(at):
        nb[at] = rms(h1[at], gain[1]).astype(BF)

    tiles(rows // 64, 64, norm_two)
    load_1.wait()

    def hidden(at):
        value = dot_nn(nb[...], w_1[:, at])
        u[:, at] = value
        act[:, at] = gelu(value).astype(BF)

    tiles(u.shape[1] // 256, 256, hidden)
    load_2.wait()

    def hidden_out(at):
        h2[:, at] = h1[:, at] + dot_nn(act[...], w_2[:, at])

    tiles(width // 256, 256, hidden_out)

    def norm_out(at):
        eo[head, at] = rms(h2[at], gain[2]).astype(BF)

    tiles(rows // 64, 64, norm_out)
    got_e = send(6, eo.at[head], eo.at[head], to_mate)
    load_ckv.wait()

    def cross_keys(slot):
        def body(at):
            ckv[slot, :, at] = dot_nn(eo[slot], w_ckv[:, at]).astype(BF)

        tiles(2 * own // 256, 256, body)

    cross_keys(head)
    got_e.wait_recv()
    cross_keys(mate)


    def cross_pair(pair):
        k2 = ckv[:, :, lanes_at(pair, LANES)].reshape(2 * rows, LANES)
        v2 = ckv[:, :, lanes_at(pair, LANES, own)].reshape(2 * rows, LANES)
        return cq[:, lanes_at(pair, LANES)], k2, v2

    st_p[...] = jnp.zeros_like(st_p)

    def cross_attend(pair):
        q2, k2, v2 = cross_pair(pair)
        stats = st_p[...]
        outs = []
        for index, side in enumerate(sides):
            scores = jnp.where(okc, dot_nt(q2 * side, k2), NEG)
            top = jnp.max(scores, axis=-1, keepdims=True)
            probs = jnp.exp(scores - top)
            total = jnp.sum(probs, axis=-1, keepdims=True)
            outs.append(dot_nn(probs.astype(BF), v2) / total)
            stats = jnp.where(lane == 2 * pair + index, top + jnp.log(total), stats)
        both = jnp.where(low_lane, outs[0], outs[1])
        cp[:, lanes_at(pair, LANES)] = both
        cp_b[:, lanes_at(pair, LANES)] = both.astype(BF)
        st_p[...] = stats

    each(pairs_d, UNROLL["cross"], cross_attend)
    mine_t = pl.ds(pl.multiple_of(chip * half, half), half)
    theirs_t = pl.ds(pl.multiple_of(across * half, half), half)
    got_c = send(7, cp_b.at[theirs_t], co_r, to_across)
    got_s = send(8, st_p.at[theirs_t], st_r, to_across)
    ff_tiles = u.shape[1] // 256

    def slopes(first, last):
        def some_cols(index, carry):
            at = pl.ds(pl.multiple_of(index * 256, 256), 256)
            u[:, at] = gelu_slope(u[:, at])
            return carry

        lax.fori_loop(first, last, some_cols, 0)

    slopes(0, ff_tiles // 2)
    got_c.wait_recv()
    got_s.wait_recv()
    l_own, l_oth = st_p[mine_t], st_r[...]
    top = jnp.maximum(l_own, l_oth)
    lse_c = top + jnp.log(jnp.exp(l_own - top) + jnp.exp(l_oth - top))
    w_own, w_oth = jnp.exp(l_own - lse_c), jnp.exp(l_oth - lse_c)

    def side_cols(array, pair):
        return jnp.where(
            low_lane, array[:, 2 * pair : 2 * pair + 1], array[:, 2 * pair + 1 : 2 * pair + 2]
        )

    for pair in range(pairs_d):
        lo = pair * LANES
        both = cp[mine_t, lo : lo + LANES] * side_cols(w_own, pair)
        both = both + co_r[:, lo : lo + LANES].astype(F32) * side_cols(w_oth, pair)
        co[:, lo : lo + LANES] = both
        co_b[:, lo : lo + LANES] = both.astype(BF)

    def exchange(index, value, meanwhile=None):
        slot = index - 9
        px_s[slot] = value.astype(BF)
        got = send(index, px_s.at[slot], px_r.at[slot], to_mate)
        if meanwhile is not None:
            meanwhile()
        got.wait_recv()
        return px_s[slot].astype(F32) + px_r[slot].astype(F32)

    load_co.wait()
    a2[...] = a1[mine_t] + exchange(9, dot_nn(co_b[...], w_co[...]))
    m_b[0:half] = rms(a2[...], gain[5]).astype(BF)
    load_d1.wait()

    def dec_hidden(at):
        value = dot_nn(m_b[0:half], w_d1[:, at])
        du[:, at] = value
        dact[:, at] = gelu(value).astype(BF)

    tiles(du.shape[1] // 512, 512, dec_hidden)
    load_d2.wait()

    def dec_slope():
        du[...] = gelu_slope(du[...])

    a3[...] = a2[...] + exchange(10, dot_nn(dact[...], w_d2[...]), dec_slope)
    f_b[...] = rms(a3[...], gain[6]).astype(BF)

    acc[...] = jnp.zeros_like(acc)

    def vocab_step(logits, table, top, total):
        new_top = jnp.maximum(top, jnp.max(logits, axis=-1, keepdims=True))
        fade = jnp.exp(top - new_top)
        probs = jnp.exp(logits - new_top)
        acc[...] = acc[...] * fade + dot_nn(probs.astype(BF), table)
        return new_top, total * fade + jnp.sum(probs, axis=-1, keepdims=True)

    def refill(index, slot):
        @pl.when(index + RING < full)
        def _():
            chunk_copy(index + RING, slot).start()

        if tail:

            @pl.when(index + RING == full)
            def _():
                tail_copy().start()

    span = UNROLL["vocab"]
    chunk_copy(0, 0).wait()
    lg[0] = dot_nt(f_b[...], ring[0])

    def vocab_chunks(turn, carry):
        first = span * turn
        slots = [lax.rem(first + k, RING) for k in range(span + 1)]
        for k in range(span):
            chunk_copy(first + k + 1, slots[k + 1]).wait()
            lg[(k + 1) % 2] = dot_nt(f_b[...], ring[slots[k + 1]])
            carry = vocab_step(lg[k % 2], ring[slots[k]], *carry)
            refill(first + k, slots[k])
        return carry

    carry = (jnp.full((half, 1), NEG, F32), jnp.zeros((half, 1), F32))
    turns = (full - 1) // span
    carry = lax.fori_loop(0, turns, vocab_chunks, carry)
    for index in range(span * turns, full):
        slot, after = index % RING, (index + 1) % RING
        if index + 1 < full:
            chunk_copy(index + 1, after).wait()
            lg[(index + 1) % 2] = dot_nt(f_b[...], ring[after])
        elif tail:
            tail_copy().wait()
            lg[(index + 1) % 2, :, 0:tail] = dot_nt(f_b[...], ring[after, 0:tail])
        carry = vocab_step(lg[index % 2], ring[slot], *carry)
        refill(index, slot)
    if tail:
        carry = vocab_step(lg[full % 2, :, 0:tail], ring[full % RING, 0:tail], *carry)
    top, total = carry
    acc_b[...] = (acc[...] / total).astype(BF)
    vl_s[...] = jnp.broadcast_to(top + jnp.log(total), vl_s.shape)
    got_a = send(11, acc_b, acc_r, to_mate)
    got_v = send(12, vl_s, vl_r, to_mate)
    pick = jnp.sum(f_b[...].astype(F32) * tgt[...], axis=-1, keepdims=True)
    got_a.wait_recv()
    got_v.wait_recv()
    l_own, l_oth = vl_s[:, 0:1], vl_r[:, 0:1]
    top = jnp.maximum(l_own, l_oth)
    lse_v = top + jnp.log(jnp.exp(l_own - top) + jnp.exp(l_oth - top))
    loss = jnp.sum(share * (lse_v - pick), axis=0, keepdims=True) * jnp.where(head == 0, 1.0, 0.0)
    mean_row = acc_b[...].astype(F32) * jnp.exp(l_own - lse_v) + acc_r[...].astype(F32) * jnp.exp(l_oth - lse_v)
    gffn[...] = rms_grad(a3[...], gain[6], share * (mean_row - tgt[...]))

    m_b[0:half] = gffn[...].astype(BF)

    def dec_hidden_grad(at):
        value = dot_nt(m_b[0:half], w_d2[at])
        dact[:, at] = (du[:, at] * value).astype(BF)

    tiles(du.shape[1] // 512, 512, dec_hidden_grad)
    slope = exchange(13, dot_nt(dact[...], w_d1[...]))
    gcross = gffn[...] + rms_grad(a2[...], gain[5], slope)
    gco[chip] = dot_nt(gcross.astype(BF), w_co[...]).astype(BF)
    stats = lse_c
    for pair in range(pairs_d):
        lo = pair * LANES
        value = gco[chip, :, lo : lo + LANES].astype(F32) * co[:, lo : lo + LANES]
        for index in range(2):
            picked_side = jnp.where(low_lane == (index == 0), value, 0.0)
            delta = jnp.sum(picked_side, axis=-1, keepdims=True)
            stats = jnp.where(lane == HD + 2 * pair + index, delta, stats)
    st_g[chip] = stats
    got_g = send(14, gco.at[chip], gco.at[chip], to_across)
    got_t = send(15, st_g.at[chip], st_g.at[chip], to_across)
    slopes(ff_tiles // 2, ff_tiles)
    got_g.wait_recv()
    got_t.wait_recv()

    def cross_back(pair):
        q2, k2, v2 = cross_pair(pair)
        do2 = gco[:, :, lanes_at(pair, LANES)].reshape(all_tgt, LANES)
        stats = st_g[...].reshape(all_tgt, LANES)
        dks, dvs = [], []
        for index, side in enumerate(sides):
            column = 2 * pair + index
            lse = jnp.sum(jnp.where(lane == column, stats, 0.0), axis=-1, keepdims=True)
            delta = jnp.sum(jnp.where(lane == HD + column, stats, 0.0), axis=-1, keepdims=True)
            scores = jnp.where(okc, dot_nt(q2 * side, k2), NEG)
            probs = jnp.exp(scores - lse)
            dp = dot_nt(do2 * side, v2)
            ds = (probs * (dp - delta)).astype(BF)
            dks.append(dot_tn(ds, q2))
            dvs.append(dot_tn(probs.astype(BF), do2))
        shape = (2, rows, LANES)
        dckv[:, :, lanes_at(pair, LANES)] = jnp.where(low_lane, *dks).astype(BF).reshape(shape)
        dckv[:, :, lanes_at(pair, LANES, own)] = jnp.where(low_lane, *dvs).astype(BF).reshape(shape)

    each(pairs_d, UNROLL["cross_back"], cross_back)
    def pair_grad_mate(at):
        gp_s[:, at] = dot_nt(dckv[mate], w_ckv[at]).astype(BF)

    tiles(width // 256, 256, pair_grad_mate)
    got_p = send(16, gp_s, gp_r, to_mate)

    def pair_grad_mine(at):
        gown[:, at] = dot_nt(dckv[head], w_ckv[at])

    tiles(width // 256, 256, pair_grad_mine)
    got_p.wait_recv()

    def out_grad(at):
        value = rms_grad(h2[at], gain[2], gown[at].astype(BF).astype(F32) + gp_r[at].astype(F32))
        go[at] = value
        nb[at] = value.astype(BF)

    tiles(rows // 64, 64, out_grad)

    def hidden_grad(at):
        act[:, at] = (u[:, at] * dot_nt(nb[...], w_2[at])).astype(BF)

    tiles(u.shape[1] // 256, 256, hidden_grad)

    def norm_two_grad(at):
        spare[:, at] = dot_nt(act[...], w_1[at])

    tiles(width // 256, 256, norm_two_grad)

    def one_grad(at):
        value = go[at] + rms_grad(h1[at], gain[1], spare[at])
        go[at] = value
        nb[at] = value.astype(BF)

    tiles(rows // 64, 64, one_grad)

    def attn_grad(at):
        d_o[:, at] = dot_nt(nb[...], w_o[at]).astype(BF)

    tiles(width // 256, 256, attn_grad)

    lead_keys = 4 * LEAD_PAD

    quad = 2 * LANES
    heads_in = quad // HD
    quad_lane = lax.broadcasted_iota(jnp.int32, (1, quad), 1)
    quad_of = [(quad_lane >= k * HD) & (quad_lane < (k + 1) * HD) for k in range(heads_in)]
    quad_b = [jnp.where(inside, 1.0, 0.0).astype(BF) for inside in quad_of]

    def lead_pair(group, part):
        pair = 2 * group + part
        at = lanes_at(pair, LANES)
        q2, do2 = q_s[:, at], d_o[:, at]
        k2 = kv[:, 0:LEAD_PAD, at].reshape(lead_keys, LANES)
        v2 = kv[:, 0:LEAD_PAD, lanes_at(pair, LANES, width)].reshape(lead_keys, LANES)
        value = do2.astype(F32) * o_f[:, at]
        dks, dvs, deltas = [], [], []
        for index, side in enumerate(sides):
            delta = jnp.sum(jnp.where(low_lane == (index == 0), value, 0.0), axis=-1, keepdims=True)
            deltas.append(delta)
            lse = lse_e[pair, :, index * HD : index * HD + 1]
            scores = jnp.where(okl, dot_nt(q2 * side, k2), NEG)
            probs = jnp.exp(scores - lse)
            ds = (probs * (dot_nt(do2 * side, v2) - delta)).astype(BF)
            dks.append(dot_tn(ds, q2))
            dvs.append(dot_tn(probs.astype(BF), do2))
        lo = part * LANES
        shape = (4, LEAD_PAD, LANES)
        dkv[group, :, :, lo : lo + LANES] = jnp.where(low_lane, *dks).astype(BF).reshape(shape)
        dkv[group, :, :, quad + lo : quad + lo + LANES] = jnp.where(low_lane, *dvs).astype(BF).reshape(shape)
        dl[pair] = jnp.where(low_lane, *[d[0:LEAD_PAD] for d in deltas])

    def stack(value):
        return jnp.concatenate([value * side for side in quad_b], axis=0)

    def column(ref, group, rows_at):
        return jnp.concatenate(
            [ref[2 * group + k // 2, rows_at, (k % 2) * HD : (k % 2) * HD + 1] for k in range(heads_in)], axis=0
        )

    def query_quad(group):
        at, vat = lanes_at(group, quad), lanes_at(group, quad, width)
        lead_rows = slice(0, LEAD_PAD)
        k4 = kv[:, :, at].reshape(keys, quad)
        v4 = kv[:, :, vat].reshape(keys, quad)
        scores = jnp.where(ok, dot_nt(stack(q_s[lead_rows, at]), k4), NEG)
        probs = jnp.exp(scores - column(lse_e, group, lead_rows))
        ds = (probs * (dot_nt(stack(d_o[lead_rows, at]), v4) - column(dl, group, lead_rows))).astype(BF)
        wide = dot_nn(ds, k4)
        value = jnp.zeros((LEAD_PAD, quad), F32)
        for k in range(heads_in):
            value = jnp.where(quad_of[k], wide[k * LEAD_PAD : (k + 1) * LEAD_PAD], value)
        gj[:, at] = (value * HD ** (-0.5)).astype(BF)

    def key_copies(group):
        plan = ((slot_across, 1, to_across), (slot_diag, 2, to_diag), (slot_mate, 0, to_mate))
        copies = []
        for k, (slot, place, peer) in enumerate(plan):
            copies.append(
                pltpu.make_async_remote_copy(
                    src_ref=dkv.at[group, slot],
                    dst_ref=dkv_r.at[group, place],
                    send_sem=send_sem.at[17 + 3 * group + k],
                    recv_sem=recv_sem.at[17 + 3 * group + k],
                    device_id=peer,
                    device_id_type=MESH,
                )
            )
        return copies

    def lead_group(group):
        lead_pair(group, 0)
        lead_pair(group, 1)
        for copy in key_copies(group):
            copy.start()

    each(width // quad, UNROLL["lead"], lead_group)
    each(width // quad, UNROLL["lead"], query_quad)
    for group in range(width // quad):
        summed = dkv[group, me].astype(F32)
        copies = key_copies(group)
        for index in range(3):
            copies[(2, 0, 1)[index]].wait_recv()
            summed = summed + dkv_r[group, index].astype(F32)
        sends.extend(copies)
        lo = group * quad
        gj[:, width + lo : width + lo + quad] = summed[:, :quad].astype(BF)
        gj[:, 2 * width + lo : 2 * width + lo + quad] = summed[:, quad:].astype(BF)

    def start_grad(at):
        spare[0:LEAD_PAD, at] = dot_nt(gj[...], w_qkv[at])

    tiles(width // 256, 256, start_grad)
    top_rows = slice(0, LEAD_PAD)
    value = go[top_rows] + rms_grad(x0[top_rows], gain[0], spare[top_rows])
    spot = lax.broadcasted_iota(jnp.int32, (LEAD_PAD, width), 0)
    extra = jnp.where(spot == leads, loss, 0.0)
    blk[...] = jnp.where(spot < leads, value, extra)

    piece = LEAD_PAD // n_grp
    slot = block_sem + 4 * blocks
    got = []
    for step in range(n_grp):
        member = lax.rem(grp + step, n_grp)
        rows_at = pl.ds(pl.multiple_of(member * piece, piece), piece)
        if step:
            got.append(send(slot, blk.at[rows_at], s1_r.at[step], {"grp": member}))
            slot += 1
    value = blk[pl.ds(pl.multiple_of(grp * piece, piece), piece)]
    for step in range(1, n_grp):
        got[step - 1].wait_recv()
        value = value + s1_r[step]
    s2_r[ex] = value
    got = []
    for step in range(1, n_ex):
        got.append(send(slot, s2_r.at[ex], s2_r.at[ex], ex_peer(step)))
        slot += 1
    for copy in got:
        copy.wait_recv()
    value = s2_r[0]
    for member in range(1, n_ex):
        value = value + s2_r[member]
    all_r[me, grp] = value
    got = []
    for step in range(1, n_grp * QUARTERS):
        got.append(send(slot, all_r.at[me, grp], all_r.at[me, grp], plane_peer(step)))
        slot += 1
    for copy in got:
        copy.wait_recv()
    out[...] = all_r[...].reshape(out.shape)
    for copy in sends:
        copy.wait_send()


def main_call(lengths, vmem, hbm):
    half = vmem[1].shape[1] // 2
    rows = (hbm[0].shape[0] - 3 * half) // 2
    wq, wo, w1, w2, dqkv, dwo, cqw, ckvw, cwo, dw1, dw2, emb = hbm[1:]
    width, own, ff, dff, tgt_all = wo.shape[0], dwo.shape[0], w1.shape[1], dw1.shape[1], 2 * half
    pairs_e = width // LANES

    def v(shape, kind=F32):
        return pltpu.VMEM(shape, kind)

    scratch = [v(w.shape, BF) for w in hbm[1:12]]
    scratch += [v((RING, CHUNK, width), BF)]
    scratch += [v((64, width))]
    scratch += [v((rows, width), BF), v((rows, width), BF), v((tgt_all + half, width), BF), v((tgt_all + half, width), BF)]
    scratch += [v((rows, width)) for _ in range(5)]
    scratch += [v((4, rows, width), BF), v((rows, width), BF), v((4, rows, 2 * width), BF)]
    scratch += [v((rows, width)), v((rows, width), BF), v((2, rows, 2 * rows)), v((2, rows, 2 * rows), BF)]
    scratch += [v((pairs_e, rows, LANES))]
    scratch += [v((2, rows, LANES)), v((2, rows, LANES)), v((2, rows, LANES)), v((rows, width), BF)]
    scratch += [v((rows, ff)), v((rows, ff), BF)]
    scratch += [v((2, rows, width), BF), v((2, rows, 2 * own), BF), v((2, rows, 2 * own), BF)]
    scratch += [v((rows, width), BF), v((rows, width), BF), v((rows, width)), v((rows, width), BF)]
    groups = width // (2 * LANES)
    scratch += [v((groups, 4, LEAD_PAD, 4 * LANES), BF), v((groups, 3, LEAD_PAD, 4 * LANES), BF), v((LEAD_PAD, 3 * width), BF)]
    scratch += [v((pairs_e, LEAD_PAD, LANES))]
    scratch += [v((tgt_all, width)), v((tgt_all, width)), v((tgt_all, width), BF), v((tgt_all, 3 * own), BF)]
    scratch += [v((tgt_all, own), BF), v((tgt_all, width), BF), v((tgt_all, width), BF), v((tgt_all, own), BF)]
    scratch += [v((tgt_all, own)), v((tgt_all, own), BF), v((tgt_all, LANES)), v((half, LANES))]
    scratch += [v((half, own), BF), v((half, own)), v((half, own), BF)]
    scratch += [v((2, half, CHUNK))]
    scratch += [v((5, half, width), BF), v((5, half, width), BF)]
    scratch += [v((half, width)), v((half, width)), v((half, dff)), v((half, dff), BF), v((half, width), BF)]
    scratch += [v((half, width)), v((half, width)), v((half, width), BF), v((half, width), BF)]
    scratch += [v((half, LANES)), v((half, LANES)), v((half, width)), v((2, half, own), BF), v((2, half, LANES))]
    n_grp, n_ex = lax.axis_size("grp"), lax.axis_size("ex")
    piece = LEAD_PAD // n_grp
    scratch += [v((LEAD_PAD, width)), v((n_grp, piece, width)), v((n_ex, piece, width))]
    scratch += [v((QUARTERS, n_grp, piece, width))]
    exchanges = 17 + 3 * groups + 4 * (rows // 64) + (n_grp - 1) + (n_ex - 1) + (n_grp * QUARTERS - 1)
    scratch += [
        pltpu.SemaphoreType.DMA((13,)),
        pltpu.SemaphoreType.DMA((RING,)),
        pltpu.SemaphoreType.DMA((exchanges,)),
        pltpu.SemaphoreType.DMA((exchanges,)),
    ]
    any_spec, vmem_spec = pl.BlockSpec(memory_space=pl.ANY), pl.BlockSpec(memory_space=pltpu.VMEM)
    return pl.pallas_call(
        main_kernel,
        out_shape=jax.ShapeDtypeStruct((QUARTERS, LEAD_PAD, width), F32),
        in_specs=[pl.BlockSpec(memory_space=pltpu.SMEM), any_spec] + [vmem_spec] * len(vmem) + [any_spec] * len(hbm[1:]),
        out_specs=vmem_spec,
        scratch_shapes=scratch,
        compiler_params=pltpu.CompilerParams(
            collective_id=1, has_side_effects=True, vmem_limit_bytes=62 * 1024 * 1024
        ),
        name="step_of_one_example",
    )(lengths, hbm[0], *vmem, *hbm[1:])


def log2(size):
    return size.bit_length() - 1


def ids_kernel(enc_ids, dec_ids, target_ids, out, lines, got, unused, send_sem, recv_sem):
    ex, chip = lax.axis_index("ex"), lax.axis_index("chip")
    chips = lax.axis_size("chip")
    seqs = lax.axis_size(SEQ)
    me = ex * chips + chip
    enc_dev, tgt_dev = enc_ids.shape[1], dec_ids.shape[1]


    def peer_of(step):
        peer = lax.rem(me + step, seqs)
        row = lax.div(peer, chips)
        return row, {"ex": row, "chip": peer - row * chips}

    barrier = pltpu.get_barrier_semaphore()
    for step in range(1, seqs):
        pl.semaphore_signal(barrier, inc=1, device_id=peer_of(step)[1], device_id_type=MESH)
    lines[:, 0:enc_dev] = enc_ids[...]
    lines[:, enc_dev : enc_dev + tgt_dev] = dec_ids[...]
    lines[:, enc_dev + tgt_dev : enc_dev + 2 * tgt_dev] = target_ids[...]
    lines[:, enc_dev + 2 * tgt_dev :] = jnp.zeros((lines.shape[0], lines.shape[1] - enc_dev - 2 * tgt_dev), jnp.int32)
    pl.semaphore_wait(barrier, seqs - 1)

    for step in range(1, seqs):
        row, peer = peer_of(step)
        pltpu.make_async_remote_copy(
            src_ref=lines.at[pl.ds(row, 1)],
            dst_ref=got.at[pl.ds(me, 1)],
            send_sem=send_sem,
            recv_sem=recv_sem,
            device_id=peer,
            device_id_type=MESH,
        ).start()
    own_line = lines.at[pl.ds(ex, 1)]
    pltpu.make_async_copy(own_line, got.at[pl.ds(me, 1)], recv_sem).start()
    pltpu.make_async_copy(own_line, unused.at[pl.ds(0, 1)], send_sem).start()
    pltpu.make_async_copy(got, got, recv_sem).wait()
    pltpu.make_async_copy(got, got, send_sem).wait()
    out[...] = got[...]


def ids_call(enc_ids, dec_ids, target_ids):
    seqs = lax.axis_size(SEQ)
    lanes = -(-(enc_ids.shape[1] + 2 * dec_ids.shape[1]) // LANES) * LANES
    return pl.pallas_call(
        ids_kernel,
        out_shape=jax.ShapeDtypeStruct((seqs, lanes), jnp.int32),
        in_specs=[pl.BlockSpec(memory_space=pltpu.VMEM)] * 3,
        out_specs=pl.BlockSpec(memory_space=pltpu.VMEM),
        scratch_shapes=[
            pltpu.VMEM((enc_ids.shape[0], lanes), jnp.int32),
            pltpu.VMEM((seqs, lanes), jnp.int32),
            pltpu.VMEM((8, lanes), jnp.int32),
            pltpu.SemaphoreType.DMA,
            pltpu.SemaphoreType.DMA,
        ],
        compiler_params=pltpu.CompilerParams(collective_id=2, has_side_effects=True),
        name="ids_of_one_example",
    )(enc_ids, dec_ids, target_ids)


GROUP = 16


AHEAD = 8


def lookup_kernel(rows, tokens, lead, enc_dev, tgt_dev, ids, table, out, blocks, spots, sems):
    chip, head = lax.axis_index("chip"), lax.axis_index("head")
    vocab_part = table.shape[0]
    enc_count = 2 * rows
    tgt_all = tgt_dev * ids.shape[0]
    half = tgt_all // 2
    groups = out.shape[0] // GROUP
    first, second = enc_count // GROUP, (enc_count + tgt_all) // GROUP

    def fetch(group):
        enc = group < first
        slot = (group * GROUP) >> log2(rows)
        enc_base = (PROMPT - lead) + tokens * (2 * chip + slot) + ((group * GROUP) & (rows - 1))
        dec_base = (group - jnp.where(group < second, first, second)) * GROUP
        dec_base = dec_base + jnp.where(group < second, 0, chip * half)
        base = jnp.where(enc, enc_base, dec_base)
        shift = jnp.where(enc, log2(enc_dev), log2(tgt_dev))
        mask = jnp.where(enc, enc_dev - 1, tgt_dev - 1)
        lane = jnp.where(enc, 0, jnp.where(group < second, enc_dev, enc_dev + tgt_dev))
        for k in range(GROUP):
            token = ids[(base + k) >> shift, lane + ((base + k) & mask)]
            upper = jnp.where(token >= vocab_part, 1, 0)
            local = token - upper * vocab_part
            spots[group * GROUP + k] = k * GROUP + (local & (GROUP - 1)) + ((upper + head - 2 * upper * head) * 4096)
            at = pl.multiple_of((local >> log2(GROUP)) << log2(GROUP), GROUP)
            pltpu.make_async_copy(
                table.at[pl.ds(at, GROUP)], blocks.at[group * GROUP + k], sems.at[group]
            ).start()

    across = lax.broadcasted_iota(jnp.int32, (8, LANES), 1)
    down = lax.broadcasted_iota(jnp.int32, (8, LANES), 0)

    def select(group):
        at = pl.ds(pl.multiple_of(group * GROUP, GROUP), GROUP)
        pltpu.make_async_copy(blocks.at[at], blocks.at[at], sems.at[group]).wait()
        chosen = []
        for part in range(GROUP // 8):
            want = jnp.full((8, LANES), -1, jnp.int32)
            for k in range(8):
                want = jnp.where(down == k, spots[group * GROUP + part * 8 + k], want)
            hits = [jnp.where(across + base == want, 1.0, 0.0) for base in range(0, GROUP * GROUP, LANES)]
            chosen.append(jnp.concatenate(hits, axis=1))
        chosen = jnp.concatenate(chosen, axis=0).astype(BF)
        out[at] = dot_nn(chosen, blocks[at].reshape(GROUP * GROUP, out.shape[1])).astype(BF)

    def loop(start, stop, *steps):
        def body(group, carry):
            for step in steps:
                step(group)
            return carry

        lax.fori_loop(start, stop, body, 0, unroll=2 if len(steps) > 1 and (stop - start) % 2 == 0 else 1)

    skip = lead // GROUP
    per_slot = rows // GROUP - skip
    needed = groups - 2 * skip

    def real(index):
        return index + skip + jnp.where(index >= per_slot, skip, 0)

    loop(0, AHEAD, lambda index: fetch(real(index)))
    loop(AHEAD, needed, lambda index: fetch(real(index)), lambda index: select(real(index - AHEAD)))
    loop(needed - AHEAD, needed, lambda index: select(real(index)))


def lookup_call(ids, table, rows, tokens, lead, enc_dev, tgt_dev):
    count = 2 * rows + tgt_dev * ids.shape[0] * 3 // 2
    width = table.shape[1]
    return pl.pallas_call(
        functools.partial(lookup_kernel, rows, tokens, lead, enc_dev, tgt_dev),
        out_shape=jax.ShapeDtypeStruct((count, width), BF),
        in_specs=[pl.BlockSpec(memory_space=pltpu.SMEM), pl.BlockSpec(memory_space=pl.ANY)],
        out_specs=pl.BlockSpec(memory_space=pltpu.VMEM),
        scratch_shapes=[
            pltpu.VMEM((count, GROUP, width), BF),
            pltpu.SMEM((count,), jnp.int32),
            pltpu.SemaphoreType.DMA((count // GROUP,)),
        ],
        compiler_params=pltpu.CompilerParams(vmem_limit_bytes=32 * 1024 * 1024),
        name="embedding_rows",
    )(ids, table)


def lamb_kernel(summed, first_old, second_old, prompt, loss, grad_norm, norms, first_new, second_new, prompt_new, work):
    lead = PROMPT // QUARTERS
    for quarter in range(QUARTERS):
        work[quarter * lead : (quarter + 1) * lead] = summed[quarter, 0:lead]
    grad = work[...]
    total = summed[0, lead : lead + 1, 0:1]
    for quarter in range(1, QUARTERS):
        total = total + summed[quarter, lead : lead + 1, 0:1]
    loss[0] = jnp.sum(total)
    norm = jnp.sqrt(jnp.sum(grad * grad))
    grad_norm[0] = norm
    clipped = grad * (clip_bound / jnp.maximum(norm, clip_bound))
    first_next = beta_first * first_old[...] + (1.0 - beta_first) * clipped
    second_next = beta_second * second_old[...] + (1.0 - beta_second) * clipped * clipped
    first_new[...] = first_next
    second_new[...] = second_next
    scaled_first = first_next / (1.0 - beta_first**STEP)
    scaled_second = second_next / (1.0 - beta_second**STEP)
    param = prompt[...]
    update = scaled_first / (jnp.sqrt(scaled_second) + adam_eps) + decay_rate * param
    param_norm = jnp.sqrt(jnp.sum(param * param))
    update_norm = jnp.sqrt(jnp.sum(update * update))
    norms[0] = param_norm
    norms[1] = update_norm
    prompt_new[...] = param - learn_rate * (param_norm / update_norm) * update


def lamb_call(summed, first_old, second_old, prompt):
    smem, vmem = pl.BlockSpec(memory_space=pltpu.SMEM), pl.BlockSpec(memory_space=pltpu.VMEM)
    like = jax.ShapeDtypeStruct(prompt.shape, F32)
    return pl.pallas_call(
        lamb_kernel,
        out_shape=(
            jax.ShapeDtypeStruct((1,), F32),
            jax.ShapeDtypeStruct((1,), F32),
            jax.ShapeDtypeStruct((2,), F32),
            like,
            like,
            like,
        ),
        in_specs=[vmem] * 4,
        out_specs=(smem, smem, smem, vmem, vmem, vmem),
        scratch_shapes=[pltpu.VMEM(prompt.shape, F32)],
        name="lamb",
    )(summed, first_old, second_old, prompt)


def shards(
    enc_ids,
    lengths,
    dec_ids,
    target_ids,
    loss_mask,
    embedding,
    prompt,
    first_moment,
    second_moment,
    gains,
    enc_qkv,
    enc_wo,
    enc_w1,
    enc_w2,
    dec_qkv,
    dec_wo,
    cross_q,
    cross_kv,
    cross_wo,
    dec_w1,
    dec_w2,
):
    width = embedding.shape[1]
    own = dec_wo.shape[0]
    enc_dev, tgt_dev = enc_ids.shape[1], dec_ids.shape[1]
    total_len = enc_dev * lax.axis_size(SEQ)
    lead = PROMPT // QUARTERS
    tokens = (total_len - PROMPT) // QUARTERS
    rows = total_len // QUARTERS
    ids = ids_call(enc_ids, dec_ids, target_ids)
    picked = lookup_call(ids, embedding, rows, tokens, lead, enc_dev, tgt_dev)
    summed = main_call(
        lengths,
        (prompt, loss_mask, gains),
        (
            picked,
            enc_qkv,
            enc_wo,
            enc_w1,
            enc_w2,
            jnp.transpose(dec_qkv, (1, 0, 2)),
            dec_wo,
            cross_q,
            cross_kv.reshape(width, 2 * own),
            cross_wo,
            dec_w1,
            dec_w2,
            embedding,
        ),
    )
    loss, grad_norm, norms, first_new, second_new, prompt_new = lamb_call(summed, first_moment, second_moment, prompt)
    return loss.reshape(()), grad_norm.reshape(()), norms, first_new, second_new, prompt_new


def solution(mesh):
    finer = Mesh(
        mesh.devices.reshape(mesh.shape["grp"], mesh.shape["seq"] // 2, 2, mesh.shape["head"]),
        ("grp", "ex", "chip", "head"),
    )
    placed = (
        P("grp", SEQ),
        P("grp"),
        P("grp", SEQ),
        P("grp", SEQ),
        P("grp", None),
        P("head", None),
        P(),
        P(),
        P(),
        P(),
        P(),
        P(),
        P(),
        P(),
        P(None, None, "head"),
        P("head", None),
        P(None, "head"),
        P(None, None, "head"),
        P("head", None),
        P(None, "head"),
        P("head", None),
    )
    return jax.shard_map(
        shards,
        mesh=finer,
        in_specs=placed,
        out_specs=(P(), P(), P(), P(), P(), P()),
        check_vma=False,
    )
```
